32 devices in a mesh: visit: 16 (over z, y, core), tile: 2 (over x).
Axes of the slice: x: 2, y: 2, z: 4, core: 2. Of those that a mesh axis runs over, the one named last changes fastest.
Arguments:
- exposures: float32 [16, 512, 256], P('visit', 'tile'), may hold values from 0.3 to 3
- sky_model: float32 [512, 256], P(('tile', 'visit')), may hold values from 0.5 to 2
- blur_kernels: float32 [16, 31, 31], P('visit'), may hold values from 0.05 to 1
- coverage: int32 [16, 2], P('visit'), may hold values from 0 to 1, as said below
Outputs:
- deconvolved: float32 [512, 256], P(('tile', 'visit'))
The draws below stay inside these ranges and needn't reach their ends.
Inputs may be any that keep to these rules, and one draw needn't show every extreme that they name: `coverage`: every tile is covered by at least one exposure.
All inputs are finite; a program needn't handle non-finite values.
Results may differ from the reference program's by a relative error of at most 0.0001.
Values sent between devices are 32-bit elements; how exact they have to be, the bound alone decides.
No kernel may reach another device: no remote copies, remote signals or barrier semaphores. Data moves between devices by JAX's collectives and lax.ppermute only.
A program may use at most 128 MiB of HBM per device.

```python
import math
import jax
import jax.numpy as jnp
from jax import lax

TILE_R = 256
TILE_C = 256
PSF = 31
ITERS = 2
EXPOSURES = 16
NTILES = 2
NROWS = 512


def draw_coverage(key, part):
    first_key = jax.random.fold_in(key, 11)
    second_key = jax.random.fold_in(key, 23)
    levels = jax.random.randint(first_key, (EXPOSURES, NTILES), 0, 1000)
    limits = 250 + 600 * jnp.arange(EXPOSURES) // EXPOSURES
    covered = levels < limits[:, None]
    forced = jax.random.randint(second_key, (NTILES,), 0, EXPOSURES)
    covered = covered | (jnp.arange(EXPOSURES)[:, None] == forced[None, :])
    return covered.astype(jnp.int32)


def level_of(key, dims, split, smallest, largest):
    factor_of = 1.0
    for dim, shards_of in split:
        steps = jax.random.uniform(jax.random.fold_in(jax.random.fold_in(key, 6), dim), (shards_of,), jnp.float32, smallest / len(split), largest / len(split))
        factor_of = factor_of * jnp.repeat(jnp.exp(steps), dims[dim] // shards_of).reshape((-1,) + (1,) * (len(dims) - 1 - dim))
    return factor_of


def setup_inputs(seed: int = 0) -> dict:
    arg_keys = jax.random.split(jax.random.key(seed), 5)
    exposures = jnp.clip(jnp.exp(math.log(3.0) - 2.3025851 * jax.random.uniform(arg_keys[0], (EXPOSURES, NROWS, TILE_C), jnp.float32) ** level_of(arg_keys[0], (EXPOSURES, NROWS, TILE_C), ((0, 16), (1, 2)), -0.2, 0.2)), 0.3, 3.0)
    sky_model = jnp.clip(jnp.exp(math.log(2.0) - 1.3862944 * jax.random.uniform(arg_keys[1], (NROWS, TILE_C), jnp.float32) ** level_of(arg_keys[1], (NROWS, TILE_C), ((0, 32),), -0.2, 0.2)), 0.5, 2.0)
    blur_kernels = jnp.clip(jnp.exp(math.log(1.0) - 2.9957323 * jax.random.uniform(arg_keys[2], (EXPOSURES, PSF, PSF), jnp.float32) ** level_of(arg_keys[2], (EXPOSURES, PSF, PSF), ((0, 16),), -0.2, 0.2)), 0.05, 1.0)
    coverage = draw_coverage(jax.random.fold_in(arg_keys[4], 71), 0)
    return dict(exposures=exposures, sky_model=sky_model, blur_kernels=blur_kernels, coverage=coverage)


def correlate(field, kernel):
    half = kernel.shape[0] // 2
    result = lax.conv_general_dilated(field[None, None], kernel[None, None], (1, 1), [(half, half), (half, half)], precision=lax.Precision.HIGHEST)
    return result[0, 0]


def reference(exposures, sky_model, blur_kernels, coverage):
    kernels = blur_kernels / jnp.sum(blur_kernels, axis=(1, 2), keepdims=True)
    row_tile = jnp.arange(NROWS) // TILE_R
    weights = coverage.astype(jnp.float32)[:, row_tile]

    def norm_step(total, member):
        weight_row, kernel = member
        field = jnp.broadcast_to(weight_row[:, None], (NROWS, TILE_C))
        return total + correlate(field, kernel), None

    zeros_field = jnp.zeros((NROWS, TILE_C), jnp.float32)
    norm_field, _ = lax.scan(norm_step, zeros_field, (weights, kernels))
    model = sky_model
    for step in range(ITERS):
        def update_step(total, member):
            counts, weight_row, kernel = member
            blurred = correlate(model, kernel[::-1, ::-1])
            ratio = weight_row[:, None] * counts / blurred
            return total + correlate(ratio, kernel), None

        numerator, _ = lax.scan(update_step, zeros_field, (exposures, weights, kernels))
        model = model * numerator / norm_field
    return model
```

```python
import jax
import jax.numpy as jnp
from jax import lax
from jax.sharding import PartitionSpec as P

ITERS = 2


def padded(array, sides, width):
    for axis, dim in sides:
        peers, length = (lax.axis_size(axis), array.shape[dim])
        up = [(i, (i + 1) % peers) for i in range(peers - 1)]
        down = [(j, i) for i, j in up]
        last = lax.slice_in_dim(array, length - width, length, axis=dim)
        initial = lax.slice_in_dim(array, 0, width, axis=dim)
        before = lax.ppermute(last, axis, up)
        after = lax.ppermute(initial, axis, down)
        array = jnp.concatenate([before, array, after], axis=dim)
    return array


def band_lookup(width, kernel_len):
    half = kernel_len // 2
    differ = jnp.arange(width)[:, None] - jnp.arange(width)[None, :] + half
    band_table = (differ[:, :, None] == jnp.arange(kernel_len)[None, None, :]).astype(jnp.float32)
    return band_table.reshape(width * width, kernel_len)


def column_operator(kernel, band_table, width):
    kernel_len = kernel.shape[0]
    operator = jnp.dot(band_table, kernel.T, precision=lax.Precision.HIGHEST)
    operator = operator.reshape(width, width, kernel_len).transpose(0, 2, 1)
    return operator.reshape(width, kernel_len * width)


def correlate(extended, operator):
    width = operator.shape[0]
    kernel_len = operator.shape[1] // width
    out_rows = extended.shape[0] - (kernel_len - 1)
    product = jnp.dot(extended, operator, precision=lax.Precision.HIGHEST)
    product = product.reshape(extended.shape[0], kernel_len, width)
    total = product[0:out_rows, 0]
    for offset in range(1, kernel_len):
        total = total + product[offset : offset + out_rows, offset]
    return total


def body(exposures, sky_model, blur_kernels, coverage):
    tile_rows = exposures.shape[1]
    tile_cols = exposures.shape[2]
    kernel_len = blur_kernels.shape[1]
    radius = kernel_len // 2
    tile_count = lax.axis_size("tile")
    tile_place = lax.axis_index("tile")
    kernels = blur_kernels / jnp.sum(blur_kernels, axis=(1, 2), keepdims=True)
    band_table = band_lookup(tile_cols, kernel_len)
    forward_ops = [column_operator(kernels[0], band_table, tile_cols)]
    flipped_ops = [column_operator(kernels[0][::-1, ::-1], band_table, tile_cols)]
    global_row = tile_place * tile_rows - radius + jnp.arange(tile_rows + 2 * radius)
    row_owner = jnp.floor_divide(global_row, tile_rows)
    selector = (row_owner[:, None] == jnp.arange(tile_count)[None, :]).astype(jnp.float32)
    weight_rows = jnp.dot(coverage.astype(jnp.float32), selector.T, precision=lax.Precision.HIGHEST)
    member = 0
    peers = lax.axis_size("visit")
    shard_rows = sky_model.shape[0]
    kernel_area = kernel_len * kernel_len
    facts = jnp.concatenate([kernels[0].reshape(-1), coverage[0].astype(jnp.float32)])
    fact_rows = -(-facts.shape[0] // tile_cols)
    facts = jnp.pad(facts, (0, fact_rows * tile_cols - facts.shape[0])).reshape(fact_rows, tile_cols)
    gathered = lax.all_gather(jnp.concatenate([sky_model, facts], axis=0), "visit", axis=0, tiled=False)
    whole = gathered[:, :shard_rows].reshape(tile_rows, tile_cols)
    all_facts = gathered[:, shard_rows:].reshape(peers, fact_rows * tile_cols)
    all_kernels = all_facts[:, :kernel_area].reshape(peers, kernel_len, kernel_len)
    all_cover = all_facts[:, kernel_area : kernel_area + tile_count]
    column = jnp.arange(tile_cols)[None, :] + jnp.arange(kernel_len)[:, None] - radius
    inside = ((column >= 0) & (column < tile_cols)).astype(jnp.float32)
    column_sums = jnp.dot(all_kernels.reshape(peers * kernel_len, kernel_len), inside, precision=lax.Precision.HIGHEST)
    first_row = tile_place * tile_rows + lax.axis_index("visit") * shard_rows
    window_row = first_row + jnp.arange(shard_rows)[:, None] + jnp.arange(kernel_len)[None, :] - radius
    window_owner = jnp.floor_divide(window_row, tile_rows)
    row_weight = sum(
        jnp.where(window_owner[:, None, :] == t, all_cover[None, :, t, None], 0.0) for t in range(tile_count)
    )
    norm_shard = jnp.dot(
        row_weight.reshape(shard_rows, peers * kernel_len), column_sums, precision=lax.Precision.HIGHEST
    )
    model_width = 2 * radius
    data_wide = padded(exposures, (("tile", 1),), radius)
    model_shard = sky_model
    for step in range(ITERS):
        if step > 0:
            copies = jnp.broadcast_to(model_shard[None], (peers,) + model_shard.shape)
            whole = lax.all_to_all(copies, "visit", 0, 0, tiled=False).reshape(tile_rows, tile_cols)
        model_wide = padded(whole, (("tile", 0),), model_width)
        blurred = correlate(model_wide, flipped_ops[member])
        weight_col = weight_rows[member][:, None]
        safe_blur = jnp.where(weight_col > 0.0, blurred, 1.0)
        ratio_wide = weight_col * data_wide[member] / safe_blur
        numerator = correlate(ratio_wide, forward_ops[member])
        shares = lax.all_to_all(numerator.reshape(peers, shard_rows, tile_cols), "visit", 0, 0, tiled=False)
        model_shard = model_shard * jnp.sum(shares, axis=0) / norm_shard
    return model_shard


def solution(mesh):
    return jax.shard_map(
        body,
        mesh=mesh,
        in_specs=(
            P("visit", "tile", None),
            P(("tile", "visit"), None),
            P("visit", None, None),
            P("visit", None),
        ),
        out_specs=P(("tile", "visit"), None),
        check_vma=False,
    )
```

```python
import jax
import jax.numpy as jnp
from jax import lax
from jax.sharding import PartitionSpec as P

ITERS = 2


def padded(array, sides, width):
    for axis, dim in sides:
        peers, length = (lax.axis_size(axis), array.shape[dim])
        up = [(i, (i + 1) % peers) for i in range(peers - 1)]
        down = [(j, i) for i, j in up]
        last = lax.slice_in_dim(array, length - width, length, axis=dim)
        initial = lax.slice_in_dim(array, 0, width, axis=dim)
        before = lax.ppermute(last, axis, up)
        after = lax.ppermute(initial, axis, down)
        array = jnp.concatenate([before, array, after], axis=dim)
    return array


def band_lookup(width, kernel_len):
    half = kernel_len // 2
    differ = jnp.arange(width)[:, None] - jnp.arange(width)[None, :] + half
    band_table = (differ[:, :, None] == jnp.arange(kernel_len)[None, None, :]).astype(jnp.float32)
    return band_table.reshape(width * width, kernel_len)


def column_operator(kernel, band_table, width):
    kernel_len = kernel.shape[0]
    operator = jnp.dot(band_table, kernel.T, precision=lax.Precision.HIGHEST)
    operator = operator.reshape(width, width, kernel_len).transpose(0, 2, 1)
    return operator.reshape(width, kernel_len * width)


def correlate(extended, operator):
    width = operator.shape[0]
    kernel_len = operator.shape[1] // width
    out_rows = extended.shape[0] - (kernel_len - 1)
    product = jnp.dot(extended, operator, precision=lax.Precision.HIGHEST)
    product = product.reshape(extended.shape[0], kernel_len, width)
    total = product[0:out_rows, 0]
    for offset in range(1, kernel_len):
        total = total + product[offset : offset + out_rows, offset]
    return total


def body(exposures, sky_model, blur_kernels, coverage):
    tile_rows = exposures.shape[1]
    tile_cols = exposures.shape[2]
    kernel_len = blur_kernels.shape[1]
    radius = kernel_len // 2
    tile_count = lax.axis_size("tile")
    tile_place = lax.axis_index("tile")
    kernels = blur_kernels / jnp.sum(blur_kernels, axis=(1, 2), keepdims=True)
    band_table = band_lookup(tile_cols, kernel_len)
    forward_ops = [column_operator(kernels[0], band_table, tile_cols)]
    flipped_ops = [column_operator(kernels[0][::-1, ::-1], band_table, tile_cols)]
    global_row = tile_place * tile_rows - radius + jnp.arange(tile_rows + 2 * radius)
    row_owner = jnp.floor_divide(global_row, tile_rows)
    selector = (row_owner[:, None] == jnp.arange(tile_count)[None, :]).astype(jnp.float32)
    weight_rows = jnp.dot(coverage.astype(jnp.float32), selector.T, precision=lax.Precision.HIGHEST)
    member = 0
    peers = lax.axis_size("visit")
    shard_rows = sky_model.shape[0]
    kernel_area = kernel_len * kernel_len
    facts = jnp.concatenate([kernels[0].reshape(-1), coverage[0].astype(jnp.float32)])
    fact_rows = -(-facts.shape[0] // tile_cols)
    facts = jnp.pad(facts, (0, fact_rows * tile_cols - facts.shape[0])).reshape(fact_rows, tile_cols)
    everyone = tile_count * peers

    def broadcast(block):
        copies = jnp.broadcast_to(block[None], (everyone,) + block.shape)
        return lax.all_to_all(copies, ("tile", "visit"), 0, 0, tiled=False)

    def widened(sky):
        rows = jnp.pad(sky, ((model_width, model_width), (0, 0)))
        return lax.dynamic_slice_in_dim(rows, tile_place * tile_rows, tile_rows + 2 * model_width, axis=0)

    model_width = 2 * radius
    gathered = broadcast(jnp.concatenate([sky_model, facts], axis=0))
    model_wide = widened(gathered[:, :shard_rows].reshape(-1, tile_cols))
    gathered = lax.dynamic_slice_in_dim(gathered, tile_place * peers, peers, axis=0)
    all_facts = gathered[:, shard_rows:].reshape(peers, fact_rows * tile_cols)
    all_kernels = all_facts[:, :kernel_area].reshape(peers, kernel_len, kernel_len)
    all_cover = all_facts[:, kernel_area : kernel_area + tile_count]
    column = jnp.arange(tile_cols)[None, :] + jnp.arange(kernel_len)[:, None] - radius
    inside = ((column >= 0) & (column < tile_cols)).astype(jnp.float32)
    column_sums = jnp.dot(all_kernels.reshape(peers * kernel_len, kernel_len), inside, precision=lax.Precision.HIGHEST)
    first_row = tile_place * tile_rows + lax.axis_index("visit") * shard_rows
    window_row = first_row + jnp.arange(shard_rows)[:, None] + jnp.arange(kernel_len)[None, :] - radius
    window_owner = jnp.floor_divide(window_row, tile_rows)
    row_weight = sum(
        jnp.where(window_owner[:, None, :] == t, all_cover[None, :, t, None], 0.0) for t in range(tile_count)
    )
    norm_shard = jnp.dot(
        row_weight.reshape(shard_rows, peers * kernel_len), column_sums, precision=lax.Precision.HIGHEST
    )
    data_wide = padded(exposures, (("tile", 1),), radius)
    model_shard = sky_model
    for step in range(ITERS):
        if step > 0:
            model_wide = widened(broadcast(model_shard).reshape(-1, tile_cols))
        blurred = correlate(model_wide, flipped_ops[member])
        weight_col = weight_rows[member][:, None]
        safe_blur = jnp.where(weight_col > 0.0, blurred, 1.0)
        ratio_wide = weight_col * data_wide[member] / safe_blur
        numerator = correlate(ratio_wide, forward_ops[member])
        shares = lax.all_to_all(numerator.reshape(peers, shard_rows, tile_cols), "visit", 0, 0, tiled=False)
        model_shard = model_shard * jnp.sum(shares, axis=0) / norm_shard
    return model_shard


def solution(mesh):
    return jax.shard_map(
        body,
        mesh=mesh,
        in_specs=(
            P("visit", "tile", None),
            P(("tile", "visit"), None),
            P("visit", None, None),
            P("visit", None),
        ),
        out_specs=P(("tile", "visit"), None),
        check_vma=False,
    )
```

```python
import functools

import jax
import jax.numpy as jnp
from jax import lax
from jax.experimental import pallas as pl
from jax.experimental.pallas import tpu as pltpu
from jax.sharding import PartitionSpec as P

ITERS = 2
LANES = 128
BLOCK = 32
WINDOW = 64
TAPS = 32
MARGIN = WINDOW // 4
VMEM_BYTES = 48 * 1024 * 1024


def split(x):
    high = x.astype(jnp.bfloat16)
    low = (x - high.astype(jnp.float32)).astype(jnp.bfloat16)
    return high, low


def dot_t(x, w):
    return lax.dot_general(x, w, (((1,), (1,)), ((), ())), preferred_element_type=jnp.float32)


def dot_split(x_high, x_low, w_high, w_low):
    return dot_t(x_high, w_high) + (dot_t(x_low, w_high) + dot_t(x_high, w_low))


def lane_of(shape):
    return lax.broadcasted_iota(jnp.int32, shape, len(shape) - 1)


def column_windows(parts):
    rows = parts[0].shape[0] - 8
    lane = lane_of((rows, LANES))
    shifts = sorted({(MARGIN - BLOCK * j) % LANES for j in range(LANES // BLOCK)})
    rolled = [{shift: pltpu.roll(part, shift, 1) for shift in shifts} for part in parts]
    windows = []
    for j in range(len(parts) * LANES // BLOCK):
        start = BLOCK * j - MARGIN
        first = start // LANES
        cut = (first + 1) * LANES - start

        def piece(slab):
            if slab < 0 or slab >= len(parts):
                return jnp.zeros((rows, LANES), jnp.float32)
            near = rolled[slab][(-start) % LANES][:rows]
            far = rolled[slab][(WINDOW - start) % LANES][8:]
            return jnp.where(lane < WINDOW, near, far)

        window = piece(first)
        if cut < WINDOW:
            window = jnp.where(lane % WINDOW < cut, window, piece(first + 1))
        windows.append(window)
    return windows


def put_field(member, parts, z_high, z_low, sum_rows):
    windows = column_windows(parts)
    for pair in range(len(windows) // 2):
        for group in range(2):
            rows = [window[16 * group : 16 * group + sum_rows] for window in windows[2 * pair : 2 * pair + 2]]
            high, low = split(jnp.concatenate(rows, axis=0))
            at = (pl.ds(2 * pair * sum_rows, 2 * sum_rows), pl.ds((2 * member + group) * LANES, LANES))
            z_high[at] = high
            if z_low is not None:
                z_low[at] = low


def gather_taps(t_ref, out_rows):
    sum_rows = out_rows + 8
    lane = lane_of((out_rows, LANES))
    halves = []
    for half in range(t_ref.shape[0] // sum_rows // 4):
        total = None
        for i in range(4):
            picked = None
            for jj in range(4):
                base = (4 * half + jj) * sum_rows + i
                near = t_ref[pl.ds(base, out_rows), pl.ds(0, LANES)]
                far = t_ref[pl.ds(base + 4, out_rows), pl.ds(LANES, LANES)]
                moved = pltpu.roll(near + far, (BLOCK * (jj - i)) % LANES, 1) if jj != i else near + far
                picked = moved if picked is None else jnp.where(lane >= BLOCK * jj, moved, picked)
            total = picked if total is None else total + picked
        halves.append(total)
    return jnp.concatenate(halves, axis=1)


def blur_all(model_refs, wb_high, wb_low, wide, x_high, x_low, g_ref):
    at = 0
    for ref in model_refs:
        wide[pl.ds(at, ref.shape[0]), :] = ref[...]
        at += ref.shape[0]
    wide[pl.ds(at, wide.shape[0] - at), :] = jnp.zeros((wide.shape[0] - at, wide.shape[1]), jnp.float32)
    slabs = wide.shape[1] // LANES
    blocks = wide.shape[1] // BLOCK
    rows = x_high.shape[0] // blocks
    for s in range(8):
        parts = [wide[pl.ds(s, rows + 24), pl.ds(LANES * i, LANES)] for i in range(slabs)]
        windows = column_windows(parts)
        for j in range(blocks):
            high, low = split(windows[j])
            for group in range(2):
                at = (pl.ds(rows * j, rows), pl.ds((8 * group + s) * LANES, LANES))
                x_high[at] = high[16 * group : 16 * group + rows]
                x_low[at] = low[16 * group : 16 * group + rows]
    step = min(2 * LANES, wb_high.shape[0])
    for at in range(0, wb_high.shape[0], step):
        g_ref[:, pl.ds(at, step)] = dot_split(
            x_high[...], x_low[...], wb_high[pl.ds(at, step), :], wb_low[pl.ds(at, step), :]
        )


def blurred_parts(g_ref, member, rows, slabs):
    lane = lane_of((rows, LANES))
    place = member % 4
    parts = []
    for slab in range(slabs):
        picked = None
        for jj in range(4):
            block = g_ref[pl.ds((4 * slab + jj) * rows, rows), pl.ds(member // 4 * LANES, LANES)]
            moved = pltpu.roll(block, (BLOCK * (jj - place)) % LANES, 1) if jj != place else block
            picked = moved if picked is None else jnp.where(lane >= BLOCK * jj, moved, picked)
        parts.append(picked)
    return parts


def update(blurred_of, data, weights, model, norm, wc_high, wc_low, z_high, z_low, t_ref, out):
    members, rows, width = data.shape
    out_rows = out.shape[0]
    for member in range(members):
        weight = jnp.broadcast_to(weights[:, member : member + 1], (rows, LANES))
        parts = []
        for slab, blurred in enumerate(blurred_of(member)):
            safe = jnp.where(weight > 0.0, blurred, 1.0)
            parts.append(weight * data[member, :, pl.ds(LANES * slab, LANES)] / safe)
        put_field(member, parts, z_high, z_low, out_rows + 8)
    t_ref[...] = dot_split(z_high[...], z_low[...], wc_high[...], wc_low[...])
    out[...] = model[...] * gather_taps(t_ref, out_rows) / norm[...]


def first_kernel(hops, table, weights, *refs):
    model_refs, refs = refs[: 2 * hops + 1], refs[2 * hops + 1 :]
    wb_high, wb_low, wc_high, wc_low, blurred, norm = refs[:6]
    wide, x_high, x_low, g_ref, z_high, t_ref = refs[6:]
    members, rows, width = blurred.shape
    lane = lane_of((TAPS // 2, LANES)) % WINDOW
    used = (lane >= 1) & (lane < TAPS)
    for member in range(members):
        entry = table[member]
        straight = jnp.where(used, entry, 0.0)
        flipped = jnp.where(used, pltpu.roll(entry, LANES - TAPS, 1), 0.0)
        for index in range(TAPS // 2):
            group, s = divmod(index, 8)
            band = jnp.broadcast_to(flipped[index : index + 1], (BLOCK, LANES))
            high, low = split(pltpu.roll(band, 0, 1, stride=1, stride_axis=0))
            at = (pl.ds(BLOCK * member, BLOCK), pl.ds(LANES * index, LANES))
            wb_high[at] = high
            wb_low[at] = low
            band = jnp.broadcast_to(straight[index : index + 1], (BLOCK, LANES))
            high, low = split(pltpu.roll(band, 0, 1, stride=1, stride_axis=0))
            at = (pl.ds(BLOCK * s, BLOCK), pl.ds((2 * member + group) * LANES, LANES))
            wc_high[at] = high
            wc_low[at] = low
    blur_all(model_refs, wb_high, wb_low, wide, x_high, x_low, g_ref)
    for member in range(members):
        for slab, part in enumerate(blurred_parts(g_ref, member, rows, width // LANES)):
            blurred[member, :, pl.ds(LANES * slab, LANES)] = part
    out_rows = norm.shape[0]
    for member in range(members):
        weight = jnp.broadcast_to(weights[:, member : member + 1], (rows, LANES))
        put_field(member, [weight] * (width // LANES), z_high, None, out_rows + 8)
    t_ref[...] = dot_t(z_high[...], wc_high[...]) + dot_t(z_high[...], wc_low[...])
    norm[...] = gather_taps(t_ref, out_rows)


def second_kernel(wc_high, wc_low, blurred, data, weights, model, norm, out, z_high, z_low, t_ref):
    width = data.shape[2]

    def blurred_of(member):
        return [blurred[member, :, pl.ds(at, LANES)] for at in range(0, width, LANES)]

    update(blurred_of, data, weights, model, norm, wc_high, wc_low, z_high, z_low, t_ref, out)


def third_kernel(hops, wb_high, wb_low, wc_high, wc_low, data, weights, norm, *refs):
    model_refs, refs = refs[: 2 * hops + 1], refs[2 * hops + 1 :]
    out, wide, x_high, x_low, g_ref, z_high, z_low, t_ref = refs
    members, rows, width = data.shape
    blur_all(model_refs, wb_high, wb_low, wide, x_high, x_low, g_ref)
    blurred_of = functools.partial(blurred_parts, g_ref, rows=rows, slabs=width // LANES)
    update(blurred_of, data, weights, model_refs[hops], norm, wc_high, wc_low, z_high, z_low, t_ref, out)


def call(kernel, out_shape, scratch_shapes, flops, *operands):
    whole = pl.BlockSpec(memory_space=pltpu.VMEM)
    return pl.pallas_call(
        kernel,
        out_shape=out_shape,
        in_specs=[whole] * len(operands),
        out_specs=jax.tree.map(lambda _: whole, out_shape),
        scratch_shapes=scratch_shapes,
        compiler_params=pltpu.CompilerParams(vmem_limit_bytes=VMEM_BYTES),
        cost_estimate=pl.CostEstimate(flops=flops, bytes_accessed=4 * 1024 * 1024, transcendentals=0),
    )(*operands)


def neighbours(shard, hops):
    tiles, members = lax.axis_size("tile"), lax.axis_size("visit")
    place = [i % members * tiles + i // members for i in range(tiles * members)]
    before, after = [], []
    for hop in range(1, hops + 1):
        up = list(zip(place[:-hop], place[hop:]))
        before.insert(0, lax.ppermute(shard, ("visit", "tile"), up))
        after.append(lax.ppermute(shard, ("visit", "tile"), [(j, i) for i, j in up]))
    return before + [shard] + after


def body(exposures, sky_model, blur_kernels, coverage):
    tile_rows, width = exposures.shape[1:]
    shard_rows = sky_model.shape[0]
    kernel_len = blur_kernels.shape[1]
    members = lax.axis_size("visit")
    tiles = lax.axis_size("tile")
    halo = TAPS // 2
    hops = -(-TAPS // shard_rows)
    rows = shard_rows + 2 * halo
    first_row = lax.axis_index("tile") * tile_rows + lax.axis_index("visit") * shard_rows

    kernel = blur_kernels[0] / jnp.sum(blur_kernels[0])
    front = TAPS - kernel_len
    both = jnp.stack([jnp.pad(k, ((front, 0), (front, 0))) for k in (kernel, kernel[::-1, ::-1])])
    table = both.reshape(2, 2, 2, 8, TAPS).transpose(1, 3, 2, 0, 4).reshape(TAPS // 2, LANES)
    cover = jnp.pad(coverage[0].astype(jnp.float32), (0, TAPS // 2 - tiles))
    table = jnp.where(jnp.arange(LANES)[None, :] == 0, cover[:, None], table)
    tables = lax.all_to_all(jnp.broadcast_to(table[None], (members,) + table.shape), "visit", 0, 0)

    counts = exposures[0]
    up = [(i, i + 1) for i in range(tiles - 1)]
    above = lax.ppermute(counts[tile_rows - halo :], "tile", up)
    below = lax.ppermute(counts[:halo], "tile", [(j, i) for i, j in up])
    tall = jnp.concatenate([above, counts, below], axis=0)
    windows = jnp.stack([tall[at : at + rows] for at in range(0, tile_rows, shard_rows)])
    data = lax.all_to_all(windows, "visit", 0, 0)

    near = neighbours(sky_model, hops)
    owner = jnp.floor_divide(first_row - halo + jnp.arange(rows), tile_rows)
    covers = tables[:, :tiles, 0]
    weights = sum(jnp.where(owner[:, None] == t, covers[None, :, t], 0.0) for t in range(tiles))
    weights = jnp.pad(weights, ((0, 0), (0, LANES - members)))

    blocks = width // BLOCK
    f32, bf16 = jnp.float32, jnp.bfloat16
    shape = jax.ShapeDtypeStruct
    depth = TAPS * WINDOW
    sum_rows = shard_rows + 8
    out_shard = shape((shard_rows, width), f32)
    blur_scratch = [
        pltpu.VMEM((shard_rows + 2 * TAPS + 16, width), f32),
        pltpu.VMEM((blocks * rows, depth), bf16),
        pltpu.VMEM((blocks * rows, depth), bf16),
        pltpu.VMEM((blocks * rows, members * BLOCK), f32),
    ]
    field = pltpu.VMEM((blocks * sum_rows, members * 4 * WINDOW), bf16)
    product = pltpu.VMEM((blocks * sum_rows, 8 * BLOCK), f32)
    blur_flops = 6 * blocks * rows * depth * members * BLOCK
    sum_flops = 6 * blocks * sum_rows * members * 4 * WINDOW * 8 * BLOCK
    wb_high, wb_low, wc_high, wc_low, blurred, norm = call(
        functools.partial(first_kernel, hops),
        (
            shape((members * BLOCK, depth), bf16),
            shape((members * BLOCK, depth), bf16),
            shape((8 * BLOCK, members * 4 * WINDOW), bf16),
            shape((8 * BLOCK, members * 4 * WINDOW), bf16),
            shape((members, rows, width), f32),
            out_shard,
        ),
        blur_scratch + [field, product],
        blur_flops + sum_flops,
        tables,
        weights,
        *near,
    )
    model = call(
        second_kernel,
        out_shard,
        [field, field, product],
        sum_flops,
        *(wc_high, wc_low, blurred, data, weights, sky_model, norm),
    )
    for _ in range(ITERS - 1):
        model = call(
            functools.partial(third_kernel, hops),
            out_shard,
            blur_scratch + [field, field, product],
            blur_flops + sum_flops,
            *(wb_high, wb_low, wc_high, wc_low, data, weights, norm),
            *neighbours(model, hops),
        )
    return model


def solution(mesh):
    return jax.shard_map(
        body,
        mesh=mesh,
        in_specs=(
            P("visit", "tile", None),
            P(("tile", "visit"), None),
            P("visit", None, None),
            P("visit", None),
        ),
        out_specs=P(("tile", "visit"), None),
        check_vma=False,
    )
```

```python
import functools

import jax
import jax.numpy as jnp
from jax import lax
from jax.experimental import pallas as pl
from jax.experimental.pallas import tpu as pltpu
from jax.sharding import PartitionSpec as P

ITERS = 2
LANES = 128
BLOCK = 32
WINDOW = 64
TAPS = 32
MARGIN = WINDOW // 4
VMEM_BYTES = 20 * 1024 * 1024


def split(x):
    high = x.astype(jnp.bfloat16)
    low = (x - high.astype(jnp.float32)).astype(jnp.bfloat16)
    return high, low


def dot_t(x, w):
    return lax.dot_general(x, w, (((1,), (1,)), ((), ())), preferred_element_type=jnp.float32)


def dot_split(x_high, x_low, w_high, w_low):
    return dot_t(x_high, w_high) + (dot_t(x_low, w_high) + dot_t(x_high, w_low))


def lane_of(shape):
    return lax.broadcasted_iota(jnp.int32, shape, len(shape) - 1)


def column_windows(parts):
    rows = parts[0].shape[0] - 8
    lane = lane_of((rows, LANES))
    shifts = sorted({(MARGIN - BLOCK * j) % LANES for j in range(LANES // BLOCK)})
    rolled = [{shift: pltpu.roll(part, shift, 1) for shift in shifts} for part in parts]
    windows = []
    for j in range(len(parts) * LANES // BLOCK):
        start = BLOCK * j - MARGIN
        first = start // LANES
        cut = (first + 1) * LANES - start

        def piece(slab):
            if slab < 0 or slab >= len(parts):
                return jnp.zeros((rows, LANES), jnp.float32)
            near = rolled[slab][(-start) % LANES][:rows]
            far = rolled[slab][(WINDOW - start) % LANES][8:]
            return jnp.where(lane < WINDOW, near, far)

        window = piece(first)
        if cut < WINDOW:
            window = jnp.where(lane % WINDOW < cut, window, piece(first + 1))
        windows.append(window)
    return windows


def put_field(member, parts, z_high, z_low, sum_rows):
    windows = column_windows(parts)
    for pair in range(len(windows) // 2):
        for group in range(2):
            rows = [window[16 * group : 16 * group + sum_rows] for window in windows[2 * pair : 2 * pair + 2]]
            high, low = split(jnp.concatenate(rows, axis=0))
            at = (pl.ds(2 * pair * sum_rows, 2 * sum_rows), pl.ds((2 * member + group) * LANES, LANES))
            z_high[at] = high
            if z_low is not None:
                z_low[at] = low


def gather_taps(t_ref, out_rows):
    sum_rows = out_rows + 8
    lane = lane_of((out_rows, LANES))
    halves = []
    for half in range(t_ref.shape[0] // sum_rows // 4):
        total = None
        for i in range(4):
            picked = None
            for jj in range(4):
                base = (4 * half + jj) * sum_rows + i
                near = t_ref[pl.ds(base, out_rows), pl.ds(0, LANES)]
                far = t_ref[pl.ds(base + 4, out_rows), pl.ds(LANES, LANES)]
                moved = pltpu.roll(near + far, (BLOCK * (jj - i)) % LANES, 1) if jj != i else near + far
                picked = moved if picked is None else jnp.where(lane >= BLOCK * jj, moved, picked)
            total = picked if total is None else total + picked
        halves.append(total)
    return jnp.concatenate(halves, axis=1)


def blur_all(model_refs, wb_high, wb_low, wide, x_high, x_low, g_ref):
    at = 0
    for ref in model_refs:
        wide[pl.ds(at, ref.shape[0]), :] = ref[...]
        at += ref.shape[0]
    wide[pl.ds(at, wide.shape[0] - at), :] = jnp.zeros((wide.shape[0] - at, wide.shape[1]), jnp.float32)
    slabs = wide.shape[1] // LANES
    blocks = wide.shape[1] // BLOCK
    rows = x_high.shape[0] // blocks
    for s in range(8):
        parts = [wide[pl.ds(s, rows + 24), pl.ds(LANES * i, LANES)] for i in range(slabs)]
        windows = column_windows(parts)
        for j in range(blocks):
            high, low = split(windows[j])
            for group in range(2):
                at = (pl.ds(rows * j, rows), pl.ds((8 * group + s) * LANES, LANES))
                x_high[at] = high[16 * group : 16 * group + rows]
                x_low[at] = low[16 * group : 16 * group + rows]
    step = min(2 * LANES, wb_high.shape[0])
    for at in range(0, wb_high.shape[0], step):
        g_ref[:, pl.ds(at, step)] = dot_split(
            x_high[...], x_low[...], wb_high[pl.ds(at, step), :], wb_low[pl.ds(at, step), :]
        )


def blurred_parts(g_ref, member, rows, slabs):
    lane = lane_of((rows, LANES))
    place = member % 4
    parts = []
    for slab in range(slabs):
        picked = None
        for jj in range(4):
            block = g_ref[pl.ds((4 * slab + jj) * rows, rows), pl.ds(member // 4 * LANES, LANES)]
            moved = pltpu.roll(block, (BLOCK * (jj - place)) % LANES, 1) if jj != place else block
            picked = moved if picked is None else jnp.where(lane >= BLOCK * jj, moved, picked)
        parts.append(picked)
    return parts


def update(blurred_of, data, weights, model, norm, wc_high, wc_low, z_high, z_low, t_ref, out):
    members, rows, width = data.shape
    out_rows = out.shape[0]
    for member in range(members):
        weight = jnp.broadcast_to(weights[:, member : member + 1], (rows, LANES))
        parts = []
        for slab, blurred in enumerate(blurred_of(member)):
            safe = jnp.where(weight > 0.0, blurred, 1.0)
            parts.append(weight * data[member, :, pl.ds(LANES * slab, LANES)] / safe)
        put_field(member, parts, z_high, z_low, out_rows + 8)
    t_ref[...] = dot_split(z_high[...], z_low[...], wc_high[...], wc_low[...])
    out[...] = model[...] * gather_taps(t_ref, out_rows) / norm[...]


def table_kernel(cover, kernels, out, padded):
    kernel = kernels[0]
    size = kernel.shape[0]
    front = TAPS - size
    padded[...] = jnp.zeros(padded.shape, jnp.float32)
    padded[pl.ds(front, size), pl.ds(front, size)] = kernel / jnp.sum(kernel)
    straight = padded[...]
    row = lax.broadcasted_iota(jnp.int32, (TAPS, TAPS), 0)
    turn_rows = (row + lane_of((TAPS, TAPS)) == TAPS).astype(jnp.float32)
    row = lax.broadcasted_iota(jnp.int32, (LANES, LANES), 0)
    turn_lanes = (row + lane_of((LANES, LANES)) == TAPS).astype(jnp.float32)
    exact = functools.partial(jnp.dot, precision=lax.Precision.HIGHEST, preferred_element_type=jnp.float32)
    flipped = exact(exact(turn_rows, straight), turn_lanes)
    both = straight + pltpu.roll(flipped, TAPS, 1)
    half = [both[8 * i : 8 * i + 8] for i in range(4)]
    table = jnp.concatenate([half[2 * i] + pltpu.roll(half[2 * i + 1], WINDOW, 1) for i in range(2)], axis=0)
    row = lax.broadcasted_iota(jnp.int32, table.shape, 0)
    lane = lane_of(table.shape)
    for tile in range(cover.shape[1]):
        table = jnp.where((row == tile) & (lane == 0), cover[0, tile].astype(jnp.float32), table)
    out[...] = jnp.broadcast_to(table[None], out.shape)


def windows_kernel(halo, counts, above, below, out):
    peers, rows, _ = out.shape
    tile_rows = counts.shape[1]
    step = rows - 2 * halo
    for peer in range(peers):
        first = peer * step - halo
        last = first + rows
        at = 0
        if first < 0:
            out[peer, pl.ds(0, -first), :] = above[pl.ds(halo + first, -first), :]
            at = -first
        inner = min(last, tile_rows) - max(first, 0)
        out[peer, pl.ds(at, inner), :] = counts[0, pl.ds(max(first, 0), inner), :]
        if last > tile_rows:
            out[peer, pl.ds(at + inner, last - tile_rows), :] = below[pl.ds(0, last - tile_rows), :]


def first_kernel(hops, table, weights, *refs):
    model_refs, refs = refs[: 2 * hops + 1], refs[2 * hops + 1 :]
    wb_high, wb_low, wc_high, wc_low, blurred, norm = refs[:6]
    wide, x_high, x_low, g_ref, z_high, t_ref = refs[6:]
    members, rows, width = blurred.shape
    lane = lane_of((TAPS // 2, LANES)) % WINDOW
    used = (lane >= 1) & (lane < TAPS)
    for member in range(members):
        entry = table[member]
        straight = jnp.where(used, entry, 0.0)
        flipped = jnp.where(used, pltpu.roll(entry, LANES - TAPS, 1), 0.0)
        for index in range(TAPS // 2):
            group, s = divmod(index, 8)
            band = jnp.broadcast_to(flipped[index : index + 1], (BLOCK, LANES))
            high, low = split(pltpu.roll(band, 0, 1, stride=1, stride_axis=0))
            at = (pl.ds(BLOCK * member, BLOCK), pl.ds(LANES * index, LANES))
            wb_high[at] = high
            wb_low[at] = low
            band = jnp.broadcast_to(straight[index : index + 1], (BLOCK, LANES))
            high, low = split(pltpu.roll(band, 0, 1, stride=1, stride_axis=0))
            at = (pl.ds(BLOCK * s, BLOCK), pl.ds((2 * member + group) * LANES, LANES))
            wc_high[at] = high
            wc_low[at] = low
    blur_all(model_refs, wb_high, wb_low, wide, x_high, x_low, g_ref)
    for member in range(members):
        for slab, part in enumerate(blurred_parts(g_ref, member, rows, width // LANES)):
            blurred[member, :, pl.ds(LANES * slab, LANES)] = part
    out_rows = norm.shape[0]
    for member in range(members):
        weight = jnp.broadcast_to(weights[:, member : member + 1], (rows, LANES))
        put_field(member, [weight] * (width // LANES), z_high, None, out_rows + 8)
    t_ref[...] = dot_t(z_high[...], wc_high[...]) + dot_t(z_high[...], wc_low[...])
    norm[...] = gather_taps(t_ref, out_rows)


def second_kernel(wc_high, wc_low, blurred, data, weights, model, norm, out, z_high, z_low, t_ref):
    width = data.shape[2]

    def blurred_of(member):
        return [blurred[member, :, pl.ds(at, LANES)] for at in range(0, width, LANES)]

    update(blurred_of, data, weights, model, norm, wc_high, wc_low, z_high, z_low, t_ref, out)


def third_kernel(hops, wb_high, wb_low, wc_high, wc_low, data, weights, norm, *refs):
    model_refs, refs = refs[: 2 * hops + 1], refs[2 * hops + 1 :]
    out, wide, x_high, x_low, g_ref, z_high, z_low, t_ref = refs
    members, rows, width = data.shape
    blur_all(model_refs, wb_high, wb_low, wide, x_high, x_low, g_ref)
    blurred_of = functools.partial(blurred_parts, g_ref, rows=rows, slabs=width // LANES)
    update(blurred_of, data, weights, model_refs[hops], norm, wc_high, wc_low, z_high, z_low, t_ref, out)


def call(kernel, out_shape, scratch_shapes, flops, *operands):
    whole = pl.BlockSpec(memory_space=pltpu.VMEM)
    scalars = pl.BlockSpec(memory_space=pltpu.SMEM)
    return pl.pallas_call(
        kernel,
        out_shape=out_shape,
        in_specs=[scalars if jnp.issubdtype(o.dtype, jnp.integer) else whole for o in operands],
        out_specs=jax.tree.map(lambda _: whole, out_shape),
        scratch_shapes=scratch_shapes,
        compiler_params=pltpu.CompilerParams(vmem_limit_bytes=VMEM_BYTES),
        cost_estimate=pl.CostEstimate(flops=flops, bytes_accessed=4 * 1024 * 1024, transcendentals=0),
    )(*operands)


def neighbours(shard, hops):
    tiles, members = lax.axis_size("tile"), lax.axis_size("visit")
    place = [i % members * tiles + i // members for i in range(tiles * members)]
    before, after = [], []
    for hop in range(1, hops + 1):
        up = list(zip(place[:-hop], place[hop:]))
        before.insert(0, lax.ppermute(shard, ("visit", "tile"), up))
        after.append(lax.ppermute(shard, ("visit", "tile"), [(j, i) for i, j in up]))
    return before + [shard] + after


def body(exposures, sky_model, blur_kernels, coverage):
    tile_rows, width = exposures.shape[1:]
    shard_rows = sky_model.shape[0]
    members = lax.axis_size("visit")
    tiles = lax.axis_size("tile")
    halo = TAPS // 2
    hops = -(-TAPS // shard_rows)
    rows = shard_rows + 2 * halo
    first_row = lax.axis_index("tile") * tile_rows + lax.axis_index("visit") * shard_rows

    f32, bf16 = jnp.float32, jnp.bfloat16
    shape = jax.ShapeDtypeStruct
    tables = call(
        table_kernel,
        shape((members, TAPS // 2, LANES), f32),
        [pltpu.VMEM((TAPS, LANES), f32)],
        1 << 22,
        *(coverage, blur_kernels),
    )
    tables = lax.all_to_all(tables, "visit", 0, 0)

    up = [(i, i + 1) for i in range(tiles - 1)]
    above = lax.ppermute(exposures[0, tile_rows - halo :], "tile", up)
    below = lax.ppermute(exposures[0, :halo], "tile", [(j, i) for i, j in up])
    windows = call(
        functools.partial(windows_kernel, halo),
        shape((members, rows, width), f32),
        [],
        1 << 22,
        *(exposures, above, below),
    )
    data = lax.all_to_all(windows, "visit", 0, 0)

    near = neighbours(sky_model, hops)
    owner = jnp.floor_divide(first_row - halo + jnp.arange(rows), tile_rows)
    covers = tables[:, :tiles, 0]
    weights = sum(jnp.where(owner[:, None] == t, covers[None, :, t], 0.0) for t in range(tiles))
    weights = jnp.pad(weights, ((0, 0), (0, LANES - members)))

    blocks = width // BLOCK
    depth = TAPS * WINDOW
    sum_rows = shard_rows + 8
    out_shard = shape((shard_rows, width), f32)
    blur_scratch = [
        pltpu.VMEM((shard_rows + 2 * TAPS + 16, width), f32),
        pltpu.VMEM((blocks * rows, depth), bf16),
        pltpu.VMEM((blocks * rows, depth), bf16),
        pltpu.VMEM((blocks * rows, members * BLOCK), f32),
    ]
    field = pltpu.VMEM((blocks * sum_rows, members * 4 * WINDOW), bf16)
    product = pltpu.VMEM((blocks * sum_rows, 8 * BLOCK), f32)
    blur_flops = 6 * blocks * rows * depth * members * BLOCK
    sum_flops = 6 * blocks * sum_rows * members * 4 * WINDOW * 8 * BLOCK
    wb_high, wb_low, wc_high, wc_low, blurred, norm = call(
        functools.partial(first_kernel, hops),
        (
            shape((members * BLOCK, depth), bf16),
            shape((members * BLOCK, depth), bf16),
            shape((8 * BLOCK, members * 4 * WINDOW), bf16),
            shape((8 * BLOCK, members * 4 * WINDOW), bf16),
            shape((members, rows, width), f32),
            out_shard,
        ),
        blur_scratch + [field, product],
        blur_flops + sum_flops,
        tables,
        weights,
        *near,
    )
    model = call(
        second_kernel,
        out_shard,
        [field, field, product],
        sum_flops,
        *(wc_high, wc_low, blurred, data, weights, sky_model, norm),
    )
    for _ in range(ITERS - 1):
        model = call(
            functools.partial(third_kernel, hops),
            out_shard,
            blur_scratch + [field, field, product],
            blur_flops + sum_flops,
            *(wb_high, wb_low, wc_high, wc_low, data, weights, norm),
            *neighbours(model, hops),
        )
    return model


def solution(mesh):
    return jax.shard_map(
        body,
        mesh=mesh,
        in_specs=(
            P("visit", "tile", None),
            P(("tile", "visit"), None),
            P("visit", None, None),
            P("visit", None),
        ),
        out_specs=P(("tile", "visit"), None),
        check_vma=False,
    )
```

```python
import functools

import jax
import jax.numpy as jnp
from jax import lax
from jax.experimental import pallas as pl
from jax.experimental.pallas import tpu as pltpu
from jax.sharding import PartitionSpec as P

ITERS = 2
LANES = 128
BLOCK = 32
WINDOW = 64
TAPS = 32
MARGIN = WINDOW // 4
VMEM_BYTES = 20 * 1024 * 1024


def split(x):
    high = x.astype(jnp.bfloat16)
    low = (x - high.astype(jnp.float32)).astype(jnp.bfloat16)
    return high, low


def dot_t(x, w):
    return lax.dot_general(x, w, (((1,), (1,)), ((), ())), preferred_element_type=jnp.float32)


def dot_split(x_high, x_low, w_high, w_low):
    return dot_t(x_high, w_high) + (dot_t(x_low, w_high) + dot_t(x_high, w_low))


def lane_of(shape):
    return lax.broadcasted_iota(jnp.int32, shape, len(shape) - 1)


def column_windows(parts):
    rows = parts[0].shape[0] - 8
    lane = lane_of((rows, LANES))
    shifts = sorted({(MARGIN - BLOCK * j) % LANES for j in range(LANES // BLOCK)})
    rolled = [{shift: pltpu.roll(part, shift, 1) for shift in shifts} for part in parts]
    windows = []
    for j in range(len(parts) * LANES // BLOCK):
        start = BLOCK * j - MARGIN
        first = start // LANES
        cut = (first + 1) * LANES - start

        def piece(slab):
            if slab < 0 or slab >= len(parts):
                return jnp.zeros((rows, LANES), jnp.float32)
            near = rolled[slab][(-start) % LANES][:rows]
            far = rolled[slab][(WINDOW - start) % LANES][8:]
            return jnp.where(lane < WINDOW, near, far)

        window = piece(first)
        if cut < WINDOW:
            window = jnp.where(lane % WINDOW < cut, window, piece(first + 1))
        windows.append(window)
    return windows


def put_field(member, parts, z_high, z_low, sum_rows):
    windows = column_windows(parts)
    for pair in range(len(windows) // 2):
        for group in range(2):
            rows = [window[16 * group : 16 * group + sum_rows] for window in windows[2 * pair : 2 * pair + 2]]
            high, low = split(jnp.concatenate(rows, axis=0))
            at = (pl.ds(2 * pair * sum_rows, 2 * sum_rows), pl.ds((2 * member + group) * LANES, LANES))
            z_high[at] = high
            if z_low is not None:
                z_low[at] = low


def gather_taps(t_ref, out_rows):
    sum_rows = out_rows + 8
    lane = lane_of((out_rows, LANES))
    halves = []
    for half in range(t_ref.shape[0] // sum_rows // 4):
        total = None
        for i in range(4):
            picked = None
            for jj in range(4):
                base = (4 * half + jj) * sum_rows + i
                near = t_ref[pl.ds(base, out_rows), pl.ds(0, LANES)]
                far = t_ref[pl.ds(base + 4, out_rows), pl.ds(LANES, LANES)]
                moved = pltpu.roll(near + far, (BLOCK * (jj - i)) % LANES, 1) if jj != i else near + far
                picked = moved if picked is None else jnp.where(lane >= BLOCK * jj, moved, picked)
            total = picked if total is None else total + picked
        halves.append(total)
    return jnp.concatenate(halves, axis=1)


def blur_all(model_refs, wb_high, wb_low, wide, x_high, x_low, g_ref):
    at = 0
    for ref in model_refs:
        wide[pl.ds(at, ref.shape[0]), :] = ref[...]
        at += ref.shape[0]
    wide[pl.ds(at, wide.shape[0] - at), :] = jnp.zeros((wide.shape[0] - at, wide.shape[1]), jnp.float32)
    slabs = wide.shape[1] // LANES
    blocks = wide.shape[1] // BLOCK
    rows = x_high.shape[0] // blocks
    for s in range(8):
        parts = [wide[pl.ds(s, rows + 24), pl.ds(LANES * i, LANES)] for i in range(slabs)]
        windows = column_windows(parts)
        for j in range(blocks):
            high, low = split(windows[j])
            for group in range(2):
                at = (pl.ds(rows * j, rows), pl.ds((8 * group + s) * LANES, LANES))
                x_high[at] = high[16 * group : 16 * group + rows]
                x_low[at] = low[16 * group : 16 * group + rows]
    step = min(2 * LANES, wb_high.shape[0])
    for at in range(0, wb_high.shape[0], step):
        g_ref[:, pl.ds(at, step)] = dot_split(
            x_high[...], x_low[...], wb_high[pl.ds(at, step), :], wb_low[pl.ds(at, step), :]
        )


def blurred_parts(g_ref, member, rows, slabs):
    lane = lane_of((rows, LANES))
    place = member % 4
    parts = []
    for slab in range(slabs):
        picked = None
        for jj in range(4):
            block = g_ref[pl.ds((4 * slab + jj) * rows, rows), pl.ds(member // 4 * LANES, LANES)]
            moved = pltpu.roll(block, (BLOCK * (jj - place)) % LANES, 1) if jj != place else block
            picked = moved if picked is None else jnp.where(lane >= BLOCK * jj, moved, picked)
        parts.append(picked)
    return parts


def table_of(kernel, cover, padded):
    size = kernel.shape[0]
    front = TAPS - size
    padded[...] = jnp.zeros(padded.shape, jnp.float32)
    padded[pl.ds(front, size), pl.ds(front, size)] = kernel / jnp.sum(kernel)
    straight = padded[...]
    row = lax.broadcasted_iota(jnp.int32, (TAPS, TAPS), 0)
    turn_rows = (row + lane_of((TAPS, TAPS)) == TAPS).astype(jnp.float32)
    row = lax.broadcasted_iota(jnp.int32, (LANES, LANES), 0)
    turn_lanes = (row + lane_of((LANES, LANES)) == TAPS).astype(jnp.float32)
    exact = functools.partial(jnp.dot, precision=lax.Precision.HIGHEST, preferred_element_type=jnp.float32)
    flipped = exact(exact(turn_rows, straight), turn_lanes)
    both = straight + pltpu.roll(flipped, TAPS, 1)
    half = [both[8 * i : 8 * i + 8] for i in range(4)]
    groups = [half[2 * i] + pltpu.roll(half[2 * i + 1], WINDOW, 1) for i in range(2)]
    row = lax.broadcasted_iota(jnp.int32, groups[0].shape, 0)
    lane = lane_of(groups[0].shape)
    for tile in range(cover.shape[1]):
        spot = (row == tile % 8) & (lane == 0)
        groups[tile // 8] = jnp.where(spot, cover[0, tile].astype(jnp.float32), groups[tile // 8])
    return groups


def send_kernel(cover, counts, kernels, out, padded):
    groups = table_of(kernels[0], cover, padded)
    own = out.shape[1] - 8
    for peer in range(out.shape[0]):
        out[peer, pl.ds(0, own), :] = counts[0, pl.ds(peer * own, own), :]
        for group in range(2):
            out[peer, pl.ds(own, 8), pl.ds(LANES * group, LANES)] = groups[group]


def weight_of(member, first_row, tile_rows, tiles, received, rows):
    own = received.shape[1] - 8
    row = first_row[0, 0] - TAPS // 2 + lax.broadcasted_iota(jnp.int32, (rows, LANES), 0)
    weight = jnp.zeros((rows, LANES), jnp.float32)
    for tile in range(tiles):
        entry = received[member, pl.ds(own + tile % 8, 1), pl.ds(tile // 8 * LANES, LANES)]
        inside = (row >= tile * tile_rows) & (row < (tile + 1) * tile_rows)
        weight = jnp.where(inside, jnp.broadcast_to(entry[:, 0:1], (rows, LANES)), weight)
    return weight


def update(blurred_of, weights_of, data_refs, model, norm, wc_high, wc_low, z_high, z_low, t_ref, out):
    out_rows, width = out.shape
    members = z_high.shape[1] // (4 * WINDOW)
    rows = out_rows + TAPS
    above = (len(data_refs) // 2) * out_rows - TAPS // 2
    for member in range(members):
        weight = weights_of(member)
        parts = []
        for slab, blurred in enumerate(blurred_of(member)):
            pieces = [ref[member, pl.ds(0, out_rows), pl.ds(LANES * slab, LANES)] for ref in data_refs]
            counts = jnp.concatenate(pieces, axis=0)[above : above + rows]
            safe = jnp.where(weight > 0.0, blurred, 1.0)
            parts.append(weight * counts / safe)
        put_field(member, parts, z_high, z_low, out_rows + 8)
    t_ref[...] = dot_split(z_high[...], z_low[...], wc_high[...], wc_low[...])
    out[...] = model[...] * gather_taps(t_ref, out_rows) / norm[...]


def first_kernel(weights_at, hops, first_row, received, *refs):
    model_refs, refs = refs[: 2 * hops + 1], refs[2 * hops + 1 :]
    wb_high, wb_low, wc_high, wc_low, blurred, norm = refs[:6]
    wide, x_high, x_low, g_ref, z_high, t_ref = refs[6:]
    members, rows, width = blurred.shape
    own = received.shape[1] - 8
    lane = lane_of((8, LANES)) % WINDOW
    used = (lane >= 1) & (lane < TAPS)
    for member in range(members):
        for group in range(2):
            entry = received[member, pl.ds(own, 8), pl.ds(LANES * group, LANES)]
            straight = jnp.where(used, entry, 0.0)
            flipped = jnp.where(used, pltpu.roll(entry, LANES - TAPS, 1), 0.0)
            for s in range(8):
                band = jnp.broadcast_to(flipped[s : s + 1], (BLOCK, LANES))
                high, low = split(pltpu.roll(band, 0, 1, stride=1, stride_axis=0))
                at = (pl.ds(BLOCK * member, BLOCK), pl.ds(LANES * (8 * group + s), LANES))
                wb_high[at] = high
                wb_low[at] = low
                band = jnp.broadcast_to(straight[s : s + 1], (BLOCK, LANES))
                high, low = split(pltpu.roll(band, 0, 1, stride=1, stride_axis=0))
                at = (pl.ds(BLOCK * s, BLOCK), pl.ds((2 * member + group) * LANES, LANES))
                wc_high[at] = high
                wc_low[at] = low
    blur_all(model_refs, wb_high, wb_low, wide, x_high, x_low, g_ref)
    for member in range(members):
        for slab, part in enumerate(blurred_parts(g_ref, member, rows, width // LANES)):
            blurred[member, :, pl.ds(LANES * slab, LANES)] = part
    out_rows = norm.shape[0]
    for member in range(members):
        weight = weights_at(member, first_row=first_row, received=received)
        put_field(member, [weight] * (width // LANES), z_high, None, out_rows + 8)
    t_ref[...] = dot_t(z_high[...], wc_high[...]) + dot_t(z_high[...], wc_low[...])
    norm[...] = gather_taps(t_ref, out_rows)


def second_kernel(weights_at, data_hops, first_row, wc_high, wc_low, blurred, model, norm, *refs):
    data_refs, refs = refs[: 2 * data_hops + 1], refs[2 * data_hops + 1 :]
    out, z_high, z_low, t_ref = refs
    width = out.shape[1]

    def blurred_of(member):
        return [blurred[member, :, pl.ds(at, LANES)] for at in range(0, width, LANES)]

    weights_of = functools.partial(weights_at, first_row=first_row, received=data_refs[data_hops])
    update(blurred_of, weights_of, data_refs, model, norm, wc_high, wc_low, z_high, z_low, t_ref, out)


def third_kernel(weights_at, data_hops, hops, first_row, wb_high, wb_low, wc_high, wc_low, norm, *refs):
    data_refs, refs = refs[: 2 * data_hops + 1], refs[2 * data_hops + 1 :]
    model_refs, refs = refs[: 2 * hops + 1], refs[2 * hops + 1 :]
    out, wide, x_high, x_low, g_ref, z_high, z_low, t_ref = refs
    out_rows, width = out.shape
    blur_all(model_refs, wb_high, wb_low, wide, x_high, x_low, g_ref)
    blurred_of = functools.partial(blurred_parts, g_ref, rows=out_rows + TAPS, slabs=width // LANES)
    weights_of = functools.partial(weights_at, first_row=first_row, received=data_refs[data_hops])
    update(blurred_of, weights_of, data_refs, model_refs[hops], norm, wc_high, wc_low, z_high, z_low, t_ref, out)


def call(kernel, out_shape, scratch_shapes, flops, *operands):
    whole = pl.BlockSpec(memory_space=pltpu.VMEM)
    scalars = pl.BlockSpec(memory_space=pltpu.SMEM)
    return pl.pallas_call(
        kernel,
        out_shape=out_shape,
        in_specs=[scalars if jnp.issubdtype(o.dtype, jnp.integer) else whole for o in operands],
        out_specs=jax.tree.map(lambda _: whole, out_shape),
        scratch_shapes=scratch_shapes,
        compiler_params=pltpu.CompilerParams(vmem_limit_bytes=VMEM_BYTES),
        cost_estimate=pl.CostEstimate(flops=flops, bytes_accessed=4 * 1024 * 1024, transcendentals=0),
    )(*operands)


def neighbours(shard, hops):
    tiles, members = lax.axis_size("tile"), lax.axis_size("visit")
    place = [i % members * tiles + i // members for i in range(tiles * members)]
    before, after = [], []
    for hop in range(1, hops + 1):
        up = list(zip(place[:-hop], place[hop:]))
        before.insert(0, lax.ppermute(shard, ("visit", "tile"), up))
        after.append(lax.ppermute(shard, ("visit", "tile"), [(j, i) for i, j in up]))
    return before + [shard] + after


def body(exposures, sky_model, blur_kernels, coverage):
    tile_rows, width = exposures.shape[1:]
    shard_rows = sky_model.shape[0]
    members = lax.axis_size("visit")
    tiles = lax.axis_size("tile")
    halo = TAPS // 2
    hops = -(-TAPS // shard_rows)
    data_hops = -(-halo // shard_rows)
    rows = shard_rows + 2 * halo
    first_row = lax.axis_index("tile") * tile_rows + lax.axis_index("visit") * shard_rows
    first_row = first_row.reshape(1, 1)

    f32, bf16 = jnp.float32, jnp.bfloat16
    shape = jax.ShapeDtypeStruct
    blocks = width // BLOCK
    depth = TAPS * WINDOW
    sum_rows = shard_rows + 8
    out_shard = shape((shard_rows, width), f32)

    sent = call(
        send_kernel,
        shape((members, shard_rows + 8, width), f32),
        [pltpu.VMEM((TAPS, LANES), f32)],
        1 << 22,
        *(coverage, exposures, blur_kernels),
    )
    received = lax.all_to_all(sent, "visit", 0, 0)
    near = neighbours(sky_model, hops)
    data = neighbours(received[:, :shard_rows], data_hops)
    data[data_hops] = received

    blur_scratch = [
        pltpu.VMEM((shard_rows + 2 * TAPS + 16, width), f32),
        pltpu.VMEM((blocks * rows, depth), bf16),
        pltpu.VMEM((blocks * rows, depth), bf16),
        pltpu.VMEM((blocks * rows, members * BLOCK), f32),
    ]
    field = pltpu.VMEM((blocks * sum_rows, members * 4 * WINDOW), bf16)
    product = pltpu.VMEM((blocks * sum_rows, 8 * BLOCK), f32)
    blur_flops = 6 * blocks * rows * depth * members * BLOCK
    sum_flops = 6 * blocks * sum_rows * members * 4 * WINDOW * 8 * BLOCK
    weights_at = functools.partial(weight_of, tile_rows=tile_rows, tiles=tiles, rows=rows)
    wb_high, wb_low, wc_high, wc_low, blurred, norm = call(
        functools.partial(first_kernel, weights_at, hops),
        (
            shape((members * BLOCK, depth), bf16),
            shape((members * BLOCK, depth), bf16),
            shape((8 * BLOCK, members * 4 * WINDOW), bf16),
            shape((8 * BLOCK, members * 4 * WINDOW), bf16),
            shape((members, rows, width), f32),
            out_shard,
        ),
        blur_scratch + [field, product],
        blur_flops + sum_flops,
        first_row,
        received,
        *near,
    )
    model = call(
        functools.partial(second_kernel, weights_at, data_hops),
        out_shard,
        [field, field, product],
        sum_flops,
        *(first_row, wc_high, wc_low, blurred, sky_model, norm),
        *data,
    )
    for _ in range(ITERS - 1):
        model = call(
            functools.partial(third_kernel, weights_at, data_hops, hops),
            out_shard,
            blur_scratch + [field, field, product],
            blur_flops + sum_flops,
            *(first_row, wb_high, wb_low, wc_high, wc_low, norm),
            *data,
            *neighbours(model, hops),
        )
    return model


def solution(mesh):
    return jax.shard_map(
        body,
        mesh=mesh,
        in_specs=(
            P("visit", "tile", None),
            P(("tile", "visit"), None),
            P("visit", None, None),
            P("visit", None),
        ),
        out_specs=P(("tile", "visit"), None),
        check_vma=False,
    )
```

```python
import functools

import jax
import jax.numpy as jnp
from jax import lax
from jax.experimental import pallas as pl
from jax.experimental.pallas import tpu as pltpu
from jax.sharding import PartitionSpec as P

ITERS = 2
LANES = 128
BLOCK = 32
WINDOW = 64
TAPS = 32
MARGIN = WINDOW // 4
VMEM_BYTES = 20 * 1024 * 1024


def split(x):
    high = x.astype(jnp.bfloat16)
    low = (x - high.astype(jnp.float32)).astype(jnp.bfloat16)
    return high, low


def dot_t(x, w):
    return lax.dot_general(x, w, (((1,), (1,)), ((), ())), preferred_element_type=jnp.float32)


def dot_split(x_high, x_low, w_high, w_low):
    return dot_t(x_high, w_high) + (dot_t(x_low, w_high) + dot_t(x_high, w_low))


def lane_of(shape):
    return lax.broadcasted_iota(jnp.int32, shape, len(shape) - 1)


def column_windows(parts):
    rows = parts[0].shape[0] - 8
    lane = lane_of((rows, LANES))
    shifts = sorted({(MARGIN - BLOCK * j) % LANES for j in range(LANES // BLOCK)})
    rolled = [{shift: pltpu.roll(part, shift, 1) for shift in shifts} for part in parts]
    windows = []
    for j in range(len(parts) * LANES // BLOCK):
        start = BLOCK * j - MARGIN
        first = start // LANES
        cut = (first + 1) * LANES - start

        def piece(slab):
            if slab < 0 or slab >= len(parts):
                return jnp.zeros((rows, LANES), jnp.float32)
            near = rolled[slab][(-start) % LANES][:rows]
            far = rolled[slab][(WINDOW - start) % LANES][8:]
            return jnp.where(lane < WINDOW, near, far)

        window = piece(first)
        if cut < WINDOW:
            window = jnp.where(lane % WINDOW < cut, window, piece(first + 1))
        windows.append(window)
    return windows


def put_field(member, parts, z_high, z_low, sum_rows):
    windows = column_windows(parts)
    for pair in range(len(windows) // 2):
        for group in range(2):
            rows = [window[16 * group : 16 * group + sum_rows] for window in windows[2 * pair : 2 * pair + 2]]
            high, low = split(jnp.concatenate(rows, axis=0))
            at = (pl.ds(2 * pair * sum_rows, 2 * sum_rows), pl.ds((2 * member + group) * LANES, LANES))
            z_high[at] = high
            if z_low is not None:
                z_low[at] = low


def gather_taps(t_ref, out_rows):
    sum_rows = out_rows + 8
    lane = lane_of((out_rows, LANES))
    halves = []
    for half in range(t_ref.shape[0] // sum_rows // 4):
        total = None
        for i in range(4):
            picked = None
            for jj in range(4):
                base = (4 * half + jj) * sum_rows + i
                near = t_ref[pl.ds(base, out_rows), pl.ds(0, LANES)]
                far = t_ref[pl.ds(base + 4, out_rows), pl.ds(LANES, LANES)]
                moved = pltpu.roll(near + far, (BLOCK * (jj - i)) % LANES, 1) if jj != i else near + far
                picked = moved if picked is None else jnp.where(lane >= BLOCK * jj, moved, picked)
            total = picked if total is None else total + picked
        halves.append(total)
    return jnp.concatenate(halves, axis=1)


def blur_all(model_refs, wb_high, wb_low, wide, x_high, x_low, g_ref):
    at = 0
    for ref in model_refs:
        wide[pl.ds(at, ref.shape[0]), :] = ref[...]
        at += ref.shape[0]
    wide[pl.ds(at, wide.shape[0] - at), :] = jnp.zeros((wide.shape[0] - at, wide.shape[1]), jnp.float32)
    slabs = wide.shape[1] // LANES
    blocks = wide.shape[1] // BLOCK
    rows = x_high.shape[0] // blocks
    for s in range(8):
        parts = [wide[pl.ds(s, rows + 24), pl.ds(LANES * i, LANES)] for i in range(slabs)]
        windows = column_windows(parts)
        for j in range(blocks):
            high, low = split(windows[j])
            for group in range(2):
                at = (pl.ds(rows * j, rows), pl.ds((8 * group + s) * LANES, LANES))
                x_high[at] = high[16 * group : 16 * group + rows]
                x_low[at] = low[16 * group : 16 * group + rows]
    step = min(2 * LANES, wb_high.shape[0])
    for at in range(0, wb_high.shape[0], step):
        g_ref[:, pl.ds(at, step)] = dot_split(
            x_high[...], x_low[...], wb_high[pl.ds(at, step), :], wb_low[pl.ds(at, step), :]
        )


def blurred_parts(g_ref, member, rows, slabs):
    lane = lane_of((rows, LANES))
    place = member % 4
    parts = []
    for slab in range(slabs):
        picked = None
        for jj in range(4):
            block = g_ref[pl.ds((4 * slab + jj) * rows, rows), pl.ds(member // 4 * LANES, LANES)]
            moved = pltpu.roll(block, (BLOCK * (jj - place)) % LANES, 1) if jj != place else block
            picked = moved if picked is None else jnp.where(lane >= BLOCK * jj, moved, picked)
        parts.append(picked)
    return parts


def table_of(kernel, cover, padded):
    size = kernel.shape[0]
    front = TAPS - size
    padded[...] = jnp.zeros(padded.shape, jnp.float32)
    padded[pl.ds(front, size), pl.ds(front, size)] = kernel / jnp.sum(kernel)
    straight = padded[...]
    row = lax.broadcasted_iota(jnp.int32, (TAPS, TAPS), 0)
    turn_rows = (row + lane_of((TAPS, TAPS)) == TAPS).astype(jnp.float32)
    row = lax.broadcasted_iota(jnp.int32, (LANES, LANES), 0)
    turn_lanes = (row + lane_of((LANES, LANES)) == TAPS).astype(jnp.float32)
    exact = functools.partial(jnp.dot, precision=lax.Precision.HIGHEST, preferred_element_type=jnp.float32)
    flipped = exact(exact(turn_rows, straight), turn_lanes)
    both = straight + pltpu.roll(flipped, TAPS, 1)
    half = [both[8 * i : 8 * i + 8] for i in range(4)]
    groups = [half[2 * i] + pltpu.roll(half[2 * i + 1], WINDOW, 1) for i in range(2)]
    row = lax.broadcasted_iota(jnp.int32, groups[0].shape, 0)
    lane = lane_of(groups[0].shape)
    for tile in range(cover.shape[1]):
        spot = (row == tile % 8) & (lane == 0)
        groups[tile // 8] = jnp.where(spot, cover[0, tile].astype(jnp.float32), groups[tile // 8])
    return groups


def send_kernel(cover, counts, kernels, out, padded):
    groups = table_of(kernels[0], cover, padded)
    own = out.shape[1] - 8
    for peer in range(out.shape[0]):
        out[peer, pl.ds(0, own), :] = counts[0, pl.ds(peer * own, own), :]
        for group in range(2):
            out[peer, pl.ds(own, 8), pl.ds(LANES * group, LANES)] = groups[group]


def weight_of(member, first_row, tile_rows, tiles, received, rows):
    own = received.shape[1] - 8
    row = first_row[0, 0] - TAPS // 2 + lax.broadcasted_iota(jnp.int32, (rows, LANES), 0)
    weight = jnp.zeros((rows, LANES), jnp.float32)
    for tile in range(tiles):
        entry = received[member, pl.ds(own + tile % 8, 1), pl.ds(tile // 8 * LANES, LANES)]
        inside = (row >= tile * tile_rows) & (row < (tile + 1) * tile_rows)
        weight = jnp.where(inside, jnp.broadcast_to(entry[:, 0:1], (rows, LANES)), weight)
    return weight


def update(blurred_of, weights_of, data_refs, model, norm, wc_high, wc_low, z_high, z_low, t_ref, out):
    out_rows, width = out.shape
    members = z_high.shape[1] // (4 * WINDOW)
    rows = out_rows + TAPS
    above = (len(data_refs) // 2) * out_rows - TAPS // 2
    for member in range(members):
        weight = weights_of(member)
        parts = []
        for slab, blurred in enumerate(blurred_of(member)):
            pieces = [ref[member, pl.ds(0, out_rows), pl.ds(LANES * slab, LANES)] for ref in data_refs]
            counts = jnp.concatenate(pieces, axis=0)[above : above + rows]
            safe = jnp.where(weight > 0.0, blurred, 1.0)
            parts.append(weight * counts / safe)
        put_field(member, parts, z_high, z_low, out_rows + 8)
    t_ref[...] = dot_split(z_high[...], z_low[...], wc_high[...], wc_low[...])
    out[...] = model[...] * gather_taps(t_ref, out_rows) / norm[...]


def first_kernel(weights_at, hops, first_row, received, *refs):
    model_refs, refs = refs[: 2 * hops + 1], refs[2 * hops + 1 :]
    wb_high, wb_low, wc_high, wc_low, blurred, norm = refs[:6]
    wide, x_high, x_low, g_ref, z_high, t_ref = refs[6:]
    members, rows, width = blurred.shape
    own = received.shape[1] - 8
    lane = lane_of((8, LANES)) % WINDOW
    used = (lane >= 1) & (lane < TAPS)
    for member in range(members):
        for group in range(2):
            entry = received[member, pl.ds(own, 8), pl.ds(LANES * group, LANES)]
            straight = jnp.where(used, entry, 0.0)
            flipped = jnp.where(used, pltpu.roll(entry, LANES - TAPS, 1), 0.0)
            for s in range(8):
                band = jnp.broadcast_to(flipped[s : s + 1], (BLOCK, LANES))
                high, low = split(pltpu.roll(band, 0, 1, stride=1, stride_axis=0))
                at = (pl.ds(BLOCK * member, BLOCK), pl.ds(LANES * (8 * group + s), LANES))
                wb_high[at] = high
                wb_low[at] = low
                band = jnp.broadcast_to(straight[s : s + 1], (BLOCK, LANES))
                high, low = split(pltpu.roll(band, 0, 1, stride=1, stride_axis=0))
                at = (pl.ds(BLOCK * s, BLOCK), pl.ds((2 * member + group) * LANES, LANES))
                wc_high[at] = high
                wc_low[at] = low
    blur_all(model_refs, wb_high, wb_low, wide, x_high, x_low, g_ref)
    for member in range(members):
        for slab, part in enumerate(blurred_parts(g_ref, member, rows, width // LANES)):
            blurred[member, :, pl.ds(LANES * slab, LANES)] = part
    out_rows = norm.shape[0]
    for member in range(members):
        weight = weights_at(member, first_row=first_row, received=received)
        put_field(member, [weight] * (width // LANES), z_high, None, out_rows + 8)
    t_ref[...] = dot_t(z_high[...], wc_high[...]) + dot_t(z_high[...], wc_low[...])
    norm[...] = gather_taps(t_ref, out_rows)


def second_kernel(weights_at, data_hops, first_row, wc_high, wc_low, blurred, model, norm, *refs):
    data_refs, refs = refs[: 2 * data_hops + 1], refs[2 * data_hops + 1 :]
    out, z_high, z_low, t_ref = refs
    width = out.shape[1]

    def blurred_of(member):
        return [blurred[member, :, pl.ds(at, LANES)] for at in range(0, width, LANES)]

    weights_of = functools.partial(weights_at, first_row=first_row, received=data_refs[data_hops])
    update(blurred_of, weights_of, data_refs, model, norm, wc_high, wc_low, z_high, z_low, t_ref, out)


def third_kernel(weights_at, data_hops, hops, first_row, wb_high, wb_low, wc_high, wc_low, norm, *refs):
    data_refs, refs = refs[: 2 * data_hops + 1], refs[2 * data_hops + 1 :]
    model_refs, refs = refs[: 2 * hops + 1], refs[2 * hops + 1 :]
    out, wide, x_high, x_low, g_ref, z_high, z_low, t_ref = refs
    out_rows, width = out.shape
    blur_all(model_refs, wb_high, wb_low, wide, x_high, x_low, g_ref)
    blurred_of = functools.partial(blurred_parts, g_ref, rows=out_rows + TAPS, slabs=width // LANES)
    weights_of = functools.partial(weights_at, first_row=first_row, received=data_refs[data_hops])
    update(blurred_of, weights_of, data_refs, model_refs[hops], norm, wc_high, wc_low, z_high, z_low, t_ref, out)


def call(kernel, out_shape, scratch_shapes, flops, *operands):
    whole = pl.BlockSpec(memory_space=pltpu.VMEM)
    scalars = pl.BlockSpec(memory_space=pltpu.SMEM)
    return pl.pallas_call(
        kernel,
        out_shape=out_shape,
        in_specs=[scalars if jnp.issubdtype(o.dtype, jnp.integer) else whole for o in operands],
        out_specs=jax.tree.map(lambda _: whole, out_shape),
        scratch_shapes=scratch_shapes,
        compiler_params=pltpu.CompilerParams(vmem_limit_bytes=VMEM_BYTES),
        cost_estimate=pl.CostEstimate(flops=flops, bytes_accessed=4 * 1024 * 1024, transcendentals=0),
    )(*operands)


def neighbours(shard, hops):
    tiles, members = lax.axis_size("tile"), lax.axis_size("visit")
    place = [i % members * tiles + i // members for i in range(tiles * members)]
    before, after = [], []
    for hop in range(1, hops + 1):
        up = list(zip(place[:-hop], place[hop:]))
        before.insert(0, lax.ppermute(shard, ("visit", "tile"), up))
        after.append(lax.ppermute(shard, ("visit", "tile"), [(j, i) for i, j in up]))
    return before + [shard] + after


def body(exposures, sky_model, blur_kernels, coverage):
    tile_rows, width = exposures.shape[1:]
    shard_rows = sky_model.shape[0]
    members = lax.axis_size("visit")
    tiles = lax.axis_size("tile")
    halo = TAPS // 2
    hops = -(-TAPS // shard_rows)
    data_hops = -(-halo // shard_rows)
    rows = shard_rows + 2 * halo
    first_row = lax.axis_index("tile") * tile_rows + lax.axis_index("visit") * shard_rows
    first_row = first_row.reshape(1, 1)

    f32, bf16 = jnp.float32, jnp.bfloat16
    shape = jax.ShapeDtypeStruct
    blocks = width // BLOCK
    depth = TAPS * WINDOW
    sum_rows = shard_rows + 8
    out_shard = shape((shard_rows, width), f32)

    sent = call(
        send_kernel,
        shape((members, shard_rows + 8, width), f32),
        [pltpu.VMEM((TAPS, LANES), f32)],
        1 << 22,
        *(coverage, exposures, blur_kernels),
    )
    sent, near = lax.optimization_barrier((sent, neighbours(sky_model, hops)))
    received = lax.all_to_all(sent, "visit", 0, 0)
    data = neighbours(received[:, :shard_rows], data_hops)
    data[data_hops] = received

    blur_scratch = [
        pltpu.VMEM((shard_rows + 2 * TAPS + 16, width), f32),
        pltpu.VMEM((blocks * rows, depth), bf16),
        pltpu.VMEM((blocks * rows, depth), bf16),
        pltpu.VMEM((blocks * rows, members * BLOCK), f32),
    ]
    field = pltpu.VMEM((blocks * sum_rows, members * 4 * WINDOW), bf16)
    product = pltpu.VMEM((blocks * sum_rows, 8 * BLOCK), f32)
    blur_flops = 6 * blocks * rows * depth * members * BLOCK
    sum_flops = 6 * blocks * sum_rows * members * 4 * WINDOW * 8 * BLOCK
    weights_at = functools.partial(weight_of, tile_rows=tile_rows, tiles=tiles, rows=rows)
    wb_high, wb_low, wc_high, wc_low, blurred, norm = call(
        functools.partial(first_kernel, weights_at, hops),
        (
            shape((members * BLOCK, depth), bf16),
            shape((members * BLOCK, depth), bf16),
            shape((8 * BLOCK, members * 4 * WINDOW), bf16),
            shape((8 * BLOCK, members * 4 * WINDOW), bf16),
            shape((members, rows, width), f32),
            out_shard,
        ),
        blur_scratch + [field, product],
        blur_flops + sum_flops,
        first_row,
        received,
        *near,
    )
    model = call(
        functools.partial(second_kernel, weights_at, data_hops),
        out_shard,
        [field, field, product],
        sum_flops,
        *(first_row, wc_high, wc_low, blurred, sky_model, norm),
        *data,
    )
    for _ in range(ITERS - 1):
        model = call(
            functools.partial(third_kernel, weights_at, data_hops, hops),
            out_shard,
            blur_scratch + [field, field, product],
            blur_flops + sum_flops,
            *(first_row, wb_high, wb_low, wc_high, wc_low, norm),
            *data,
            *neighbours(model, hops),
        )
    return model


def solution(mesh):
    return jax.shard_map(
        body,
        mesh=mesh,
        in_specs=(
            P("visit", "tile", None),
            P(("tile", "visit"), None),
            P("visit", None, None),
            P("visit", None),
        ),
        out_specs=P(("tile", "visit"), None),
        check_vma=False,
    )
```

```python
import functools

import jax
import jax.numpy as jnp
from jax import lax
from jax.experimental import pallas as pl
from jax.experimental.pallas import tpu as pltpu
from jax.sharding import PartitionSpec as P

LANES = 128
BLOCK = 32
WINDOW = 64
TAPS = 32
MARGIN = WINDOW // 4
VMEM_BYTES = 20 * 1024 * 1024


def split(x):
    high = x.astype(jnp.bfloat16)
    low = (x - high.astype(jnp.float32)).astype(jnp.bfloat16)
    return high, low


def dot_t(x, w):
    return lax.dot_general(x, w, (((1,), (1,)), ((), ())), preferred_element_type=jnp.float32)


def dot_split(x_high, x_low, w_high, w_low):
    return dot_t(x_high, w_high) + (dot_t(x_low, w_high) + dot_t(x_high, w_low))


def lane_of(shape):
    return lax.broadcasted_iota(jnp.int32, shape, len(shape) - 1)


def column_windows(parts):
    rows = parts[0].shape[0] - 8
    lane = lane_of((rows, LANES))
    shifts = sorted({(MARGIN - BLOCK * j) % LANES for j in range(LANES // BLOCK)})
    rolled = [{shift: pltpu.roll(part, shift, 1) for shift in shifts} for part in parts]
    windows = []
    for j in range(len(parts) * LANES // BLOCK):
        start = BLOCK * j - MARGIN
        first = start // LANES
        cut = (first + 1) * LANES - start

        def piece(slab):
            if slab < 0 or slab >= len(parts):
                return jnp.zeros((rows, LANES), jnp.float32)
            near = rolled[slab][(-start) % LANES][:rows]
            far = rolled[slab][(WINDOW - start) % LANES][8:]
            return jnp.where(lane < WINDOW, near, far)

        window = piece(first)
        if cut < WINDOW:
            window = jnp.where(lane % WINDOW < cut, window, piece(first + 1))
        windows.append(window)
    return windows


def put_field(member, parts, z_high, z_low, sum_rows):
    windows = column_windows(parts)
    for pair in range(len(windows) // 2):
        for group in range(2):
            rows = [window[16 * group : 16 * group + sum_rows] for window in windows[2 * pair : 2 * pair + 2]]
            high, low = split(jnp.concatenate(rows, axis=0))
            at = (pl.ds(2 * pair * sum_rows, 2 * sum_rows), pl.ds((2 * member + group) * LANES, LANES))
            z_high[at] = high
            if z_low is not None:
                z_low[at] = low


def gather_taps(t_ref, out_rows):
    sum_rows = out_rows + 8
    lane = lane_of((out_rows, LANES))
    halves = []
    for half in range(t_ref.shape[0] // sum_rows // 4):
        total = None
        for i in range(4):
            picked = None
            for jj in range(4):
                base = (4 * half + jj) * sum_rows + i
                near = t_ref[pl.ds(base, out_rows), pl.ds(0, LANES)]
                far = t_ref[pl.ds(base + 4, out_rows), pl.ds(LANES, LANES)]
                moved = pltpu.roll(near + far, (BLOCK * (jj - i)) % LANES, 1) if jj != i else near + far
                picked = moved if picked is None else jnp.where(lane >= BLOCK * jj, moved, picked)
            total = picked if total is None else total + picked
        halves.append(total)
    return jnp.concatenate(halves, axis=1)


def blur_all(wb_high, wb_low, wide, x_high, x_low, g_ref):
    slabs = wide.shape[1] // LANES
    blocks = wide.shape[1] // BLOCK
    rows = x_high.shape[0] // blocks
    for s in range(8):
        parts = [wide[pl.ds(s, rows + 24), pl.ds(LANES * i, LANES)] for i in range(slabs)]
        windows = column_windows(parts)
        for j in range(blocks):
            high, low = split(windows[j])
            for group in range(2):
                at = (pl.ds(rows * j, rows), pl.ds((8 * group + s) * LANES, LANES))
                x_high[at] = high[16 * group : 16 * group + rows]
                x_low[at] = low[16 * group : 16 * group + rows]
    step = min(2 * LANES, wb_high.shape[0])
    for at in range(0, wb_high.shape[0], step):
        g_ref[:, pl.ds(at, step)] = dot_split(
            x_high[...], x_low[...], wb_high[pl.ds(at, step), :], wb_low[pl.ds(at, step), :]
        )


def blurred_parts(g_ref, member, rows, slabs):
    lane = lane_of((rows, LANES))
    place = member % 4
    parts = []
    for slab in range(slabs):
        picked = None
        for jj in range(4):
            block = g_ref[pl.ds((4 * slab + jj) * rows, rows), pl.ds(member // 4 * LANES, LANES)]
            moved = pltpu.roll(block, (BLOCK * (jj - place)) % LANES, 1) if jj != place else block
            picked = moved if picked is None else jnp.where(lane >= BLOCK * jj, moved, picked)
        parts.append(picked)
    return parts


def table_of(kernel, cover, padded):
    size = kernel.shape[0]
    front = TAPS - size
    padded[...] = jnp.zeros(padded.shape, jnp.float32)
    padded[pl.ds(front, size), pl.ds(front, size)] = kernel / jnp.sum(kernel)
    straight = padded[...]
    row = lax.broadcasted_iota(jnp.int32, (TAPS, TAPS), 0)
    turn_rows = (row + lane_of((TAPS, TAPS)) == TAPS).astype(jnp.float32)
    row = lax.broadcasted_iota(jnp.int32, (LANES, LANES), 0)
    turn_lanes = (row + lane_of((LANES, LANES)) == TAPS).astype(jnp.float32)
    exact = functools.partial(jnp.dot, precision=lax.Precision.HIGHEST, preferred_element_type=jnp.float32)
    flipped = exact(exact(turn_rows, straight), turn_lanes)
    both = straight + pltpu.roll(flipped, TAPS, 1)
    half = [both[8 * i : 8 * i + 8] for i in range(4)]
    groups = [half[2 * i] + pltpu.roll(half[2 * i + 1], WINDOW, 1) for i in range(2)]
    row = lax.broadcasted_iota(jnp.int32, groups[0].shape, 0)
    lane = lane_of(groups[0].shape)
    for tile in range(cover.shape[1]):
        spot = (row == tile % 8) & (lane == 0)
        entry = jnp.broadcast_to(cover[0:1, tile : tile + 1].astype(jnp.float32), spot.shape)
        groups[tile // 8] = jnp.where(spot, entry, groups[tile // 8])
    return groups


def send_kernel(cover, counts, kernels, out, padded):
    groups = table_of(kernels[0], cover, padded)
    own = out.shape[1] - 8
    for peer in range(out.shape[0]):
        out[peer, pl.ds(0, own), :] = counts[0, pl.ds(peer * own, own), :]
        for group in range(2):
            out[peer, pl.ds(own, 8), pl.ds(LANES * group, LANES)] = groups[group]


def weight_of(member, first_row, tile_rows, tiles, received, rows):
    own = received.shape[1] - 8
    row = first_row - TAPS // 2 + lax.broadcasted_iota(jnp.int32, (rows, LANES), 0)
    weight = jnp.zeros((rows, LANES), jnp.float32)
    for tile in range(tiles):
        entry = received[member, pl.ds(own + tile % 8, 1), pl.ds(tile // 8 * LANES, LANES)]
        inside = (row >= tile * tile_rows) & (row < (tile + 1) * tile_rows)
        weight = jnp.where(inside, jnp.broadcast_to(entry[:, 0:1], (rows, LANES)), weight)
    return weight


def update(blurred_of, weight_at, counts_of, model, norm, wc_high, wc_low, z_high, z_low, t_ref, out):
    out_rows = out.shape[0]
    for member in range(z_high.shape[1] // (4 * WINDOW)):
        weight = weight_at(member)
        parts = []
        for blurred, counts in zip(blurred_of(member), counts_of(member)):
            safe = jnp.where(weight > 0.0, blurred, 1.0)
            parts.append(weight * counts / safe)
        put_field(member, parts, z_high, z_low, out_rows + 8)
    t_ref[...] = dot_split(z_high[...], z_low[...], wc_high[...], wc_low[...])
    out[...] = model * gather_taps(t_ref, out_rows) / norm


def put_model(model_refs, wide):
    at = 0
    for ref in model_refs:
        wide[pl.ds(at, ref.shape[0]), :] = ref[...]
        at += ref.shape[0]


def first_kernel(
    weight_at, at, received, before, own, after, wb_high, wb_low, wc_high, wc_low, blurred, norm, wide, x_high, x_low, g_ref, z_high, t_ref
):
    members, rows, width = blurred.shape
    table_row = received.shape[1] - 8
    lane = lane_of((8, LANES)) % WINDOW
    used = (lane >= 1) & (lane < TAPS)
    for member in range(members):
        for group in range(2):
            entry = received[member, pl.ds(table_row, 8), pl.ds(LANES * group, LANES)]
            straight = jnp.where(used, entry, 0.0)
            flipped = jnp.where(used, pltpu.roll(entry, LANES - TAPS, 1), 0.0)
            for s in range(8):
                band = jnp.broadcast_to(flipped[s : s + 1], (BLOCK, LANES))
                high, low = split(pltpu.roll(band, 0, 1, stride=1, stride_axis=0))
                spot = (pl.ds(BLOCK * member, BLOCK), pl.ds(LANES * (8 * group + s), LANES))
                wb_high[spot] = high
                wb_low[spot] = low
                band = jnp.broadcast_to(straight[s : s + 1], (BLOCK, LANES))
                high, low = split(pltpu.roll(band, 0, 1, stride=1, stride_axis=0))
                spot = (pl.ds(BLOCK * s, BLOCK), pl.ds((2 * member + group) * LANES, LANES))
                wc_high[spot] = high
                wc_low[spot] = low
    put_model((before, own, after), wide)
    blur_all(wb_high, wb_low, wide, x_high, x_low, g_ref)
    for member in range(members):
        for slab, part in enumerate(blurred_parts(g_ref, member, rows, width // LANES)):
            blurred[member, :, pl.ds(LANES * slab, LANES)] = part
    out_rows = norm.shape[0]
    for member in range(members):
        weight = weight_at(member, at[0, 0], received=received, rows=rows)
        put_field(member, [weight] * (width // LANES), z_high, None, out_rows + 8)
    t_ref[...] = dot_t(z_high[...], wc_high[...]) + dot_t(z_high[...], wc_low[...])
    norm[...] = gather_taps(t_ref, out_rows)


def second_kernel(weight_at, group, at, wc_high, wc_low, received, blurred, model, norm, *refs):
    pair_refs, (out, data, z_high, z_low, t_ref, window) = refs[:group], refs[group:]
    members, shard_rows = pair_refs[0].shape[1:3]
    out_rows, width = out.shape
    place = at[0, 1]
    slabs = [pl.ds(first, LANES) for first in range(0, width, LANES)]

    def blurred_of(member):
        return [blurred[member, :, slab] for slab in slabs]

    def counts_of(member):
        parts = []
        for slab in slabs:
            own, edge = ([ref[i, member, :, slab] for ref in pair_refs] for i in range(2))
            own, edge = group_order(own, place), group_order(edge, place)
            parts.append(jnp.concatenate(edge[group // 2 :] + own + edge[: group // 2], axis=0))
            window[:, slab] = parts[-1]
        data[member] = window[pl.ds(pl.multiple_of(place * shard_rows, shard_rows), data.shape[1]), :]
        return parts

    weight_of_group = functools.partial(weight_at, first_row=at[0, 0], received=received, rows=out_rows + TAPS)
    update(blurred_of, weight_of_group, counts_of, model[...], norm[...], wc_high, wc_low, z_high, z_low, t_ref, out)


def third_kernel(
    weight_at, at, wb_high, wb_low, wc_high, wc_low, received, norm, data, before, own, after, out, tall, wide, x_high, x_low, g_ref, z_high, z_low, t_ref
):
    out_rows, width = out.shape
    rows = out_rows + TAPS
    first = pl.multiple_of(at[0, 1] * out_rows, out_rows)
    put_model((before, own, after), tall)
    wide[...] = tall[pl.ds(first, wide.shape[0]), :]
    blur_all(wb_high, wb_low, wide, x_high, x_low, g_ref)
    blurred_of = functools.partial(blurred_parts, g_ref, rows=rows, slabs=width // LANES)

    def counts_of(member):
        return [data[member, :, pl.ds(slab, LANES)] for slab in range(0, width, LANES)]

    weight_of_shard = functools.partial(weight_at, first_row=at[0, 0] + first, received=received, rows=rows)
    model, scale = own[pl.ds(first, out_rows), :], norm[pl.ds(first, out_rows), :]
    update(blurred_of, weight_of_shard, counts_of, model, scale, wc_high, wc_low, z_high, z_low, t_ref, out)


def call(kernel, out_shape, scratch_shapes, flops, *operands, scalars=0):
    whole = pl.BlockSpec(memory_space=pltpu.VMEM)
    scalar = pl.BlockSpec(memory_space=pltpu.SMEM)
    return pl.pallas_call(
        kernel,
        out_shape=out_shape,
        in_specs=[scalar] * scalars + [whole] * (len(operands) - scalars),
        out_specs=jax.tree.map(lambda _: whole, out_shape),
        scratch_shapes=scratch_shapes,
        compiler_params=pltpu.CompilerParams(vmem_limit_bytes=VMEM_BYTES),
        cost_estimate=pl.CostEstimate(flops=flops, bytes_accessed=4 * 1024 * 1024, transcendentals=0),
    )(*operands)


def strip_permute(array, target):
    tiles, members = lax.axis_size("tile"), lax.axis_size("visit")
    count = tiles * members
    place = [i % members * tiles + i // members for i in range(count)]
    pairs = [(place[i], place[target(i)]) for i in range(count) if 0 <= target(i) < count]
    return lax.ppermute(array, ("visit", "tile"), pairs)


def group_gather(array, group):
    return [array] + [strip_permute(array, lambda i: i // group * group + (i + k) % group) for k in range(1, group)]


def group_order(arrays, place):
    ordered = []
    for slot in range(len(arrays)):
        back = (place - slot) % len(arrays)
        picked = arrays[0]
        for k in range(1, len(arrays)):
            picked = jnp.where(back == k, arrays[k], picked)
        ordered.append(picked)
    return ordered


def group_neighbours(rows, group):
    return [strip_permute(rows, lambda i: i + group), rows, strip_permute(rows, lambda i: i - group)]


def body(exposures, sky_model, blur_kernels, coverage):
    tile_rows, width = exposures.shape[1:]
    shard_rows = sky_model.shape[0]
    members = lax.axis_size("visit")
    tiles = lax.axis_size("tile")
    group = TAPS // shard_rows
    place = lax.axis_index("visit") % group
    group_row = lax.axis_index("tile") * tile_rows + (lax.axis_index("visit") - place) * shard_rows
    at = jnp.stack([group_row, place]).reshape(1, 2)

    f32, bf16 = jnp.float32, jnp.bfloat16
    shape = jax.ShapeDtypeStruct
    blocks = width // BLOCK
    depth = TAPS * WINDOW

    sent = call(
        send_kernel,
        shape((members, shard_rows + 8, width), f32),
        [pltpu.VMEM((TAPS, LANES), f32)],
        1 << 22,
        *(coverage, exposures, blur_kernels),
    )
    received = lax.all_to_all(sent, "visit", 0, 0)
    mine = jnp.concatenate(group_order(group_gather(sky_model, group), place), axis=0)
    near = group_neighbours(mine, group)
    own = received[:, :shard_rows]
    edge = strip_permute(own, lambda i: i + group if 2 * (i % group) >= group else i - group)

    def blur_scratch(out_rows):
        rows = out_rows + TAPS
        return [
            pltpu.VMEM((rows + TAPS, width), f32),
            pltpu.VMEM((blocks * rows, depth), bf16),
            pltpu.VMEM((blocks * rows, depth), bf16),
            pltpu.VMEM((blocks * rows, members * BLOCK), f32),
        ]

    def field(out_rows):
        return pltpu.VMEM((blocks * (out_rows + 8), members * 4 * WINDOW), bf16)

    def product(out_rows):
        return pltpu.VMEM((blocks * (out_rows + 8), 8 * BLOCK), f32)

    blur_flops = 6 * blocks * (TAPS + shard_rows) * depth * members * BLOCK
    sum_flops = 6 * blocks * (shard_rows + 8) * members * 4 * WINDOW * 8 * BLOCK
    weight_at = functools.partial(weight_of, tile_rows=tile_rows, tiles=tiles)
    wb_high, wb_low, wc_high, wc_low, blurred, norm = call(
        functools.partial(first_kernel, weight_at),
        (
            shape((members * BLOCK, depth), bf16),
            shape((members * BLOCK, depth), bf16),
            shape((8 * BLOCK, members * 4 * WINDOW), bf16),
            shape((8 * BLOCK, members * 4 * WINDOW), bf16),
            shape((members, 2 * TAPS, width), f32),
            shape((TAPS, width), f32),
        ),
        blur_scratch(TAPS) + [field(TAPS), product(TAPS)],
        blur_flops + sum_flops,
        *(at, received, *near),
        scalars=1,
    )
    pairs = group_gather(jnp.stack([own, edge]), group)
    model, data = call(
        functools.partial(second_kernel, weight_at, group),
        (shape((TAPS, width), f32), shape((members, shard_rows + TAPS, width), f32)),
        [field(TAPS), field(TAPS), product(TAPS), pltpu.VMEM((2 * TAPS, width), f32)],
        sum_flops,
        *(at, wc_high, wc_low, received, blurred, mine, norm, *pairs),
        scalars=1,
    )
    return call(
        functools.partial(third_kernel, weight_at),
        shape((shard_rows, width), f32),
        [pltpu.VMEM((3 * TAPS, width), f32)]
        + blur_scratch(shard_rows)
        + [field(shard_rows), field(shard_rows), product(shard_rows)],
        blur_flops + sum_flops,
        *(at, wb_high, wb_low, wc_high, wc_low, received, norm, data, *group_neighbours(model, group)),
        scalars=1,
    )


def solution(mesh):
    return jax.shard_map(
        body,
        mesh=mesh,
        in_specs=(
            P("visit", "tile", None),
            P(("tile", "visit"), None),
            P("visit", None, None),
            P("visit", None),
        ),
        out_specs=P(("tile", "visit"), None),
        check_vma=False,
    )
```

```python
import functools

import jax
import jax.numpy as jnp
from jax import lax
from jax.experimental import pallas as pl
from jax.experimental.pallas import tpu as pltpu
from jax.sharding import PartitionSpec as P

LANES = 128
BLOCK = 32
WINDOW = 64
TAPS = 32
MARGIN = WINDOW // 4
VMEM_BYTES = 20 * 1024 * 1024


def split(x):
    high = x.astype(jnp.bfloat16)
    low = (x - high.astype(jnp.float32)).astype(jnp.bfloat16)
    return high, low


def dot_t(x, w):
    return lax.dot_general(x, w, (((1,), (1,)), ((), ())), preferred_element_type=jnp.float32)


def dot_split(x_high, x_low, w_high, w_low):
    return dot_t(x_high, w_high) + (dot_t(x_low, w_high) + dot_t(x_high, w_low))


def lane_of(shape):
    return lax.broadcasted_iota(jnp.int32, shape, len(shape) - 1)


def column_windows(parts):
    rows = parts[0].shape[0] - 8
    lane = lane_of((rows, LANES))
    shifts = sorted({(MARGIN - BLOCK * j) % LANES for j in range(LANES // BLOCK)})
    rolled = [{shift: pltpu.roll(part, shift, 1) for shift in shifts} for part in parts]
    windows = []
    for j in range(len(parts) * LANES // BLOCK):
        start = BLOCK * j - MARGIN
        first = start // LANES
        cut = (first + 1) * LANES - start

        def piece(slab):
            if slab < 0 or slab >= len(parts):
                return jnp.zeros((rows, LANES), jnp.float32)
            near = rolled[slab][(-start) % LANES][:rows]
            far = rolled[slab][(WINDOW - start) % LANES][8:]
            return jnp.where(lane < WINDOW, near, far)

        window = piece(first)
        if cut < WINDOW:
            window = jnp.where(lane % WINDOW < cut, window, piece(first + 1))
        windows.append(window)
    return windows


def put_field(member, parts, z_high, z_low, sum_rows):
    windows = column_windows(parts)
    for pair in range(len(windows) // 2):
        for group in range(2):
            rows = [window[16 * group : 16 * group + sum_rows] for window in windows[2 * pair : 2 * pair + 2]]
            high, low = split(jnp.concatenate(rows, axis=0))
            at = (pl.ds(2 * pair * sum_rows, 2 * sum_rows), pl.ds((2 * member + group) * LANES, LANES))
            z_high[at] = high
            if z_low is not None:
                z_low[at] = low


def gather_taps(t_ref, out_rows):
    sum_rows = out_rows + 8
    lane = lane_of((out_rows, LANES))
    halves = []
    for half in range(t_ref.shape[0] // sum_rows // 4):
        total = None
        for i in range(4):
            picked = None
            for jj in range(4):
                base = (4 * half + jj) * sum_rows + i
                near = t_ref[pl.ds(base, out_rows), pl.ds(0, LANES)]
                far = t_ref[pl.ds(base + 4, out_rows), pl.ds(LANES, LANES)]
                moved = pltpu.roll(near + far, (BLOCK * (jj - i)) % LANES, 1) if jj != i else near + far
                picked = moved if picked is None else jnp.where(lane >= BLOCK * jj, moved, picked)
            total = picked if total is None else total + picked
        halves.append(total)
    return jnp.concatenate(halves, axis=1)


def blur_all(wb_high, wb_low, wide, x_high, x_low, g_ref):
    slabs = wide.shape[1] // LANES
    blocks = wide.shape[1] // BLOCK
    rows = x_high.shape[0] // blocks
    for s in range(8):
        parts = [wide[pl.ds(s, rows + 24), pl.ds(LANES * i, LANES)] for i in range(slabs)]
        windows = column_windows(parts)
        for j in range(blocks):
            high, low = split(windows[j])
            for group in range(2):
                at = (pl.ds(rows * j, rows), pl.ds((8 * group + s) * LANES, LANES))
                x_high[at] = high[16 * group : 16 * group + rows]
                x_low[at] = low[16 * group : 16 * group + rows]
    step = min(2 * LANES, wb_high.shape[0])
    for at in range(0, wb_high.shape[0], step):
        g_ref[:, pl.ds(at, step)] = dot_split(
            x_high[...], x_low[...], wb_high[pl.ds(at, step), :], wb_low[pl.ds(at, step), :]
        )


def blurred_parts(g_ref, member, rows, slabs):
    lane = lane_of((rows, LANES))
    place = member % 4
    parts = []
    for slab in range(slabs):
        picked = None
        for jj in range(4):
            block = g_ref[pl.ds((4 * slab + jj) * rows, rows), pl.ds(member // 4 * LANES, LANES)]
            moved = pltpu.roll(block, (BLOCK * (jj - place)) % LANES, 1) if jj != place else block
            picked = moved if picked is None else jnp.where(lane >= BLOCK * jj, moved, picked)
        parts.append(picked)
    return parts


def table_of(kernel, cover, padded):
    size = kernel.shape[0]
    front = TAPS - size
    padded[...] = jnp.zeros(padded.shape, jnp.float32)
    padded[pl.ds(front, size), pl.ds(front, size)] = kernel / jnp.sum(kernel)
    straight = padded[...]
    row = lax.broadcasted_iota(jnp.int32, (TAPS, TAPS), 0)
    turn_rows = (row + lane_of((TAPS, TAPS)) == TAPS).astype(jnp.float32)
    row = lax.broadcasted_iota(jnp.int32, (LANES, LANES), 0)
    turn_lanes = (row + lane_of((LANES, LANES)) == TAPS).astype(jnp.float32)
    exact = functools.partial(jnp.dot, precision=lax.Precision.HIGHEST, preferred_element_type=jnp.float32)
    flipped = exact(exact(turn_rows, straight), turn_lanes)
    both = straight + pltpu.roll(flipped, TAPS, 1)
    half = [both[8 * i : 8 * i + 8] for i in range(4)]
    groups = [half[2 * i] + pltpu.roll(half[2 * i + 1], WINDOW, 1) for i in range(2)]
    row = lax.broadcasted_iota(jnp.int32, groups[0].shape, 0)
    lane = lane_of(groups[0].shape)
    for tile in range(cover.shape[1]):
        spot = (row == tile % 8) & (lane == 0)
        entry = jnp.broadcast_to(cover[0:1, tile : tile + 1].astype(jnp.float32), spot.shape)
        groups[tile // 8] = jnp.where(spot, entry, groups[tile // 8])
    return groups


def send_kernel(cover, counts, kernels, out, padded):
    groups = table_of(kernels[0], cover, padded)
    own = out.shape[1] - 8
    for peer in range(out.shape[0]):
        out[peer, pl.ds(0, own), :] = counts[0, pl.ds(peer * own, own), :]
        for group in range(2):
            out[peer, pl.ds(own, 8), pl.ds(LANES * group, LANES)] = groups[group]


def weight_of(member, first_row, tile_rows, tiles, received, rows):
    own = received.shape[1] - 8
    row = first_row - TAPS // 2 + lax.broadcasted_iota(jnp.int32, (rows, LANES), 0)
    weight = jnp.zeros((rows, LANES), jnp.float32)
    for tile in range(tiles):
        entry = received[member, pl.ds(own + tile % 8, 1), pl.ds(tile // 8 * LANES, LANES)]
        inside = (row >= tile * tile_rows) & (row < (tile + 1) * tile_rows)
        weight = jnp.where(inside, jnp.broadcast_to(entry[:, 0:1], (rows, LANES)), weight)
    return weight


def update(blurred_of, weight_at, counts_of, model, norm, wc_high, wc_low, z_high, z_low, t_ref, out):
    out_rows = out.shape[0]
    for member in range(z_high.shape[1] // (4 * WINDOW)):
        weight = weight_at(member)
        parts = []
        for blurred, counts in zip(blurred_of(member), counts_of(member)):
            safe = jnp.where(weight > 0.0, blurred, 1.0)
            parts.append(weight * counts / safe)
        put_field(member, parts, z_high, z_low, out_rows + 8)
    t_ref[...] = dot_split(z_high[...], z_low[...], wc_high[...], wc_low[...])
    out[...] = model * gather_taps(t_ref, out_rows) / norm


def put_model(model_refs, wide):
    at = 0
    for ref in model_refs:
        wide[pl.ds(at, ref.shape[0]), :] = ref[...]
        at += ref.shape[0]


def build_kernel(weight_at, at, received, wb_high, wb_low, wc_high, wc_low, norm, z_high, t_ref):
    members = received.shape[0]
    out_rows, width = norm.shape
    table_row = received.shape[1] - 8
    lane = lane_of((8, LANES)) % WINDOW
    used = (lane >= 1) & (lane < TAPS)
    for member in range(members):
        for group in range(2):
            entry = received[member, pl.ds(table_row, 8), pl.ds(LANES * group, LANES)]
            straight = jnp.where(used, entry, 0.0)
            flipped = jnp.where(used, pltpu.roll(entry, LANES - TAPS, 1), 0.0)
            for s in range(8):
                band = jnp.broadcast_to(flipped[s : s + 1], (BLOCK, LANES))
                high, low = split(pltpu.roll(band, 0, 1, stride=1, stride_axis=0))
                spot = (pl.ds(BLOCK * member, BLOCK), pl.ds(LANES * (8 * group + s), LANES))
                wb_high[spot] = high
                wb_low[spot] = low
                band = jnp.broadcast_to(straight[s : s + 1], (BLOCK, LANES))
                high, low = split(pltpu.roll(band, 0, 1, stride=1, stride_axis=0))
                spot = (pl.ds(BLOCK * s, BLOCK), pl.ds((2 * member + group) * LANES, LANES))
                wc_high[spot] = high
                wc_low[spot] = low
    for member in range(members):
        weight = weight_at(member, at[0, 0], received=received, rows=out_rows + TAPS)
        put_field(member, [weight] * (width // LANES), z_high, None, out_rows + 8)
    t_ref[...] = dot_t(z_high[...], wc_high[...]) + dot_t(z_high[...], wc_low[...])
    norm[...] = gather_taps(t_ref, out_rows)


def blur_kernel(wb_high, wb_low, before, own, after, blurred, wide, x_high, x_low, g_ref):
    members, rows, width = blurred.shape
    put_model((before, own, after), wide)
    blur_all(wb_high, wb_low, wide, x_high, x_low, g_ref)
    for member in range(members):
        for slab, part in enumerate(blurred_parts(g_ref, member, rows, width // LANES)):
            blurred[member, :, pl.ds(LANES * slab, LANES)] = part


def second_kernel(weight_at, group, at, wc_high, wc_low, received, blurred, model, norm, *refs):
    pair_refs, (out, data, z_high, z_low, t_ref, window) = refs[:group], refs[group:]
    members, shard_rows = pair_refs[0].shape[1:3]
    out_rows, width = out.shape
    place = at[0, 1]
    slabs = [pl.ds(first, LANES) for first in range(0, width, LANES)]

    def blurred_of(member):
        return [blurred[member, :, slab] for slab in slabs]

    def counts_of(member):
        parts = []
        for slab in slabs:
            own, edge = ([ref[i, member, :, slab] for ref in pair_refs] for i in range(2))
            own, edge = group_order(own, place), group_order(edge, place)
            parts.append(jnp.concatenate(edge[group // 2 :] + own + edge[: group // 2], axis=0))
            window[:, slab] = parts[-1]
        data[member] = window[pl.ds(pl.multiple_of(place * shard_rows, shard_rows), data.shape[1]), :]
        return parts

    weight_of_group = functools.partial(weight_at, first_row=at[0, 0], received=received, rows=out_rows + TAPS)
    update(blurred_of, weight_of_group, counts_of, model[...], norm[...], wc_high, wc_low, z_high, z_low, t_ref, out)


def third_kernel(
    weight_at, at, wb_high, wb_low, wc_high, wc_low, received, norm, data, before, own, after, out, tall, wide, x_high, x_low, g_ref, z_high, z_low, t_ref
):
    out_rows, width = out.shape
    rows = out_rows + TAPS
    first = pl.multiple_of(at[0, 1] * out_rows, out_rows)
    put_model((before, own, after), tall)
    wide[...] = tall[pl.ds(first, wide.shape[0]), :]
    blur_all(wb_high, wb_low, wide, x_high, x_low, g_ref)
    blurred_of = functools.partial(blurred_parts, g_ref, rows=rows, slabs=width // LANES)

    def counts_of(member):
        return [data[member, :, pl.ds(slab, LANES)] for slab in range(0, width, LANES)]

    weight_of_shard = functools.partial(weight_at, first_row=at[0, 0] + first, received=received, rows=rows)
    model, scale = own[pl.ds(first, out_rows), :], norm[pl.ds(first, out_rows), :]
    update(blurred_of, weight_of_shard, counts_of, model, scale, wc_high, wc_low, z_high, z_low, t_ref, out)


def call(kernel, out_shape, scratch_shapes, flops, *operands, scalars=0):
    whole = pl.BlockSpec(memory_space=pltpu.VMEM)
    scalar = pl.BlockSpec(memory_space=pltpu.SMEM)
    return pl.pallas_call(
        kernel,
        out_shape=out_shape,
        in_specs=[scalar] * scalars + [whole] * (len(operands) - scalars),
        out_specs=jax.tree.map(lambda _: whole, out_shape),
        scratch_shapes=scratch_shapes,
        compiler_params=pltpu.CompilerParams(vmem_limit_bytes=VMEM_BYTES),
        cost_estimate=pl.CostEstimate(flops=flops, bytes_accessed=4 * 1024 * 1024, transcendentals=0),
    )(*operands)


def strip_permute(array, target):
    tiles, members = lax.axis_size("tile"), lax.axis_size("visit")
    count = tiles * members
    place = [i % members * tiles + i // members for i in range(count)]
    pairs = [(place[i], place[target(i)]) for i in range(count) if 0 <= target(i) < count]
    return lax.ppermute(array, ("visit", "tile"), pairs)


def group_gather(array, group):
    return [array] + [strip_permute(array, lambda i: i // group * group + (i + k) % group) for k in range(1, group)]


def group_order(arrays, place):
    ordered = []
    for slot in range(len(arrays)):
        back = (place - slot) % len(arrays)
        picked = arrays[0]
        for k in range(1, len(arrays)):
            picked = jnp.where(back == k, arrays[k], picked)
        ordered.append(picked)
    return ordered


def group_neighbours(rows, group):
    return [strip_permute(rows, lambda i: i + group), rows, strip_permute(rows, lambda i: i - group)]


def body(exposures, sky_model, blur_kernels, coverage):
    tile_rows, width = exposures.shape[1:]
    shard_rows = sky_model.shape[0]
    members = lax.axis_size("visit")
    tiles = lax.axis_size("tile")
    group = TAPS // shard_rows
    place = lax.axis_index("visit") % group
    group_row = lax.axis_index("tile") * tile_rows + (lax.axis_index("visit") - place) * shard_rows
    at = jnp.stack([group_row, place]).reshape(1, 2)

    f32, bf16 = jnp.float32, jnp.bfloat16
    shape = jax.ShapeDtypeStruct
    blocks = width // BLOCK
    depth = TAPS * WINDOW

    sent = call(
        send_kernel,
        shape((members, shard_rows + 8, width), f32),
        [pltpu.VMEM((TAPS, LANES), f32)],
        1 << 22,
        *(coverage, exposures, blur_kernels),
    )
    received = lax.all_to_all(sent, "visit", 0, 0)
    mine = jnp.concatenate(group_order(group_gather(sky_model, group), place), axis=0)
    near = group_neighbours(mine, group)
    received, near = lax.optimization_barrier((received, near))
    own = received[:, :shard_rows]
    edge = strip_permute(own, lambda i: i + group if 2 * (i % group) >= group else i - group)

    def blur_scratch(out_rows):
        rows = out_rows + TAPS
        return [
            pltpu.VMEM((rows + TAPS, width), f32),
            pltpu.VMEM((blocks * rows, depth), bf16),
            pltpu.VMEM((blocks * rows, depth), bf16),
            pltpu.VMEM((blocks * rows, members * BLOCK), f32),
        ]

    def field(out_rows):
        return pltpu.VMEM((blocks * (out_rows + 8), members * 4 * WINDOW), bf16)

    def product(out_rows):
        return pltpu.VMEM((blocks * (out_rows + 8), 8 * BLOCK), f32)

    blur_flops = 6 * blocks * (TAPS + shard_rows) * depth * members * BLOCK
    sum_flops = 6 * blocks * (shard_rows + 8) * members * 4 * WINDOW * 8 * BLOCK
    weight_at = functools.partial(weight_of, tile_rows=tile_rows, tiles=tiles)
    wb_high, wb_low, wc_high, wc_low, norm = call(
        functools.partial(build_kernel, weight_at),
        (
            shape((members * BLOCK, depth), bf16),
            shape((members * BLOCK, depth), bf16),
            shape((8 * BLOCK, members * 4 * WINDOW), bf16),
            shape((8 * BLOCK, members * 4 * WINDOW), bf16),
            shape((TAPS, width), f32),
        ),
        [field(TAPS), product(TAPS)],
        2 * sum_flops,
        *(at, received),
        scalars=1,
    )
    blurred = call(
        blur_kernel,
        shape((members, 2 * TAPS, width), f32),
        blur_scratch(TAPS),
        blur_flops,
        *(wb_high, wb_low, *near),
    )
    both, norm = lax.optimization_barrier((jnp.stack([own, edge]), norm))
    pairs = group_gather(both, group)
    model, data = call(
        functools.partial(second_kernel, weight_at, group),
        (shape((TAPS, width), f32), shape((members, shard_rows + TAPS, width), f32)),
        [field(TAPS), field(TAPS), product(TAPS), pltpu.VMEM((2 * TAPS, width), f32)],
        sum_flops,
        *(at, wc_high, wc_low, received, blurred, mine, norm, *pairs),
        scalars=1,
    )
    return call(
        functools.partial(third_kernel, weight_at),
        shape((shard_rows, width), f32),
        [pltpu.VMEM((3 * TAPS, width), f32)]
        + blur_scratch(shard_rows)
        + [field(shard_rows), field(shard_rows), product(shard_rows)],
        blur_flops + sum_flops,
        *(at, wb_high, wb_low, wc_high, wc_low, received, norm, data, *group_neighbours(model, group)),
        scalars=1,
    )


def solution(mesh):
    return jax.shard_map(
        body,
        mesh=mesh,
        in_specs=(
            P("visit", "tile", None),
            P(("tile", "visit"), None),
            P("visit", None, None),
            P("visit", None),
        ),
        out_specs=P(("tile", "visit"), None),
        check_vma=False,
    )
```

```python
import functools

import jax
import jax.numpy as jnp
from jax import lax
from jax.experimental import pallas as pl
from jax.experimental.pallas import tpu as pltpu
from jax.sharding import PartitionSpec as P

LANES = 128
BLOCK = 32
WINDOW = 64
TAPS = 32
MARGIN = WINDOW // 4
VMEM_BYTES = 20 * 1024 * 1024


def split(x):
    high = x.astype(jnp.bfloat16)
    low = (x - high.astype(jnp.float32)).astype(jnp.bfloat16)
    return high, low


def dot_t(x, w):
    return lax.dot_general(x, w, (((1,), (1,)), ((), ())), preferred_element_type=jnp.float32)


def dot_split(x_high, x_low, w_high, w_low):
    return dot_t(x_high, w_high) + (dot_t(x_low, w_high) + dot_t(x_high, w_low))


def lane_of(shape):
    return lax.broadcasted_iota(jnp.int32, shape, len(shape) - 1)


def column_windows(parts):
    rows = parts[0].shape[0] - 8
    lane = lane_of((rows, LANES))
    shifts = sorted({(MARGIN - BLOCK * j) % LANES for j in range(LANES // BLOCK)})
    rolled = [{shift: pltpu.roll(part, shift, 1) for shift in shifts} for part in parts]
    windows = []
    for j in range(len(parts) * LANES // BLOCK):
        start = BLOCK * j - MARGIN
        first = start // LANES
        cut = (first + 1) * LANES - start

        def piece(slab):
            if slab < 0 or slab >= len(parts):
                return jnp.zeros((rows, LANES), jnp.float32)
            near = rolled[slab][(-start) % LANES][:rows]
            far = rolled[slab][(WINDOW - start) % LANES][8:]
            return jnp.where(lane < WINDOW, near, far)

        window = piece(first)
        if cut < WINDOW:
            window = jnp.where(lane % WINDOW < cut, window, piece(first + 1))
        windows.append(window)
    return windows


def put_field(member, parts, z_high, z_low, sum_rows):
    windows = column_windows(parts)
    for pair in range(len(windows) // 2):
        for group in range(2):
            rows = [window[16 * group : 16 * group + sum_rows] for window in windows[2 * pair : 2 * pair + 2]]
            high, low = split(jnp.concatenate(rows, axis=0))
            at = (pl.ds(2 * pair * sum_rows, 2 * sum_rows), pl.ds((2 * member + group) * LANES, LANES))
            z_high[at] = high
            if z_low is not None:
                z_low[at] = low


def gather_taps(t_ref, out_rows):
    sum_rows = out_rows + 8
    lane = lane_of((out_rows, LANES))
    halves = []
    for half in range(t_ref.shape[0] // sum_rows // 4):
        total = None
        for i in range(4):
            picked = None
            for jj in range(4):
                base = (4 * half + jj) * sum_rows + i
                near = t_ref[pl.ds(base, out_rows), pl.ds(0, LANES)]
                far = t_ref[pl.ds(base + 4, out_rows), pl.ds(LANES, LANES)]
                moved = pltpu.roll(near + far, (BLOCK * (jj - i)) % LANES, 1) if jj != i else near + far
                picked = moved if picked is None else jnp.where(lane >= BLOCK * jj, moved, picked)
            total = picked if total is None else total + picked
        halves.append(total)
    return jnp.concatenate(halves, axis=1)


def blur_all(wb_high, wb_low, wide, x_high, x_low, g_ref):
    slabs = wide.shape[1] // LANES
    blocks = wide.shape[1] // BLOCK
    rows = x_high.shape[0] // blocks
    for s in range(8):
        parts = [wide[pl.ds(s, rows + 24), pl.ds(LANES * i, LANES)] for i in range(slabs)]
        windows = column_windows(parts)
        for j in range(blocks):
            high, low = split(windows[j])
            for group in range(2):
                at = (pl.ds(rows * j, rows), pl.ds((8 * group + s) * LANES, LANES))
                x_high[at] = high[16 * group : 16 * group + rows]
                x_low[at] = low[16 * group : 16 * group + rows]
    step = min(2 * LANES, wb_high.shape[0])
    for at in range(0, wb_high.shape[0], step):
        g_ref[:, pl.ds(at, step)] = dot_split(
            x_high[...], x_low[...], wb_high[pl.ds(at, step), :], wb_low[pl.ds(at, step), :]
        )


def blurred_parts(g_ref, member, rows, slabs):
    lane = lane_of((rows, LANES))
    place = member % 4
    parts = []
    for slab in range(slabs):
        picked = None
        for jj in range(4):
            block = g_ref[pl.ds((4 * slab + jj) * rows, rows), pl.ds(member // 4 * LANES, LANES)]
            moved = pltpu.roll(block, (BLOCK * (jj - place)) % LANES, 1) if jj != place else block
            picked = moved if picked is None else jnp.where(lane >= BLOCK * jj, moved, picked)
        parts.append(picked)
    return parts


def table_of(kernel, cover, padded):
    size = kernel.shape[0]
    front = TAPS - size
    padded[...] = jnp.zeros(padded.shape, jnp.float32)
    padded[pl.ds(front, size), pl.ds(front, size)] = kernel / jnp.sum(kernel)
    straight = padded[...]
    row = lax.broadcasted_iota(jnp.int32, (TAPS, TAPS), 0)
    turn_rows = (row + lane_of((TAPS, TAPS)) == TAPS).astype(jnp.float32)
    row = lax.broadcasted_iota(jnp.int32, (LANES, LANES), 0)
    turn_lanes = (row + lane_of((LANES, LANES)) == TAPS).astype(jnp.float32)
    exact = functools.partial(jnp.dot, precision=lax.Precision.HIGHEST, preferred_element_type=jnp.float32)
    flipped = exact(exact(turn_rows, straight), turn_lanes)
    both = straight + pltpu.roll(flipped, TAPS, 1)
    half = [both[8 * i : 8 * i + 8] for i in range(4)]
    groups = [half[2 * i] + pltpu.roll(half[2 * i + 1], WINDOW, 1) for i in range(2)]
    row = lax.broadcasted_iota(jnp.int32, groups[0].shape, 0)
    lane = lane_of(groups[0].shape)
    for tile in range(cover.shape[1]):
        spot = (row == tile % 8) & (lane == 0)
        entry = jnp.broadcast_to(cover[0:1, tile : tile + 1].astype(jnp.float32), spot.shape)
        groups[tile // 8] = jnp.where(spot, entry, groups[tile // 8])
    return groups


def send_kernel(group, cover, counts, above, below, kernels, out, padded):
    groups = table_of(kernels[0], cover, padded)
    peers = out.shape[0]
    own = (out.shape[1] - 8) // 2
    for peer in range(peers):
        place = peer % group
        out[peer, pl.ds(0, own), :] = counts[0, pl.ds(peer * own, own), :]
        block = peer - group if 2 * place >= group else peer + group
        if block < 0:
            edge = above[pl.ds((place - group // 2) * own, own), :]
        elif block >= peers:
            edge = below[pl.ds(place * own, own), :]
        else:
            edge = counts[0, pl.ds(block * own, own), :]
        out[peer, pl.ds(own, own), :] = edge
        for half in range(2):
            out[peer, pl.ds(2 * own, 8), pl.ds(LANES * half, LANES)] = groups[half]


def weight_of(member, first_row, tile_rows, tiles, received, rows):
    own = received.shape[1] - 8
    row = first_row - TAPS // 2 + lax.broadcasted_iota(jnp.int32, (rows, LANES), 0)
    weight = jnp.zeros((rows, LANES), jnp.float32)
    for tile in range(tiles):
        entry = received[member, pl.ds(own + tile % 8, 1), pl.ds(tile // 8 * LANES, LANES)]
        inside = (row >= tile * tile_rows) & (row < (tile + 1) * tile_rows)
        weight = jnp.where(inside, jnp.broadcast_to(entry[:, 0:1], (rows, LANES)), weight)
    return weight


def update(blurred_of, weight_at, counts_of, model, norm, wc_high, wc_low, z_high, z_low, t_ref, out):
    out_rows = out.shape[0]
    for member in range(z_high.shape[1] // (4 * WINDOW)):
        weight = weight_at(member)
        parts = []
        for blurred, counts in zip(blurred_of(member), counts_of(member)):
            safe = jnp.where(weight > 0.0, blurred, 1.0)
            parts.append(weight * counts / safe)
        put_field(member, parts, z_high, z_low, out_rows + 8)
    t_ref[...] = dot_split(z_high[...], z_low[...], wc_high[...], wc_low[...])
    out[...] = model * gather_taps(t_ref, out_rows) / norm


def put_model(model_refs, wide):
    at = 0
    for ref in model_refs:
        wide[pl.ds(at, ref.shape[0]), :] = ref[...]
        at += ref.shape[0]


def first_kernel(
    weight_at, at, received, before, own, after, wb_high, wb_low, wc_high, wc_low, blurred, norm, wide, x_high, x_low, g_ref, z_high, t_ref
):
    members, rows, width = blurred.shape
    out_rows = norm.shape[0]
    table_row = received.shape[1] - 8
    lane = lane_of((8, LANES)) % WINDOW
    used = (lane >= 1) & (lane < TAPS)
    for member in range(members):
        for group in range(2):
            entry = received[member, pl.ds(table_row, 8), pl.ds(LANES * group, LANES)]
            straight = jnp.where(used, entry, 0.0)
            flipped = jnp.where(used, pltpu.roll(entry, LANES - TAPS, 1), 0.0)
            for s in range(8):
                band = jnp.broadcast_to(flipped[s : s + 1], (BLOCK, LANES))
                high, low = split(pltpu.roll(band, 0, 1, stride=1, stride_axis=0))
                spot = (pl.ds(BLOCK * member, BLOCK), pl.ds(LANES * (8 * group + s), LANES))
                wb_high[spot] = high
                wb_low[spot] = low
                band = jnp.broadcast_to(straight[s : s + 1], (BLOCK, LANES))
                high, low = split(pltpu.roll(band, 0, 1, stride=1, stride_axis=0))
                spot = (pl.ds(BLOCK * s, BLOCK), pl.ds((2 * member + group) * LANES, LANES))
                wc_high[spot] = high
                wc_low[spot] = low
    put_model((before, own, after), wide)
    blur_all(wb_high, wb_low, wide, x_high, x_low, g_ref)
    for member in range(members):
        for slab, part in enumerate(blurred_parts(g_ref, member, rows, width // LANES)):
            blurred[member, :, pl.ds(LANES * slab, LANES)] = part
    for member in range(members):
        weight = weight_at(member, at[0, 0], received=received, rows=rows)
        put_field(member, [weight] * (width // LANES), z_high, None, out_rows + 8)
    t_ref[...] = dot_t(z_high[...], wc_high[...]) + dot_t(z_high[...], wc_low[...])
    norm[...] = gather_taps(t_ref, out_rows)


def second_kernel(weight_at, group, at, wc_high, wc_low, received, blurred, model, norm, *refs):
    pair_refs, (out, data, z_high, z_low, t_ref, window) = refs[:group], refs[group:]
    shard_rows = (received.shape[1] - 8) // 2
    out_rows, width = out.shape
    place = at[0, 1]
    slabs = [pl.ds(first, LANES) for first in range(0, width, LANES)]

    def blurred_of(member):
        return [blurred[member, :, slab] for slab in slabs]

    def counts_of(member):
        parts = []
        for slab in slabs:
            own, edge = ([ref[member, pl.ds(first, shard_rows), slab] for ref in pair_refs] for first in (0, shard_rows))
            own, edge = group_order(own, place), group_order(edge, place)
            parts.append(jnp.concatenate(edge[group // 2 :] + own + edge[: group // 2], axis=0))
            window[:, slab] = parts[-1]
        data[member] = window[pl.ds(pl.multiple_of(place * shard_rows, shard_rows), data.shape[1]), :]
        return parts

    weight_of_group = functools.partial(weight_at, first_row=at[0, 0], received=received, rows=out_rows + TAPS)
    update(blurred_of, weight_of_group, counts_of, model[...], norm[...], wc_high, wc_low, z_high, z_low, t_ref, out)


def third_kernel(
    weight_at, at, wb_high, wb_low, wc_high, wc_low, received, norm, data, before, own, after, out, tall, wide, x_high, x_low, g_ref, z_high, z_low, t_ref
):
    out_rows, width = out.shape
    rows = out_rows + TAPS
    first = pl.multiple_of(at[0, 1] * out_rows, out_rows)
    put_model((before, own, after), tall)
    wide[...] = tall[pl.ds(first, wide.shape[0]), :]
    blur_all(wb_high, wb_low, wide, x_high, x_low, g_ref)
    blurred_of = functools.partial(blurred_parts, g_ref, rows=rows, slabs=width // LANES)

    def counts_of(member):
        return [data[member, :, pl.ds(slab, LANES)] for slab in range(0, width, LANES)]

    weight_of_shard = functools.partial(weight_at, first_row=at[0, 0] + first, received=received, rows=rows)
    model, scale = own[pl.ds(first, out_rows), :], norm[pl.ds(first, out_rows), :]
    update(blurred_of, weight_of_shard, counts_of, model, scale, wc_high, wc_low, z_high, z_low, t_ref, out)


def call(kernel, out_shape, scratch_shapes, flops, *operands, scalars=0):
    whole = pl.BlockSpec(memory_space=pltpu.VMEM)
    scalar = pl.BlockSpec(memory_space=pltpu.SMEM)
    return pl.pallas_call(
        kernel,
        out_shape=out_shape,
        in_specs=[scalar] * scalars + [whole] * (len(operands) - scalars),
        out_specs=jax.tree.map(lambda _: whole, out_shape),
        scratch_shapes=scratch_shapes,
        compiler_params=pltpu.CompilerParams(vmem_limit_bytes=VMEM_BYTES),
        cost_estimate=pl.CostEstimate(flops=flops, bytes_accessed=4 * 1024 * 1024, transcendentals=0),
    )(*operands)


def strip_permute(array, target):
    tiles, members = lax.axis_size("tile"), lax.axis_size("visit")
    count = tiles * members
    place = [i % members * tiles + i // members for i in range(count)]
    pairs = [(place[i], place[target(i)]) for i in range(count) if 0 <= target(i) < count]
    return lax.ppermute(array, ("visit", "tile"), pairs)


def group_gather(array, group):
    return [array] + [strip_permute(array, lambda i: i // group * group + (i + k) % group) for k in range(1, group)]


def group_order(arrays, place):
    ordered = []
    for slot in range(len(arrays)):
        back = (place - slot) % len(arrays)
        picked = arrays[0]
        for k in range(1, len(arrays)):
            picked = jnp.where(back == k, arrays[k], picked)
        ordered.append(picked)
    return ordered


def group_neighbours(rows, group):
    return [strip_permute(rows, lambda i: i + group), rows, strip_permute(rows, lambda i: i - group)]


def body(exposures, sky_model, blur_kernels, coverage):
    tile_rows, width = exposures.shape[1:]
    shard_rows = sky_model.shape[0]
    members = lax.axis_size("visit")
    tiles = lax.axis_size("tile")
    group = TAPS // shard_rows
    place = lax.axis_index("visit") % group
    group_row = lax.axis_index("tile") * tile_rows + (lax.axis_index("visit") - place) * shard_rows
    at = jnp.stack([group_row, place]).reshape(1, 2)

    f32, bf16 = jnp.float32, jnp.bfloat16
    shape = jax.ShapeDtypeStruct
    blocks = width // BLOCK
    depth = TAPS * WINDOW

    halo = TAPS // 2
    first, last = exposures[0, :halo], exposures[0, tile_rows - halo :]
    if tiles == 2:
        above = below = lax.ppermute(jnp.where(lax.axis_index("tile") == 0, last, first), "tile", [(0, 1), (1, 0)])
    else:
        above = lax.ppermute(last, "tile", [(i, i + 1) for i in range(tiles - 1)])
        below = lax.ppermute(first, "tile", [(i + 1, i) for i in range(tiles - 1)])
    sent = call(
        functools.partial(send_kernel, group),
        shape((members, 2 * shard_rows + 8, width), f32),
        [pltpu.VMEM((TAPS, LANES), f32)],
        1 << 22,
        *(coverage, exposures, above, below, blur_kernels),
    )
    received = lax.all_to_all(sent, "visit", 0, 0)
    mine = jnp.concatenate(group_order(group_gather(sky_model, group), place), axis=0)
    near = group_neighbours(mine, group)
    received, near = lax.optimization_barrier((received, near))
    pairs = group_gather(received, group)

    def blur_scratch(out_rows):
        rows = out_rows + TAPS
        return [
            pltpu.VMEM((rows + TAPS, width), f32),
            pltpu.VMEM((blocks * rows, depth), bf16),
            pltpu.VMEM((blocks * rows, depth), bf16),
            pltpu.VMEM((blocks * rows, members * BLOCK), f32),
        ]

    def field(out_rows):
        return pltpu.VMEM((blocks * (out_rows + 8), members * 4 * WINDOW), bf16)

    def product(out_rows):
        return pltpu.VMEM((blocks * (out_rows + 8), 8 * BLOCK), f32)

    blur_flops = 6 * blocks * (TAPS + shard_rows) * depth * members * BLOCK
    sum_flops = 6 * blocks * (shard_rows + 8) * members * 4 * WINDOW * 8 * BLOCK
    weight_at = functools.partial(weight_of, tile_rows=tile_rows, tiles=tiles)
    wb_high, wb_low, wc_high, wc_low, blurred, norm = call(
        functools.partial(first_kernel, weight_at),
        (
            shape((members * BLOCK, depth), bf16),
            shape((members * BLOCK, depth), bf16),
            shape((8 * BLOCK, members * 4 * WINDOW), bf16),
            shape((8 * BLOCK, members * 4 * WINDOW), bf16),
            shape((members, 2 * TAPS, width), f32),
            shape((TAPS, width), f32),
        ),
        blur_scratch(TAPS) + [field(TAPS), product(TAPS)],
        blur_flops + sum_flops,
        *(at, received, *near),
        scalars=1,
    )
    model, data = call(
        functools.partial(second_kernel, weight_at, group),
        (shape((TAPS, width), f32), shape((members, shard_rows + TAPS, width), f32)),
        [field(TAPS), field(TAPS), product(TAPS), pltpu.VMEM((2 * TAPS, width), f32)],
        sum_flops,
        *(at, wc_high, wc_low, received, blurred, mine, norm, *pairs),
        scalars=1,
    )
    return call(
        functools.partial(third_kernel, weight_at),
        shape((shard_rows, width), f32),
        [pltpu.VMEM((3 * TAPS, width), f32)]
        + blur_scratch(shard_rows)
        + [field(shard_rows), field(shard_rows), product(shard_rows)],
        blur_flops + sum_flops,
        *(at, wb_high, wb_low, wc_high, wc_low, received, norm, data, *group_neighbours(model, group)),
        scalars=1,
    )


def solution(mesh):
    return jax.shard_map(
        body,
        mesh=mesh,
        in_specs=(
            P("visit", "tile", None),
            P(("tile", "visit"), None),
            P("visit", None, None),
            P("visit", None),
        ),
        out_specs=P(("tile", "visit"), None),
        check_vma=False,
    )
```

```python
import functools

import jax
import jax.numpy as jnp
from jax import lax
from jax.experimental import pallas as pl
from jax.experimental.pallas import tpu as pltpu
from jax.sharding import PartitionSpec as P

LANES = 128
BLOCK = 32
WINDOW = 64
TAPS = 32
MARGIN = WINDOW // 4
CHUNK = 4
VMEM_BYTES = 20 * 1024 * 1024


def split(x):
    high = x.astype(jnp.bfloat16)
    low = (x - high.astype(jnp.float32)).astype(jnp.bfloat16)
    return high, low


def dot_t(x, w):
    return lax.dot_general(x, w, (((1,), (1,)), ((), ())), preferred_element_type=jnp.float32)


def dot_split(both, w_high, w_low):
    rows = both.shape[0] // 2
    wide = dot_t(both[...], w_high)
    return wide[:rows] + (wide[rows:] + dot_t(both[pl.ds(0, rows), :], w_low))


def lane_of(shape):
    return lax.broadcasted_iota(jnp.int32, shape, len(shape) - 1)


def column_windows(parts):
    rows = parts[0].shape[0] - 8
    lane = lane_of((rows, LANES))
    shifts = sorted({(MARGIN - BLOCK * j) % LANES for j in range(LANES // BLOCK)})
    rolled = [{shift: pltpu.roll(part, shift, 1) for shift in shifts} for part in parts]
    windows = []
    for j in range(len(parts) * LANES // BLOCK):
        start = BLOCK * j - MARGIN
        first = start // LANES
        cut = (first + 1) * LANES - start

        def piece(slab):
            if slab < 0 or slab >= len(parts):
                return jnp.zeros((rows, LANES), jnp.float32)
            near = rolled[slab][(-start) % LANES][:rows]
            far = rolled[slab][(WINDOW - start) % LANES][8:]
            return jnp.where(lane < WINDOW, near, far)

        window = piece(first)
        if cut < WINDOW:
            window = jnp.where(lane % WINDOW < cut, window, piece(first + 1))
        windows.append(window)
    return windows


def put_field(member, parts, z_ref, sum_rows):
    windows = column_windows(parts)
    for pair in range(len(windows) // 2):
        for group in range(2):
            rows = [window[16 * group : 16 * group + sum_rows] for window in windows[2 * pair : 2 * pair + 2]]
            high, low = split(jnp.concatenate(rows, axis=0))
            lanes = pl.ds((2 * member + group) * LANES, LANES)
            z_ref[pl.ds(2 * pair * sum_rows, 2 * sum_rows), lanes] = high
            z_ref[pl.ds((2 * pair + len(windows)) * sum_rows, 2 * sum_rows), lanes] = low


def gather_taps(t_ref, out_rows):
    sum_rows = out_rows + 8
    lane = lane_of((out_rows, LANES))
    halves = []
    for half in range(t_ref.shape[0] // sum_rows // 4):
        total = None
        for i in range(4):
            picked = None
            for jj in range(4):
                base = (4 * half + jj) * sum_rows + i
                near = t_ref[pl.ds(base, out_rows), pl.ds(0, LANES)]
                far = t_ref[pl.ds(base + 4, out_rows), pl.ds(LANES, LANES)]
                moved = pltpu.roll(near + far, (BLOCK * (jj - i)) % LANES, 1) if jj != i else near + far
                picked = moved if picked is None else jnp.where(lane >= BLOCK * jj, moved, picked)
            total = picked if total is None else total + picked
        halves.append(total)
    return jnp.concatenate(halves, axis=1)


def blur_all(wb_high, wb_low, wide, x_ref, g_ref):
    slabs = wide.shape[1] // LANES
    blocks = wide.shape[1] // BLOCK
    half = x_ref.shape[0] // 2
    rows = half // blocks
    for s in range(8):
        parts = [wide[pl.ds(s, rows + 24), pl.ds(LANES * i, LANES)] for i in range(slabs)]
        windows = column_windows(parts)
        for j in range(blocks):
            high, low = split(windows[j])
            for group in range(2):
                lanes = pl.ds((8 * group + s) * LANES, LANES)
                x_ref[pl.ds(rows * j, rows), lanes] = high[16 * group : 16 * group + rows]
                x_ref[pl.ds(half + rows * j, rows), lanes] = low[16 * group : 16 * group + rows]
    step = min(2 * LANES, wb_high.shape[0])
    for at in range(0, wb_high.shape[0], step):
        g_ref[:, pl.ds(at, step)] = dot_split(x_ref, wb_high[pl.ds(at, step), :], wb_low[pl.ds(at, step), :])


def blurred_parts(g_ref, member, rows, slabs):
    lane = lane_of((rows, LANES))
    place = member % 4
    parts = []
    for slab in range(slabs):
        picked = None
        for jj in range(4):
            block = g_ref[pl.ds((4 * slab + jj) * rows, rows), pl.ds(member // 4 * LANES, LANES)]
            moved = pltpu.roll(block, (BLOCK * (jj - place)) % LANES, 1) if jj != place else block
            picked = moved if picked is None else jnp.where(lane >= BLOCK * jj, moved, picked)
        parts.append(picked)
    return parts


def table_of(kernel, cover, padded):
    size = kernel.shape[0]
    front = TAPS - size
    padded[...] = jnp.zeros(padded.shape, jnp.float32)
    padded[pl.ds(front, size), pl.ds(front, size)] = kernel / jnp.sum(kernel)
    straight = padded[...]
    row = lax.broadcasted_iota(jnp.int32, (TAPS, TAPS), 0)
    turn_rows = (row + lane_of((TAPS, TAPS)) == TAPS).astype(jnp.float32)
    row = lax.broadcasted_iota(jnp.int32, (LANES, LANES), 0)
    turn_lanes = (row + lane_of((LANES, LANES)) == TAPS).astype(jnp.float32)
    exact = functools.partial(jnp.dot, precision=lax.Precision.HIGHEST, preferred_element_type=jnp.float32)
    flipped = exact(exact(turn_rows, straight), turn_lanes)
    both = straight + pltpu.roll(flipped, TAPS, 1)
    half = [both[8 * i : 8 * i + 8] for i in range(4)]
    groups = [half[2 * i] + pltpu.roll(half[2 * i + 1], WINDOW, 1) for i in range(2)]
    row = lax.broadcasted_iota(jnp.int32, groups[0].shape, 0)
    lane = lane_of(groups[0].shape)
    for tile in range(cover.shape[1]):
        spot = (row == tile % 8) & (lane == 0)
        entry = jnp.broadcast_to(cover[0:1, tile : tile + 1].astype(jnp.float32), spot.shape)
        groups[tile // 8] = jnp.where(spot, entry, groups[tile // 8])
    return groups


def send_kernel(group, cover, counts, above, below, kernels, out, padded):
    groups = table_of(kernels[0], cover, padded)
    peers = out.shape[0]
    own = (out.shape[1] - 8) // 2
    for peer in range(peers):
        place = peer % group
        out[peer, pl.ds(0, own), :] = counts[0, pl.ds(peer * own, own), :]
        block = peer - group if 2 * place >= group else peer + group
        if block < 0:
            edge = above[pl.ds((place - group // 2) * own, own), :]
        elif block >= peers:
            edge = below[pl.ds(place * own, own), :]
        else:
            edge = counts[0, pl.ds(block * own, own), :]
        out[peer, pl.ds(own, own), :] = edge
        for half in range(2):
            out[peer, pl.ds(2 * own, 8), pl.ds(LANES * half, LANES)] = groups[half]


def weight_of(member, first_row, tile_rows, tiles, received, rows):
    own = received.shape[1] - 8
    row = first_row - TAPS // 2 + lax.broadcasted_iota(jnp.int32, (rows, LANES), 0)
    weight = jnp.zeros((rows, LANES), jnp.float32)
    for tile in range(tiles):
        entry = received[member, pl.ds(own + tile % 8, 1), pl.ds(tile // 8 * LANES, LANES)]
        inside = (row >= tile * tile_rows) & (row < (tile + 1) * tile_rows)
        weight = jnp.where(inside, jnp.broadcast_to(entry[:, 0:1], (rows, LANES)), weight)
    return weight


def update(blurred_of, weight_at, counts_of, model, norm, wc_high, wc_low, z_ref, t_ref, out):
    out_rows = out.shape[0]
    members = z_ref.shape[1] // (4 * WINDOW)
    for first in range(0, members, CHUNK):
        for member in range(first, first + CHUNK):
            weight = weight_at(member)
            parts = []
            for blurred, counts in zip(blurred_of(member), counts_of(member)):
                safe = jnp.where(weight > 0.0, blurred, 1.0)
                parts.append(weight * counts / safe)
            put_field(member, parts, z_ref, out_rows + 8)
        lanes = pl.ds(4 * WINDOW * first, 4 * WINDOW * CHUNK)
        part = dot_split(z_ref.at[:, lanes], wc_high[:, lanes], wc_low[:, lanes])
        t_ref[...] = part if first == 0 else t_ref[...] + part
    out[...] = model * gather_taps(t_ref, out_rows) / norm


def norm_field(first_row, tile_rows, tiles, received, norm):
    out_rows, width = norm.shape
    members = received.shape[0]
    table_row = received.shape[1] - 8
    tables = [
        received[:, pl.ds(table_row, 8), pl.ds(LANES * group, LANES)].reshape(8 * members, LANES) for group in range(2)
    ]
    entry = lax.broadcasted_iota(jnp.int32, (8 * members, 8 * members), 0)
    lane = lane_of((8 * members, 8 * members))
    covers = []
    for tile in range(tiles):
        column = jnp.broadcast_to(tables[tile // 8][:, 0:1], entry.shape)
        spot = entry == lane // 8 * 8 + tile % 8
        covers.append(jnp.sum(jnp.where(spot, column, 0.0), axis=0, keepdims=True))
    row = lax.broadcasted_iota(jnp.int32, (out_rows, 8 * members), 0) + lane_of((out_rows, 8 * members)) % 8
    total = None
    for index in range(4):
        group, half = divmod(index, 2)
        offset = lax.broadcasted_iota(jnp.int32, (LANES, width), 0) - WINDOW * half
        column = lane_of((LANES, width)) + offset - TAPS // 2
        inside = (offset >= 1) & (offset < TAPS) & (column >= 0) & (column < width)
        inside = inside.astype(jnp.bfloat16)
        high, low = split(tables[group])
        sums = jnp.dot(high, inside, preferred_element_type=jnp.float32)
        sums = sums + jnp.dot(low, inside, preferred_element_type=jnp.float32)
        place = row + (first_row - TAPS // 2 + 8 * index)
        weight = jnp.zeros(place.shape, jnp.float32)
        for tile in range(tiles):
            covered = (place >= tile * tile_rows) & (place < (tile + 1) * tile_rows)
            weight = jnp.where(covered, jnp.broadcast_to(covers[tile], place.shape), weight)
        weight = weight.astype(jnp.bfloat16)
        high, low = split(sums)
        part = jnp.dot(weight, high, preferred_element_type=jnp.float32)
        part = part + jnp.dot(weight, low, preferred_element_type=jnp.float32)
        total = part if total is None else total + part
    norm[...] = total


def put_model(model_refs, wide):
    at = 0
    for ref in model_refs:
        wide[pl.ds(at, ref.shape[0]), :] = ref[...]
        at += ref.shape[0]


def first_kernel(
    norm_at, at, received, before, own, after, wb_high, wb_low, wc_high, wc_low, blurred, norm, wide, x_ref, g_ref
):
    members, rows, width = blurred.shape
    table_row = received.shape[1] - 8
    lane = lane_of((8, LANES)) % WINDOW
    used = (lane >= 1) & (lane < TAPS)
    for member in range(members):
        for group in range(2):
            entry = received[member, pl.ds(table_row, 8), pl.ds(LANES * group, LANES)]
            straight = jnp.where(used, entry, 0.0)
            flipped = jnp.where(used, pltpu.roll(entry, LANES - TAPS, 1), 0.0)
            for s in range(8):
                band = jnp.broadcast_to(flipped[s : s + 1], (BLOCK, LANES))
                high, low = split(pltpu.roll(band, 0, 1, stride=1, stride_axis=0))
                spot = (pl.ds(BLOCK * member, BLOCK), pl.ds(LANES * (8 * group + s), LANES))
                wb_high[spot] = high
                wb_low[spot] = low
                band = jnp.broadcast_to(straight[s : s + 1], (BLOCK, LANES))
                high, low = split(pltpu.roll(band, 0, 1, stride=1, stride_axis=0))
                spot = (pl.ds(BLOCK * s, BLOCK), pl.ds((2 * member + group) * LANES, LANES))
                wc_high[spot] = high
                wc_low[spot] = low
    put_model((before, own, after), wide)
    blur_all(wb_high, wb_low, wide, x_ref, g_ref)
    for member in range(members):
        for slab, part in enumerate(blurred_parts(g_ref, member, rows, width // LANES)):
            blurred[member, :, pl.ds(LANES * slab, LANES)] = part
    norm_at(at[0, 0], received=received, norm=norm)


def second_kernel(weight_at, group, at, wc_high, wc_low, received, blurred, model, norm, *refs):
    pair_refs, (out, data, z_ref, t_ref, window) = refs[:group], refs[group:]
    shard_rows = (received.shape[1] - 8) // 2
    out_rows, width = out.shape
    place = at[0, 1]
    slabs = [pl.ds(first, LANES) for first in range(0, width, LANES)]

    def blurred_of(member):
        return [blurred[member, :, slab] for slab in slabs]

    def counts_of(member):
        parts = []
        for slab in slabs:
            own, edge = ([ref[member, pl.ds(first, shard_rows), slab] for ref in pair_refs] for first in (0, shard_rows))
            own, edge = group_order(own, place), group_order(edge, place)
            parts.append(jnp.concatenate(edge[group // 2 :] + own + edge[: group // 2], axis=0))
            window[:, slab] = parts[-1]
        data[member] = window[pl.ds(pl.multiple_of(place * shard_rows, shard_rows), data.shape[1]), :]
        return parts

    weight_of_group = functools.partial(weight_at, first_row=at[0, 0], received=received, rows=out_rows + TAPS)
    update(blurred_of, weight_of_group, counts_of, model[...], norm[...], wc_high, wc_low, z_ref, t_ref, out)


def third_kernel(
    weight_at, at, wb_high, wb_low, wc_high, wc_low, received, norm, data, before, own, after, out, tall, wide, x_ref, g_ref, z_ref, t_ref
):
    out_rows, width = out.shape
    rows = out_rows + TAPS
    first = pl.multiple_of(at[0, 1] * out_rows, out_rows)
    put_model((before, own, after), tall)
    wide[...] = tall[pl.ds(first, wide.shape[0]), :]
    blur_all(wb_high, wb_low, wide, x_ref, g_ref)
    blurred_of = functools.partial(blurred_parts, g_ref, rows=rows, slabs=width // LANES)

    def counts_of(member):
        return [data[member, :, pl.ds(slab, LANES)] for slab in range(0, width, LANES)]

    weight_of_shard = functools.partial(weight_at, first_row=at[0, 0] + first, received=received, rows=rows)
    model, scale = own[pl.ds(first, out_rows), :], norm[pl.ds(first, out_rows), :]
    update(blurred_of, weight_of_shard, counts_of, model, scale, wc_high, wc_low, z_ref, t_ref, out)


def call(kernel, out_shape, scratch_shapes, flops, *operands, scalars=0):
    whole = pl.BlockSpec(memory_space=pltpu.VMEM)
    scalar = pl.BlockSpec(memory_space=pltpu.SMEM)
    return pl.pallas_call(
        kernel,
        out_shape=out_shape,
        in_specs=[scalar] * scalars + [whole] * (len(operands) - scalars),
        out_specs=jax.tree.map(lambda _: whole, out_shape),
        scratch_shapes=scratch_shapes,
        compiler_params=pltpu.CompilerParams(vmem_limit_bytes=VMEM_BYTES),
        cost_estimate=pl.CostEstimate(flops=flops, bytes_accessed=4 * 1024 * 1024, transcendentals=0),
    )(*operands)


def strip_permute(array, target):
    tiles, members = lax.axis_size("tile"), lax.axis_size("visit")
    count = tiles * members
    place = [i % members * tiles + i // members for i in range(count)]
    pairs = [(place[i], place[target(i)]) for i in range(count) if 0 <= target(i) < count]
    return lax.ppermute(array, ("visit", "tile"), pairs)


def group_gather(array, group):
    return [array] + [strip_permute(array, lambda i: i // group * group + (i + k) % group) for k in range(1, group)]


def group_order(arrays, place):
    ordered = []
    for slot in range(len(arrays)):
        back = (place - slot) % len(arrays)
        picked = arrays[0]
        for k in range(1, len(arrays)):
            picked = jnp.where(back == k, arrays[k], picked)
        ordered.append(picked)
    return ordered


def group_neighbours(rows, group):
    return [strip_permute(rows, lambda i: i + group), rows, strip_permute(rows, lambda i: i - group)]


def body(exposures, sky_model, blur_kernels, coverage):
    tile_rows, width = exposures.shape[1:]
    shard_rows = sky_model.shape[0]
    members = lax.axis_size("visit")
    tiles = lax.axis_size("tile")
    group = TAPS // shard_rows
    place = lax.axis_index("visit") % group
    group_row = lax.axis_index("tile") * tile_rows + (lax.axis_index("visit") - place) * shard_rows
    at = jnp.stack([group_row, place]).reshape(1, 2)

    f32, bf16 = jnp.float32, jnp.bfloat16
    shape = jax.ShapeDtypeStruct
    blocks = width // BLOCK
    depth = TAPS * WINDOW

    halo = TAPS // 2
    first, last = exposures[0, :halo], exposures[0, tile_rows - halo :]
    if tiles == 2:
        above = below = lax.ppermute(jnp.where(lax.axis_index("tile") == 0, last, first), "tile", [(0, 1), (1, 0)])
    else:
        above = lax.ppermute(last, "tile", [(i, i + 1) for i in range(tiles - 1)])
        below = lax.ppermute(first, "tile", [(i + 1, i) for i in range(tiles - 1)])
    sent = call(
        functools.partial(send_kernel, group),
        shape((members, 2 * shard_rows + 8, width), f32),
        [pltpu.VMEM((TAPS, LANES), f32)],
        1 << 22,
        *(coverage, exposures, above, below, blur_kernels),
    )
    received = lax.all_to_all(sent, "visit", 0, 0)
    mine = jnp.concatenate(group_order(group_gather(sky_model, group), place), axis=0)
    near = group_neighbours(mine, group)
    received, near = lax.optimization_barrier((received, near))
    pairs = group_gather(received, group)

    def blur_scratch(out_rows):
        rows = out_rows + TAPS
        return [
            pltpu.VMEM((rows + TAPS, width), f32),
            pltpu.VMEM((2 * blocks * rows, depth), bf16),
            pltpu.VMEM((blocks * rows, members * BLOCK), f32),
        ]

    def field(out_rows):
        return pltpu.VMEM((2 * blocks * (out_rows + 8), members * 4 * WINDOW), bf16)

    def product(out_rows):
        return pltpu.VMEM((blocks * (out_rows + 8), 8 * BLOCK), f32)

    blur_flops = 6 * blocks * (TAPS + shard_rows) * depth * members * BLOCK
    sum_flops = 6 * blocks * (shard_rows + 8) * members * 4 * WINDOW * 8 * BLOCK
    weight_at = functools.partial(weight_of, tile_rows=tile_rows, tiles=tiles)
    wb_high, wb_low, wc_high, wc_low, blurred, norm = call(
        functools.partial(first_kernel, functools.partial(norm_field, tile_rows=tile_rows, tiles=tiles)),
        (
            shape((members * BLOCK, depth), bf16),
            shape((members * BLOCK, depth), bf16),
            shape((8 * BLOCK, members * 4 * WINDOW), bf16),
            shape((8 * BLOCK, members * 4 * WINDOW), bf16),
            shape((members, 2 * TAPS, width), f32),
            shape((TAPS, width), f32),
        ),
        blur_scratch(TAPS),
        blur_flops + sum_flops,
        *(at, received, *near),
        scalars=1,
    )
    model, data = call(
        functools.partial(second_kernel, weight_at, group),
        (shape((TAPS, width), f32), shape((members, shard_rows + TAPS, width), f32)),
        [field(TAPS), product(TAPS), pltpu.VMEM((2 * TAPS, width), f32)],
        sum_flops,
        *(at, wc_high, wc_low, received, blurred, mine, norm, *pairs),
        scalars=1,
    )
    return call(
        functools.partial(third_kernel, weight_at),
        shape((shard_rows, width), f32),
        [pltpu.VMEM((3 * TAPS, width), f32)]
        + blur_scratch(shard_rows)
        + [field(shard_rows), product(shard_rows)],
        blur_flops + sum_flops,
        *(at, wb_high, wb_low, wc_high, wc_low, received, norm, data, *group_neighbours(model, group)),
        scalars=1,
    )


def solution(mesh):
    return jax.shard_map(
        body,
        mesh=mesh,
        in_specs=(
            P("visit", "tile", None),
            P(("tile", "visit"), None),
            P("visit", None, None),
            P("visit", None),
        ),
        out_specs=P(("tile", "visit"), None),
        check_vma=False,
    )
```

```python
import functools

import jax
import jax.numpy as jnp
from jax import lax
from jax.experimental import pallas as pl
from jax.experimental.pallas import tpu as pltpu
from jax.sharding import PartitionSpec as P

LANES = 128
BLOCK = 32
WINDOW = 64
TAPS = 32
MARGIN = WINDOW // 4
CHUNK = 4
VMEM_BYTES = 20 * 1024 * 1024


def split(x):
    high = x.astype(jnp.bfloat16)
    low = (x - high.astype(jnp.float32)).astype(jnp.bfloat16)
    return high, low


def dot_t(x, w):
    return lax.dot_general(x, w, (((1,), (1,)), ((), ())), preferred_element_type=jnp.float32)


def dot_split(both, w_high, w_low):
    rows = both.shape[0] // 2
    wide = dot_t(both[...], w_high)
    return wide[:rows] + (wide[rows:] + dot_t(both[pl.ds(0, rows), :], w_low))


def lane_of(shape):
    return lax.broadcasted_iota(jnp.int32, shape, len(shape) - 1)


def column_windows(parts):
    rows = parts[0].shape[0] - 8
    lane = lane_of((rows, LANES))
    shifts = sorted({(MARGIN - BLOCK * j) % LANES for j in range(LANES // BLOCK)})
    rolled = [{shift: pltpu.roll(part, shift, 1) for shift in shifts} for part in parts]
    windows = []
    for j in range(len(parts) * LANES // BLOCK):
        start = BLOCK * j - MARGIN
        first = start // LANES
        cut = (first + 1) * LANES - start

        def piece(slab):
            if slab < 0 or slab >= len(parts):
                return jnp.zeros((rows, LANES), jnp.float32)
            near = rolled[slab][(-start) % LANES][:rows]
            far = rolled[slab][(WINDOW - start) % LANES][8:]
            return jnp.where(lane < WINDOW, near, far)

        window = piece(first)
        if cut < WINDOW:
            window = jnp.where(lane % WINDOW < cut, window, piece(first + 1))
        windows.append(window)
    return windows


def put_field(member, parts, z_ref, sum_rows):
    windows = column_windows(parts)
    for pair in range(len(windows) // 2):
        for group in range(2):
            rows = [window[16 * group : 16 * group + sum_rows] for window in windows[2 * pair : 2 * pair + 2]]
            high, low = split(jnp.concatenate(rows, axis=0))
            lanes = pl.ds((2 * member + group) * LANES, LANES)
            z_ref[pl.ds(2 * pair * sum_rows, 2 * sum_rows), lanes] = high
            z_ref[pl.ds((2 * pair + len(windows)) * sum_rows, 2 * sum_rows), lanes] = low


def gather_taps(t_ref, out_rows):
    sum_rows = out_rows + 8
    lane = lane_of((out_rows, LANES))
    halves = []
    for half in range(t_ref.shape[0] // sum_rows // 4):
        total = None
        for i in range(4):
            picked = None
            for jj in range(4):
                base = (4 * half + jj) * sum_rows + i
                near = t_ref[pl.ds(base, out_rows), pl.ds(0, LANES)]
                far = t_ref[pl.ds(base + 4, out_rows), pl.ds(LANES, LANES)]
                moved = pltpu.roll(near + far, (BLOCK * (jj - i)) % LANES, 1) if jj != i else near + far
                picked = moved if picked is None else jnp.where(lane >= BLOCK * jj, moved, picked)
            total = picked if total is None else total + picked
        halves.append(total)
    return jnp.concatenate(halves, axis=1)


def blur_all(wb_high, wb_low, wide, x_ref, g_ref):
    slabs = wide.shape[1] // LANES
    blocks = wide.shape[1] // BLOCK
    half = x_ref.shape[0] // 2
    rows = half // blocks
    for s in range(8):
        parts = [wide[pl.ds(s, rows + 24), pl.ds(LANES * i, LANES)] for i in range(slabs)]
        windows = column_windows(parts)
        for j in range(blocks):
            high, low = split(windows[j])
            for group in range(2):
                lanes = pl.ds((8 * group + s) * LANES, LANES)
                x_ref[pl.ds(rows * j, rows), lanes] = high[16 * group : 16 * group + rows]
                x_ref[pl.ds(half + rows * j, rows), lanes] = low[16 * group : 16 * group + rows]
    step = min(2 * LANES, wb_high.shape[0])
    for at in range(0, wb_high.shape[0], step):
        g_ref[:, pl.ds(at, step)] = dot_split(x_ref, wb_high[pl.ds(at, step), :], wb_low[pl.ds(at, step), :])


def blurred_parts(g_ref, member, rows, slabs):
    lane = lane_of((rows, LANES))
    place = member % 4
    parts = []
    for slab in range(slabs):
        picked = None
        for jj in range(4):
            block = g_ref[pl.ds((4 * slab + jj) * rows, rows), pl.ds(member // 4 * LANES, LANES)]
            moved = pltpu.roll(block, (BLOCK * (jj - place)) % LANES, 1) if jj != place else block
            picked = moved if picked is None else jnp.where(lane >= BLOCK * jj, moved, picked)
        parts.append(picked)
    return parts


def table_of(kernel, cover, padded):
    size = kernel.shape[0]
    front = TAPS - size
    padded[...] = jnp.zeros(padded.shape, jnp.float32)
    for row in range(size):
        padded[pl.ds(front + row, 1), pl.ds(front, size)] = kernel[row]
    straight = padded[...]
    straight = straight / jnp.sum(straight)
    row = lax.broadcasted_iota(jnp.int32, (TAPS, TAPS), 0)
    turn_rows = (row + lane_of((TAPS, TAPS)) == TAPS).astype(jnp.float32)
    row = lax.broadcasted_iota(jnp.int32, (LANES, LANES), 0)
    turn_lanes = (row + lane_of((LANES, LANES)) == TAPS).astype(jnp.float32)
    exact = functools.partial(jnp.dot, precision=lax.Precision.HIGHEST, preferred_element_type=jnp.float32)
    flipped = exact(exact(turn_rows, straight), turn_lanes)
    both = straight + pltpu.roll(flipped, TAPS, 1)
    half = [both[8 * i : 8 * i + 8] for i in range(4)]
    groups = [half[2 * i] + pltpu.roll(half[2 * i + 1], WINDOW, 1) for i in range(2)]
    row = lax.broadcasted_iota(jnp.int32, groups[0].shape, 0)
    lane = lane_of(groups[0].shape)
    for tile in range(cover.shape[1]):
        spot = (row == tile % 8) & (lane == 0)
        entry = jnp.broadcast_to(cover[0:1, tile : tile + 1].astype(jnp.float32), spot.shape)
        groups[tile // 8] = jnp.where(spot, entry, groups[tile // 8])
    return groups


def send_kernel(group, cover, counts, kernels, above, below, out, padded):
    groups = table_of(kernels, cover, padded)
    peers = out.shape[0]
    own = (out.shape[1] - 8) // 2
    for peer in range(peers):
        place = peer % group
        out[peer, pl.ds(0, own), :] = counts[0, pl.ds(peer * own, own), :]
        block = peer - group if 2 * place >= group else peer + group
        if block < 0:
            edge = above[pl.ds((place - group // 2) * own, own), :]
        elif block >= peers:
            edge = below[pl.ds(place * own, own), :]
        else:
            edge = counts[0, pl.ds(block * own, own), :]
        out[peer, pl.ds(own, own), :] = edge
        for half in range(2):
            out[peer, pl.ds(2 * own, 8), pl.ds(LANES * half, LANES)] = groups[half]


def weight_of(member, first_row, tile_rows, tiles, received, rows):
    own = received.shape[1] - 8
    row = first_row - TAPS // 2 + lax.broadcasted_iota(jnp.int32, (rows, LANES), 0)
    weight = jnp.zeros((rows, LANES), jnp.float32)
    for tile in range(tiles):
        entry = received[member, pl.ds(own + tile % 8, 1), pl.ds(tile // 8 * LANES, LANES)]
        inside = (row >= tile * tile_rows) & (row < (tile + 1) * tile_rows)
        weight = jnp.where(inside, jnp.broadcast_to(entry[:, 0:1], (rows, LANES)), weight)
    return weight


def update(blurred_of, weight_at, counts_of, model, norm, wc_high, wc_low, z_ref, t_ref, out):
    out_rows = out.shape[0]
    members = z_ref.shape[1] // (4 * WINDOW)
    for first in range(0, members, CHUNK):
        for member in range(first, first + CHUNK):
            weight = weight_at(member)
            parts = []
            for blurred, counts in zip(blurred_of(member), counts_of(member)):
                safe = jnp.where(weight > 0.0, blurred, 1.0)
                parts.append(weight * counts / safe)
            put_field(member, parts, z_ref, out_rows + 8)
        lanes = pl.ds(4 * WINDOW * first, 4 * WINDOW * CHUNK)
        part = dot_split(z_ref.at[:, lanes], wc_high[:, lanes], wc_low[:, lanes])
        t_ref[...] = part if first == 0 else t_ref[...] + part
    out[...] = model * gather_taps(t_ref, out_rows) / norm


def norm_field(first_row, tile_rows, tiles, received, norm):
    out_rows, width = norm.shape
    members = received.shape[0]
    table_row = received.shape[1] - 8
    tables = [
        received[:, pl.ds(table_row, 8), pl.ds(LANES * group, LANES)].reshape(8 * members, LANES) for group in range(2)
    ]
    entry = lax.broadcasted_iota(jnp.int32, (8 * members, 8 * members), 0)
    lane = lane_of((8 * members, 8 * members))
    covers = []
    for tile in range(tiles):
        column = jnp.broadcast_to(tables[tile // 8][:, 0:1], entry.shape)
        spot = entry == lane // 8 * 8 + tile % 8
        covers.append(jnp.sum(jnp.where(spot, column, 0.0), axis=0, keepdims=True))
    row = lax.broadcasted_iota(jnp.int32, (out_rows, 8 * members), 0) + lane_of((out_rows, 8 * members)) % 8
    total = None
    for index in range(4):
        group, half = divmod(index, 2)
        offset = lax.broadcasted_iota(jnp.int32, (LANES, width), 0) - WINDOW * half
        column = lane_of((LANES, width)) + offset - TAPS // 2
        inside = (offset >= 1) & (offset < TAPS) & (column >= 0) & (column < width)
        inside = inside.astype(jnp.bfloat16)
        high, low = split(tables[group])
        sums = jnp.dot(high, inside, preferred_element_type=jnp.float32)
        sums = sums + jnp.dot(low, inside, preferred_element_type=jnp.float32)
        place = row + (first_row - TAPS // 2 + 8 * index)
        weight = jnp.zeros(place.shape, jnp.float32)
        for tile in range(tiles):
            covered = (place >= tile * tile_rows) & (place < (tile + 1) * tile_rows)
            weight = jnp.where(covered, jnp.broadcast_to(covers[tile], place.shape), weight)
        weight = weight.astype(jnp.bfloat16)
        high, low = split(sums)
        part = jnp.dot(weight, high, preferred_element_type=jnp.float32)
        part = part + jnp.dot(weight, low, preferred_element_type=jnp.float32)
        total = part if total is None else total + part
    norm[...] = total


def put_model(refs, parity, wide):
    even_swap, own, odd_swap = refs
    rows = own.shape[0]
    wide[pl.ds(rows, rows), :] = own[...]
    wide[pl.ds(pl.multiple_of(2 * rows * (1 - parity), rows), rows), :] = even_swap[...]
    wide[pl.ds(pl.multiple_of(2 * rows * parity, rows), rows), :] = odd_swap[...]


def first_kernel(
    norm_at, at, received, even_swap, own, odd_swap, wb_high, wb_low, wc_high, wc_low, blurred, norm, wide, x_ref, g_ref
):
    members, rows, width = blurred.shape
    table_row = received.shape[1] - 8
    lane = lane_of((8, LANES)) % WINDOW
    used = (lane >= 1) & (lane < TAPS)
    for member in range(members):
        for group in range(2):
            entry = received[member, pl.ds(table_row, 8), pl.ds(LANES * group, LANES)]
            straight = jnp.where(used, entry, 0.0)
            flipped = jnp.where(used, pltpu.roll(entry, LANES - TAPS, 1), 0.0)
            for s in range(8):
                band = jnp.broadcast_to(flipped[s : s + 1], (BLOCK, LANES))
                high, low = split(pltpu.roll(band, 0, 1, stride=1, stride_axis=0))
                spot = (pl.ds(BLOCK * member, BLOCK), pl.ds(LANES * (8 * group + s), LANES))
                wb_high[spot] = high
                wb_low[spot] = low
                band = jnp.broadcast_to(straight[s : s + 1], (BLOCK, LANES))
                high, low = split(pltpu.roll(band, 0, 1, stride=1, stride_axis=0))
                spot = (pl.ds(BLOCK * s, BLOCK), pl.ds((2 * member + group) * LANES, LANES))
                wc_high[spot] = high
                wc_low[spot] = low
    put_model((even_swap, own, odd_swap), at[0, 2], wide)
    blur_all(wb_high, wb_low, wide, x_ref, g_ref)
    for member in range(members):
        for slab, part in enumerate(blurred_parts(g_ref, member, rows, width // LANES)):
            blurred[member, :, pl.ds(LANES * slab, LANES)] = part
    norm_at(at[0, 0], received=received, norm=norm)


def second_kernel(weight_at, group, at, wc_high, wc_low, received, blurred, model, norm, *refs):
    pair_refs, (out, data, z_ref, t_ref, window) = refs[:group], refs[group:]
    shard_rows = (received.shape[1] - 8) // 2
    out_rows, width = out.shape
    place = at[0, 1]
    slabs = [pl.ds(first, LANES) for first in range(0, width, LANES)]

    def blurred_of(member):
        return [blurred[member, :, slab] for slab in slabs]

    def counts_of(member):
        parts = []
        for slab in slabs:
            own, edge = ([ref[member, pl.ds(first, shard_rows), slab] for ref in pair_refs] for first in (0, shard_rows))
            own, edge = group_order(own, place), group_order(edge, place)
            parts.append(jnp.concatenate(edge[group // 2 :] + own + edge[: group // 2], axis=0))
            window[:, slab] = parts[-1]
        data[member] = window[pl.ds(pl.multiple_of(place * shard_rows, shard_rows), data.shape[1]), :]
        return parts

    weight_of_group = functools.partial(weight_at, first_row=at[0, 0], received=received, rows=out_rows + TAPS)
    update(blurred_of, weight_of_group, counts_of, model[...], norm[...], wc_high, wc_low, z_ref, t_ref, out)


def third_kernel(
    weight_at, at, wb_high, wb_low, wc_high, wc_low, received, norm, data, even_swap, own, odd_swap, out, tall, wide, x_ref, g_ref, z_ref, t_ref
):
    out_rows, width = out.shape
    rows = out_rows + TAPS
    first = pl.multiple_of(at[0, 1] * out_rows, out_rows)
    put_model((even_swap, own, odd_swap), at[0, 2], tall)
    wide[...] = tall[pl.ds(first, wide.shape[0]), :]
    blur_all(wb_high, wb_low, wide, x_ref, g_ref)
    blurred_of = functools.partial(blurred_parts, g_ref, rows=rows, slabs=width // LANES)

    def counts_of(member):
        return [data[member, :, pl.ds(slab, LANES)] for slab in range(0, width, LANES)]

    weight_of_shard = functools.partial(weight_at, first_row=at[0, 0] + first, received=received, rows=rows)
    model, scale = own[pl.ds(first, out_rows), :], norm[pl.ds(first, out_rows), :]
    update(blurred_of, weight_of_shard, counts_of, model, scale, wc_high, wc_low, z_ref, t_ref, out)


def call(kernel, out_shape, scratch_shapes, flops, *operands, scalars=0):
    whole = pl.BlockSpec(memory_space=pltpu.VMEM)
    scalar = pl.BlockSpec(memory_space=pltpu.SMEM)
    return pl.pallas_call(
        kernel,
        out_shape=out_shape,
        in_specs=[scalar] * scalars + [whole] * (len(operands) - scalars),
        out_specs=jax.tree.map(lambda _: whole, out_shape),
        scratch_shapes=scratch_shapes,
        compiler_params=pltpu.CompilerParams(vmem_limit_bytes=VMEM_BYTES),
        cost_estimate=pl.CostEstimate(flops=flops, bytes_accessed=4 * 1024 * 1024, transcendentals=0),
    )(*operands)


def strip_permute(array, target):
    tiles, members = lax.axis_size("tile"), lax.axis_size("visit")
    count = tiles * members
    place = [i % members * tiles + i // members for i in range(count)]
    pairs = [(place[i], place[target(i)]) for i in range(count) if 0 <= target(i) < count]
    return lax.ppermute(array, ("visit", "tile"), pairs)


def group_gather(array, group):
    return [array] + [strip_permute(array, lambda i: i // group * group + (i + k) % group) for k in range(1, group)]


def group_order(arrays, place):
    ordered = []
    for slot in range(len(arrays)):
        back = (place - slot) % len(arrays)
        picked = arrays[0]
        for k in range(1, len(arrays)):
            picked = jnp.where(back == k, arrays[k], picked)
        ordered.append(picked)
    return ordered


def group_swaps(rows, group):
    def partner(first):
        return lambda i: i + group if i // group % 2 == first else i - group

    return [strip_permute(rows, partner(0)), rows, strip_permute(rows, partner(1))]


def body(exposures, sky_model, blur_kernels, coverage):
    tile_rows, width = exposures.shape[1:]
    shard_rows = sky_model.shape[0]
    members = lax.axis_size("visit")
    tiles = lax.axis_size("tile")
    group = TAPS // shard_rows
    place = lax.axis_index("visit") % group
    group_row = lax.axis_index("tile") * tile_rows + (lax.axis_index("visit") - place) * shard_rows
    parity = lax.axis_index("visit") // group % 2
    at = jnp.stack([group_row, place, parity]).reshape(1, 3)

    f32, bf16 = jnp.float32, jnp.bfloat16
    shape = jax.ShapeDtypeStruct
    blocks = width // BLOCK
    depth = TAPS * WINDOW

    halo = TAPS // 2
    first, last = exposures[0, :halo], exposures[0, tile_rows - halo :]
    if tiles == 2:
        above = below = lax.ppermute(jnp.where(lax.axis_index("tile") == 0, last, first), "tile", [(0, 1), (1, 0)])
    else:
        above = lax.ppermute(last, "tile", [(i, i + 1) for i in range(tiles - 1)])
        below = lax.ppermute(first, "tile", [(i + 1, i) for i in range(tiles - 1)])
    sent = call(
        functools.partial(send_kernel, group),
        shape((members, 2 * shard_rows + 8, width), f32),
        [pltpu.VMEM((TAPS, LANES), f32)],
        1 << 22,
        *(coverage, exposures, jnp.transpose(blur_kernels, (1, 0, 2)), above, below),
    )
    received = lax.all_to_all(sent, "visit", 0, 0)
    mine = jnp.concatenate(group_order(group_gather(sky_model, group), place), axis=0)
    near = group_swaps(mine, group)
    received, near = lax.optimization_barrier((received, near))
    pairs = group_gather(received, group)

    def blur_scratch(out_rows):
        rows = out_rows + TAPS
        return [
            pltpu.VMEM((rows + TAPS, width), f32),
            pltpu.VMEM((2 * blocks * rows, depth), bf16),
            pltpu.VMEM((blocks * rows, members * BLOCK), f32),
        ]

    def field(out_rows):
        return pltpu.VMEM((2 * blocks * (out_rows + 8), members * 4 * WINDOW), bf16)

    def product(out_rows):
        return pltpu.VMEM((blocks * (out_rows + 8), 8 * BLOCK), f32)

    blur_flops = 6 * blocks * (TAPS + shard_rows) * depth * members * BLOCK
    sum_flops = 6 * blocks * (shard_rows + 8) * members * 4 * WINDOW * 8 * BLOCK
    weight_at = functools.partial(weight_of, tile_rows=tile_rows, tiles=tiles)
    wb_high, wb_low, wc_high, wc_low, blurred, norm = call(
        functools.partial(first_kernel, functools.partial(norm_field, tile_rows=tile_rows, tiles=tiles)),
        (
            shape((members * BLOCK, depth), bf16),
            shape((members * BLOCK, depth), bf16),
            shape((8 * BLOCK, members * 4 * WINDOW), bf16),
            shape((8 * BLOCK, members * 4 * WINDOW), bf16),
            shape((members, 2 * TAPS, width), f32),
            shape((TAPS, width), f32),
        ),
        blur_scratch(TAPS),
        blur_flops + sum_flops,
        *(at, received, *near),
        scalars=1,
    )
    model, data = call(
        functools.partial(second_kernel, weight_at, group),
        (shape((TAPS, width), f32), shape((members, shard_rows + TAPS, width), f32)),
        [field(TAPS), product(TAPS), pltpu.VMEM((2 * TAPS, width), f32)],
        sum_flops,
        *(at, wc_high, wc_low, received, blurred, mine, norm, *pairs),
        scalars=1,
    )
    return call(
        functools.partial(third_kernel, weight_at),
        shape((shard_rows, width), f32),
        [pltpu.VMEM((3 * TAPS, width), f32)]
        + blur_scratch(shard_rows)
        + [field(shard_rows), product(shard_rows)],
        blur_flops + sum_flops,
        *(at, wb_high, wb_low, wc_high, wc_low, received, norm, data, *group_swaps(model, group)),
        scalars=1,
    )


def solution(mesh):
    return jax.shard_map(
        body,
        mesh=mesh,
        in_specs=(
            P("visit", "tile", None),
            P(("tile", "visit"), None),
            P("visit", None, None),
            P("visit", None),
        ),
        out_specs=P(("tile", "visit"), None),
        check_vma=False,
    )
```

```python
import functools

import jax
import jax.numpy as jnp
from jax import lax
from jax.experimental import pallas as pl
from jax.experimental.pallas import tpu as pltpu
from jax.sharding import PartitionSpec as P

LANES = 128
BLOCK = 32
WINDOW = 64
TAPS = 32
MARGIN = WINDOW // 4
CHUNK = LANES // BLOCK
VMEM_BYTES = 20 * 1024 * 1024


def split(x):
    high = x.astype(jnp.bfloat16)
    low = (x - high.astype(jnp.float32)).astype(jnp.bfloat16)
    return high, low


def dot_t(x, w):
    return lax.dot_general(x, w, (((1,), (1,)), ((), ())), preferred_element_type=jnp.float32)


def dot_split(both, w_high, w_low):
    rows = both.shape[0] // 2
    wide = dot_t(both[...], w_high)
    return wide[:rows] + (wide[rows:] + dot_t(both[pl.ds(0, rows), :], w_low))


def lanes_at(first, size=LANES):
    return pl.ds(pl.multiple_of(first, LANES), size)


def lane_of(shape):
    return lax.broadcasted_iota(jnp.int32, shape, len(shape) - 1)


def column_windows(parts):
    rows = parts[0].shape[0] - 8
    lane = lane_of((rows, LANES))
    shifts = sorted({(MARGIN - BLOCK * j) % LANES for j in range(LANES // BLOCK)})
    rolled = [{shift: pltpu.roll(part, shift, 1) for shift in shifts} for part in parts]
    windows = []
    for j in range(len(parts) * LANES // BLOCK):
        start = BLOCK * j - MARGIN
        first = start // LANES
        cut = (first + 1) * LANES - start

        def piece(slab):
            if slab < 0 or slab >= len(parts):
                return jnp.zeros((rows, LANES), jnp.float32)
            near = rolled[slab][(-start) % LANES][:rows]
            far = rolled[slab][(WINDOW - start) % LANES][8:]
            return jnp.where(lane < WINDOW, near, far)

        window = piece(first)
        if cut < WINDOW:
            window = jnp.where(lane % WINDOW < cut, window, piece(first + 1))
        windows.append(window)
    return windows


def put_field(member, parts, z_ref, sum_rows):
    windows = column_windows(parts)
    for pair in range(len(windows) // 2):
        for group in range(2):
            rows = [window[16 * group : 16 * group + sum_rows] for window in windows[2 * pair : 2 * pair + 2]]
            high, low = split(jnp.concatenate(rows, axis=0))
            lanes = lanes_at((2 * member + group) * LANES)
            z_ref[pl.ds(2 * pair * sum_rows, 2 * sum_rows), lanes] = high
            z_ref[pl.ds((2 * pair + len(windows)) * sum_rows, 2 * sum_rows), lanes] = low


def gather_taps(t_ref, out_rows):
    sum_rows = out_rows + 8
    lane = lane_of((out_rows, LANES))
    halves = []
    for half in range(t_ref.shape[0] // sum_rows // 4):
        total = None
        for i in range(4):
            picked = None
            for jj in range(4):
                base = (4 * half + jj) * sum_rows + i
                near = t_ref[pl.ds(base, out_rows), pl.ds(0, LANES)]
                far = t_ref[pl.ds(base + 4, out_rows), pl.ds(LANES, LANES)]
                moved = pltpu.roll(near + far, (BLOCK * (jj - i)) % LANES, 1) if jj != i else near + far
                picked = moved if picked is None else jnp.where(lane >= BLOCK * jj, moved, picked)
            total = picked if total is None else total + picked
        halves.append(total)
    return jnp.concatenate(halves, axis=1)


def blur_all(wb_high, wb_low, wide, x_ref, g_ref):
    slabs = wide.shape[1] // LANES
    blocks = wide.shape[1] // BLOCK
    half = x_ref.shape[0] // 2
    rows = half // blocks
    for s in range(8):
        parts = [wide[pl.ds(s, rows + 24), pl.ds(LANES * i, LANES)] for i in range(slabs)]
        windows = column_windows(parts)
        for j in range(blocks):
            high, low = split(windows[j])
            for group in range(2):
                lanes = pl.ds((8 * group + s) * LANES, LANES)
                x_ref[pl.ds(rows * j, rows), lanes] = high[16 * group : 16 * group + rows]
                x_ref[pl.ds(half + rows * j, rows), lanes] = low[16 * group : 16 * group + rows]
    step = 2 * LANES

    def product(index, carry):
        at = pl.multiple_of(index * step, step)
        g_ref[:, lanes_at(at, step)] = dot_split(x_ref, wb_high[pl.ds(at, step), :], wb_low[pl.ds(at, step), :])
        return carry

    lax.fori_loop(0, wb_high.shape[0] // step, product, 0)


def blurred_parts(g_ref, chunk, place, rows, slabs):
    lane = lane_of((rows, LANES))
    parts = []
    for slab in range(slabs):
        picked = None
        for jj in range(4):
            block = g_ref[pl.ds((4 * slab + jj) * rows, rows), lanes_at(chunk * LANES)]
            moved = pltpu.roll(block, (BLOCK * (jj - place)) % LANES, 1) if jj != place else block
            picked = moved if picked is None else jnp.where(lane >= BLOCK * jj, moved, picked)
        parts.append(picked)
    return parts


def table_of(kernel, cover, padded):
    size = kernel.shape[0]
    front = TAPS - size
    padded[...] = jnp.zeros(padded.shape, jnp.float32)
    for row in range(size):
        padded[pl.ds(front + row, 1), pl.ds(front, size)] = kernel[row]
    straight = padded[...]
    straight = straight / jnp.sum(straight)
    row = lax.broadcasted_iota(jnp.int32, (TAPS, TAPS), 0)
    turn_rows = (row + lane_of((TAPS, TAPS)) == TAPS).astype(jnp.float32)
    row = lax.broadcasted_iota(jnp.int32, (LANES, LANES), 0)
    turn_lanes = (row + lane_of((LANES, LANES)) == TAPS).astype(jnp.float32)
    exact = functools.partial(jnp.dot, precision=lax.Precision.HIGHEST, preferred_element_type=jnp.float32)
    flipped = exact(exact(turn_rows, straight), turn_lanes)
    both = straight + pltpu.roll(flipped, TAPS, 1)
    half = [both[8 * i : 8 * i + 8] for i in range(4)]
    groups = [half[2 * i] + pltpu.roll(half[2 * i + 1], WINDOW, 1) for i in range(2)]
    row = lax.broadcasted_iota(jnp.int32, groups[0].shape, 0)
    lane = lane_of(groups[0].shape)
    for tile in range(cover.shape[1]):
        spot = (row == tile % 8) & (lane == 0)
        entry = jnp.broadcast_to(cover[0:1, tile : tile + 1].astype(jnp.float32), spot.shape)
        groups[tile // 8] = jnp.where(spot, entry, groups[tile // 8])
    return groups


def send_kernel(group, cover, counts, kernels, above, below, out, padded):
    groups = table_of(kernels, cover, padded)
    peers = out.shape[0]
    own = (out.shape[1] - 8) // 2
    for peer in range(peers):
        place = peer % group
        out[peer, pl.ds(0, own), :] = counts[0, pl.ds(peer * own, own), :]
        block = peer - group if 2 * place >= group else peer + group
        if block < 0:
            edge = above[pl.ds((place - group // 2) * own, own), :]
        elif block >= peers:
            edge = below[pl.ds(place * own, own), :]
        else:
            edge = counts[0, pl.ds(block * own, own), :]
        out[peer, pl.ds(own, own), :] = edge
        for half in range(2):
            out[peer, pl.ds(2 * own, 8), pl.ds(LANES * half, LANES)] = groups[half]


def weight_of(member, first_row, tile_rows, tiles, received, rows):
    own = received.shape[1] - 8
    row = first_row - TAPS // 2 + lax.broadcasted_iota(jnp.int32, (rows, LANES), 0)
    weight = jnp.zeros((rows, LANES), jnp.float32)
    for tile in range(tiles):
        entry = received[member, pl.ds(own + tile % 8, 1), pl.ds(tile // 8 * LANES, LANES)]
        inside = (row >= tile * tile_rows) & (row < (tile + 1) * tile_rows)
        weight = jnp.where(inside, jnp.broadcast_to(entry[:, 0:1], (rows, LANES)), weight)
    return weight


def update(blurred_of, weight_at, counts_of, model, norm, wc_high, wc_low, z_ref, t_ref, out):
    out_rows = out.shape[0]
    t_ref[...] = jnp.zeros(t_ref.shape, jnp.float32)

    def add(chunk, carry):
        for place in range(CHUNK):
            member = chunk * CHUNK + place
            weight = weight_at(member)
            parts = []
            for blurred, counts in zip(blurred_of(chunk, place), counts_of(member)):
                safe = jnp.where(weight > 0.0, blurred, 1.0)
                parts.append(weight * counts / safe)
            put_field(place, parts, z_ref, out_rows + 8)
        lanes = lanes_at(chunk * z_ref.shape[1], z_ref.shape[1])
        t_ref[...] += dot_split(z_ref, wc_high[:, lanes], wc_low[:, lanes])
        return carry

    lax.fori_loop(0, wc_high.shape[1] // z_ref.shape[1], add, 0)
    out[...] = model * gather_taps(t_ref, out_rows) / norm


def norm_field(first_row, tile_rows, tiles, received, norm):
    out_rows, width = norm.shape
    members = received.shape[0]
    table_row = received.shape[1] - 8
    tables = [
        received[:, pl.ds(table_row, 8), pl.ds(LANES * group, LANES)].reshape(8 * members, LANES) for group in range(2)
    ]
    entry = lax.broadcasted_iota(jnp.int32, (8 * members, 8 * members), 0)
    lane = lane_of((8 * members, 8 * members))
    covers = []
    for tile in range(tiles):
        column = jnp.broadcast_to(tables[tile // 8][:, 0:1], entry.shape)
        spot = entry == lane // 8 * 8 + tile % 8
        covers.append(jnp.sum(jnp.where(spot, column, 0.0), axis=0, keepdims=True))
    row = lax.broadcasted_iota(jnp.int32, (out_rows, 8 * members), 0) + lane_of((out_rows, 8 * members)) % 8
    total = None
    for index in range(4):
        group, half = divmod(index, 2)
        offset = lax.broadcasted_iota(jnp.int32, (LANES, width), 0) - WINDOW * half
        column = lane_of((LANES, width)) + offset - TAPS // 2
        inside = (offset >= 1) & (offset < TAPS) & (column >= 0) & (column < width)
        inside = inside.astype(jnp.bfloat16)
        high, low = split(tables[group])
        sums = jnp.dot(high, inside, preferred_element_type=jnp.float32)
        sums = sums + jnp.dot(low, inside, preferred_element_type=jnp.float32)
        place = row + (first_row - TAPS // 2 + 8 * index)
        weight = jnp.zeros(place.shape, jnp.float32)
        for tile in range(tiles):
            covered = (place >= tile * tile_rows) & (place < (tile + 1) * tile_rows)
            weight = jnp.where(covered, jnp.broadcast_to(covers[tile], place.shape), weight)
        weight = weight.astype(jnp.bfloat16)
        high, low = split(sums)
        part = jnp.dot(weight, high, preferred_element_type=jnp.float32)
        part = part + jnp.dot(weight, low, preferred_element_type=jnp.float32)
        total = part if total is None else total + part
    norm[...] = total


def put_model(refs, parity, wide):
    even_swap, own, odd_swap = refs
    rows = own.shape[0]
    wide[pl.ds(rows, rows), :] = own[...]
    wide[pl.ds(pl.multiple_of(2 * rows * (1 - parity), rows), rows), :] = even_swap[...]
    wide[pl.ds(pl.multiple_of(2 * rows * parity, rows), rows), :] = odd_swap[...]


def first_kernel(
    norm_at, at, received, even_swap, own, odd_swap, wb_high, wb_low, wc_high, wc_low, blurred, norm, wide, x_ref, g_ref
):
    members, rows, width = blurred.shape
    table_row = received.shape[1] - 8
    lane = lane_of((8, LANES)) % WINDOW
    used = (lane >= 1) & (lane < TAPS)
    def build(member, carry):
        for group in range(2):
            entry = received[member, pl.ds(table_row, 8), pl.ds(LANES * group, LANES)]
            straight = jnp.where(used, entry, 0.0)
            flipped = jnp.where(used, pltpu.roll(entry, LANES - TAPS, 1), 0.0)
            for s in range(8):
                band = jnp.broadcast_to(flipped[s : s + 1], (BLOCK, LANES))
                high, low = split(pltpu.roll(band, 0, 1, stride=1, stride_axis=0))
                spot = (pl.ds(pl.multiple_of(BLOCK * member, BLOCK), BLOCK), pl.ds(LANES * (8 * group + s), LANES))
                wb_high[spot] = high
                wb_low[spot] = low
                band = jnp.broadcast_to(straight[s : s + 1], (BLOCK, LANES))
                high, low = split(pltpu.roll(band, 0, 1, stride=1, stride_axis=0))
                spot = (pl.ds(BLOCK * s, BLOCK), lanes_at((2 * member + group) * LANES))
                wc_high[spot] = high
                wc_low[spot] = low
        return carry

    lax.fori_loop(0, members, build, 0)
    put_model((even_swap, own, odd_swap), at[0, 2], wide)
    blur_all(wb_high, wb_low, wide, x_ref, g_ref)

    def reorder(chunk, carry):
        for place in range(CHUNK):
            for slab, part in enumerate(blurred_parts(g_ref, chunk, place, rows, width // LANES)):
                blurred[chunk * CHUNK + place, :, pl.ds(LANES * slab, LANES)] = part
        return carry

    lax.fori_loop(0, members // CHUNK, reorder, 0)
    norm_at(at[0, 0], received=received, norm=norm)


def second_kernel(weight_at, group, at, wc_high, wc_low, received, blurred, model, norm, *refs):
    pair_refs, (out, data, z_ref, t_ref, window) = refs[:group], refs[group:]
    shard_rows = (received.shape[1] - 8) // 2
    out_rows, width = out.shape
    place = at[0, 1]
    slabs = [pl.ds(first, LANES) for first in range(0, width, LANES)]

    def blurred_of(chunk, place):
        return [blurred[chunk * CHUNK + place, :, slab] for slab in slabs]

    def counts_of(member):
        parts = []
        for slab in slabs:
            own, edge = ([ref[member, pl.ds(first, shard_rows), slab] for ref in pair_refs] for first in (0, shard_rows))
            own, edge = group_order(own, place), group_order(edge, place)
            parts.append(jnp.concatenate(edge[group // 2 :] + own + edge[: group // 2], axis=0))
            window[:, slab] = parts[-1]
        data[member] = window[pl.ds(pl.multiple_of(place * shard_rows, shard_rows), data.shape[1]), :]
        return parts

    weight_of_group = functools.partial(weight_at, first_row=at[0, 0], received=received, rows=out_rows + TAPS)
    update(blurred_of, weight_of_group, counts_of, model[...], norm[...], wc_high, wc_low, z_ref, t_ref, out)


def third_kernel(
    weight_at, at, wb_high, wb_low, wc_high, wc_low, received, norm, data, even_swap, own, odd_swap, out, tall, wide, x_ref, g_ref, z_ref, t_ref
):
    out_rows, width = out.shape
    rows = out_rows + TAPS
    first = pl.multiple_of(at[0, 1] * out_rows, out_rows)
    put_model((even_swap, own, odd_swap), at[0, 2], tall)
    wide[...] = tall[pl.ds(first, wide.shape[0]), :]
    blur_all(wb_high, wb_low, wide, x_ref, g_ref)
    blurred_of = functools.partial(blurred_parts, g_ref, rows=rows, slabs=width // LANES)

    def counts_of(member):
        return [data[member, :, pl.ds(slab, LANES)] for slab in range(0, width, LANES)]

    weight_of_shard = functools.partial(weight_at, first_row=at[0, 0] + first, received=received, rows=rows)
    model, scale = own[pl.ds(first, out_rows), :], norm[pl.ds(first, out_rows), :]
    update(blurred_of, weight_of_shard, counts_of, model, scale, wc_high, wc_low, z_ref, t_ref, out)


def call(kernel, out_shape, scratch_shapes, flops, *operands, scalars=0):
    whole = pl.BlockSpec(memory_space=pltpu.VMEM)
    scalar = pl.BlockSpec(memory_space=pltpu.SMEM)
    return pl.pallas_call(
        kernel,
        out_shape=out_shape,
        in_specs=[scalar] * scalars + [whole] * (len(operands) - scalars),
        out_specs=jax.tree.map(lambda _: whole, out_shape),
        scratch_shapes=scratch_shapes,
        compiler_params=pltpu.CompilerParams(vmem_limit_bytes=VMEM_BYTES),
        cost_estimate=pl.CostEstimate(flops=flops, bytes_accessed=4 * 1024 * 1024, transcendentals=0),
    )(*operands)


def strip_permute(array, target):
    tiles, members = lax.axis_size("tile"), lax.axis_size("visit")
    count = tiles * members
    place = [i % members * tiles + i // members for i in range(count)]
    pairs = [(place[i], place[target(i)]) for i in range(count) if 0 <= target(i) < count]
    return lax.ppermute(array, ("visit", "tile"), pairs)


def group_gather(array, group):
    return [array] + [strip_permute(array, lambda i: i // group * group + (i + k) % group) for k in range(1, group)]


def group_order(arrays, place):
    ordered = []
    for slot in range(len(arrays)):
        back = (place - slot) % len(arrays)
        picked = arrays[0]
        for k in range(1, len(arrays)):
            picked = jnp.where(back == k, arrays[k], picked)
        ordered.append(picked)
    return ordered


def group_swaps(rows, group):
    def partner(first):
        return lambda i: i + group if i // group % 2 == first else i - group

    return [strip_permute(rows, partner(0)), rows, strip_permute(rows, partner(1))]


def body(exposures, sky_model, blur_kernels, coverage):
    tile_rows, width = exposures.shape[1:]
    shard_rows = sky_model.shape[0]
    members = lax.axis_size("visit")
    tiles = lax.axis_size("tile")
    group = TAPS // shard_rows
    place = lax.axis_index("visit") % group
    group_row = lax.axis_index("tile") * tile_rows + (lax.axis_index("visit") - place) * shard_rows
    parity = lax.axis_index("visit") // group % 2
    at = jnp.stack([group_row, place, parity]).reshape(1, 3)

    f32, bf16 = jnp.float32, jnp.bfloat16
    shape = jax.ShapeDtypeStruct
    blocks = width // BLOCK
    depth = TAPS * WINDOW

    halo = TAPS // 2
    first, last = exposures[0, :halo], exposures[0, tile_rows - halo :]
    if tiles == 2:
        above = below = lax.ppermute(jnp.where(lax.axis_index("tile") == 0, last, first), "tile", [(0, 1), (1, 0)])
    else:
        above = lax.ppermute(last, "tile", [(i, i + 1) for i in range(tiles - 1)])
        below = lax.ppermute(first, "tile", [(i + 1, i) for i in range(tiles - 1)])
    sent = call(
        functools.partial(send_kernel, group),
        shape((members, 2 * shard_rows + 8, width), f32),
        [pltpu.VMEM((TAPS, LANES), f32)],
        1 << 22,
        *(coverage, exposures, jnp.transpose(blur_kernels, (1, 0, 2)), above, below),
    )
    received = lax.all_to_all(sent, "visit", 0, 0)
    mine = jnp.concatenate(group_order(group_gather(sky_model, group), place), axis=0)
    near = group_swaps(mine, group)
    received, near = lax.optimization_barrier((received, near))
    pairs = group_gather(received, group)

    def blur_scratch(out_rows):
        rows = out_rows + TAPS
        return [
            pltpu.VMEM((rows + TAPS, width), f32),
            pltpu.VMEM((2 * blocks * rows, depth), bf16),
            pltpu.VMEM((blocks * rows, members * BLOCK), f32),
        ]

    def field(out_rows):
        return pltpu.VMEM((2 * blocks * (out_rows + 8), CHUNK * 4 * WINDOW), bf16)

    def product(out_rows):
        return pltpu.VMEM((blocks * (out_rows + 8), 8 * BLOCK), f32)

    blur_flops = 6 * blocks * (TAPS + shard_rows) * depth * members * BLOCK
    sum_flops = 6 * blocks * (shard_rows + 8) * members * 4 * WINDOW * 8 * BLOCK
    weight_at = functools.partial(weight_of, tile_rows=tile_rows, tiles=tiles)
    wb_high, wb_low, wc_high, wc_low, blurred, norm = call(
        functools.partial(first_kernel, functools.partial(norm_field, tile_rows=tile_rows, tiles=tiles)),
        (
            shape((members * BLOCK, depth), bf16),
            shape((members * BLOCK, depth), bf16),
            shape((8 * BLOCK, members * 4 * WINDOW), bf16),
            shape((8 * BLOCK, members * 4 * WINDOW), bf16),
            shape((members, 2 * TAPS, width), f32),
            shape((TAPS, width), f32),
        ),
        blur_scratch(TAPS),
        blur_flops + sum_flops,
        *(at, received, *near),
        scalars=1,
    )
    model, data = call(
        functools.partial(second_kernel, weight_at, group),
        (shape((TAPS, width), f32), shape((members, shard_rows + TAPS, width), f32)),
        [field(TAPS), product(TAPS), pltpu.VMEM((2 * TAPS, width), f32)],
        sum_flops,
        *(at, wc_high, wc_low, received, blurred, mine, norm, *pairs),
        scalars=1,
    )
    return call(
        functools.partial(third_kernel, weight_at),
        shape((shard_rows, width), f32),
        [pltpu.VMEM((3 * TAPS, width), f32)]
        + blur_scratch(shard_rows)
        + [field(shard_rows), product(shard_rows)],
        blur_flops + sum_flops,
        *(at, wb_high, wb_low, wc_high, wc_low, received, norm, data, *group_swaps(model, group)),
        scalars=1,
    )


def solution(mesh):
    return jax.shard_map(
        body,
        mesh=mesh,
        in_specs=(
            P("visit", "tile", None),
            P(("tile", "visit"), None),
            P("visit", None, None),
            P("visit", None),
        ),
        out_specs=P(("tile", "visit"), None),
        check_vma=False,
    )
```

```python
import functools

import jax
import jax.numpy as jnp
from jax import lax
from jax.experimental import pallas as pl
from jax.experimental.pallas import tpu as pltpu
from jax.sharding import PartitionSpec as P

LANES = 128
BLOCK = 32
WINDOW = 64
TAPS = 32
MARGIN = WINDOW // 4
CHUNK = 4
VMEM_BYTES = 20 * 1024 * 1024


def split(x):
    high = x.astype(jnp.bfloat16)
    low = (x - high.astype(jnp.float32)).astype(jnp.bfloat16)
    return high, low


def dot_t(x, w):
    return lax.dot_general(x, w, (((1,), (1,)), ((), ())), preferred_element_type=jnp.float32)


def dot_split(both, w_high, w_low):
    rows = both.shape[0] // 2
    wide = dot_t(both[...], w_high)
    return wide[:rows] + (wide[rows:] + dot_t(both[pl.ds(0, rows), :], w_low))


def lane_of(shape):
    return lax.broadcasted_iota(jnp.int32, shape, len(shape) - 1)


def column_windows(parts):
    rows = parts[0].shape[0] - 8
    lane = lane_of((rows, LANES))
    shifts = sorted({(MARGIN - BLOCK * j) % LANES for j in range(LANES // BLOCK)})
    rolled = [{shift: pltpu.roll(part, shift, 1) for shift in shifts} for part in parts]
    windows = []
    for j in range(len(parts) * LANES // BLOCK):
        start = BLOCK * j - MARGIN
        first = start // LANES
        cut = (first + 1) * LANES - start

        def piece(slab):
            if slab < 0 or slab >= len(parts):
                return jnp.zeros((rows, LANES), jnp.float32)
            near = rolled[slab][(-start) % LANES][:rows]
            far = rolled[slab][(WINDOW - start) % LANES][8:]
            return jnp.where(lane < WINDOW, near, far)

        window = piece(first)
        if cut < WINDOW:
            window = jnp.where(lane % WINDOW < cut, window, piece(first + 1))
        windows.append(window)
    return windows


def put_field(member, parts, z_ref, sum_rows):
    windows = column_windows(parts)
    for pair in range(len(windows) // 2):
        for group in range(2):
            rows = [window[16 * group : 16 * group + sum_rows] for window in windows[2 * pair : 2 * pair + 2]]
            high, low = split(jnp.concatenate(rows, axis=0))
            lanes = pl.ds((2 * member + group) * LANES, LANES)
            z_ref[pl.ds(2 * pair * sum_rows, 2 * sum_rows), lanes] = high
            z_ref[pl.ds((2 * pair + len(windows)) * sum_rows, 2 * sum_rows), lanes] = low


def gather_taps(t_ref, out_rows):
    sum_rows = out_rows + 8
    lane = lane_of((out_rows, LANES))
    halves = []
    for half in range(t_ref.shape[0] // sum_rows // 4):
        total = None
        for i in range(4):
            picked = None
            for jj in range(4):
                base = (4 * half + jj) * sum_rows + i
                near = t_ref[pl.ds(base, out_rows), pl.ds(0, LANES)]
                far = t_ref[pl.ds(base + 4, out_rows), pl.ds(LANES, LANES)]
                moved = pltpu.roll(near + far, (BLOCK * (jj - i)) % LANES, 1) if jj != i else near + far
                picked = moved if picked is None else jnp.where(lane >= BLOCK * jj, moved, picked)
            total = picked if total is None else total + picked
        halves.append(total)
    return jnp.concatenate(halves, axis=1)


def lay_model(wide, x_ref, shifts):
    slabs = wide.shape[1] // LANES
    blocks = wide.shape[1] // BLOCK
    half = x_ref.shape[0] // 2
    rows = half // blocks
    for s in shifts:
        parts = [wide[pl.ds(s, rows + 24), pl.ds(LANES * i, LANES)] for i in range(slabs)]
        windows = column_windows(parts)
        for j in range(blocks):
            high, low = split(windows[j])
            for group in range(2):
                lanes = pl.ds((2 * s + group) * LANES, LANES)
                x_ref[pl.ds(rows * j, rows), lanes] = high[16 * group : 16 * group + rows]
                x_ref[pl.ds(half + rows * j, rows), lanes] = low[16 * group : 16 * group + rows]


def blur_all(operator_for, wb_high, wb_low, wide, x_ref, g_ref):
    step = 2 * LANES
    depth = x_ref.shape[1] // 2
    for at in range(0, wb_high.shape[0], step):
        members = pl.ds(at, step)
        operator_for(range(at // BLOCK, (at + step) // BLOCK))
        if at == 0:
            for half in range(2):
                lay_model(wide, x_ref, range(4 * half, 4 * half + 4))
                lanes = pl.ds(depth * half, depth)
                part = dot_split(x_ref.at[:, lanes], wb_high[members, lanes], wb_low[members, lanes])
                g_ref[:, members] = part if half == 0 else g_ref[:, members] + part
        else:
            g_ref[:, members] = dot_split(x_ref, wb_high[members, :], wb_low[members, :])


def blurred_parts(g_ref, member, rows, slabs):
    lane = lane_of((rows, LANES))
    place = member % 4
    parts = []
    for slab in range(slabs):
        picked = None
        for jj in range(4):
            block = g_ref[pl.ds((4 * slab + jj) * rows, rows), pl.ds(member // 4 * LANES, LANES)]
            moved = pltpu.roll(block, (BLOCK * (jj - place)) % LANES, 1) if jj != place else block
            picked = moved if picked is None else jnp.where(lane >= BLOCK * jj, moved, picked)
        parts.append(picked)
    return parts


def table_of(kernel, cover, padded):
    size = kernel.shape[0]
    front = TAPS - size
    padded[...] = jnp.zeros(padded.shape, jnp.float32)
    for row in range(size):
        padded[pl.ds(front + row, 1), pl.ds(front, size)] = kernel[row]
    straight = padded[...]
    straight = straight / jnp.sum(straight)
    row = lax.broadcasted_iota(jnp.int32, (TAPS, TAPS), 0)
    turn_rows = (row + lane_of((TAPS, TAPS)) == TAPS).astype(jnp.float32)
    row = lax.broadcasted_iota(jnp.int32, (LANES, LANES), 0)
    turn_lanes = (row + lane_of((LANES, LANES)) == TAPS).astype(jnp.float32)
    exact = functools.partial(jnp.dot, precision=lax.Precision.HIGHEST, preferred_element_type=jnp.float32)
    flipped = exact(exact(turn_rows, straight), turn_lanes)
    both = straight + pltpu.roll(flipped, TAPS, 1)
    half = [both[8 * i : 8 * i + 8] for i in range(4)]
    groups = [half[2 * i] + pltpu.roll(half[2 * i + 1], WINDOW, 1) for i in range(2)]
    row = lax.broadcasted_iota(jnp.int32, groups[0].shape, 0)
    lane = lane_of(groups[0].shape)
    for tile in range(cover.shape[1]):
        spot = (row == tile % 8) & (lane == 0)
        entry = jnp.broadcast_to(cover[0:1, tile : tile + 1].astype(jnp.float32), spot.shape)
        groups[tile // 8] = jnp.where(spot, entry, groups[tile // 8])
    return groups


def send_kernel(group, cover, counts, kernels, above, below, out, padded):
    groups = table_of(kernels, cover, padded)
    peers = out.shape[0]
    own = (out.shape[1] - 8) // 2
    for peer in range(peers):
        place = peer % group
        out[peer, pl.ds(0, own), :] = counts[0, pl.ds(peer * own, own), :]
        block = peer - group if 2 * place >= group else peer + group
        if block < 0:
            edge = above[pl.ds((place - group // 2) * own, own), :]
        elif block >= peers:
            edge = below[pl.ds(place * own, own), :]
        else:
            edge = counts[0, pl.ds(block * own, own), :]
        out[peer, pl.ds(own, own), :] = edge
        for half in range(2):
            out[peer, pl.ds(2 * own, 8), pl.ds(LANES * half, LANES)] = groups[half]


def weight_of(member, first_row, tile_rows, tiles, received, rows):
    own = received.shape[1] - 8
    row = first_row - TAPS // 2 + lax.broadcasted_iota(jnp.int32, (rows, LANES), 0)
    weight = jnp.zeros((rows, LANES), jnp.float32)
    for tile in range(tiles):
        entry = received[member, pl.ds(own + tile % 8, 1), pl.ds(tile // 8 * LANES, LANES)]
        inside = (row >= tile * tile_rows) & (row < (tile + 1) * tile_rows)
        weight = jnp.where(inside, jnp.broadcast_to(entry[:, 0:1], (rows, LANES)), weight)
    return weight


def update(blurred_of, weight_at, counts_of, model, norm, wc_high, wc_low, z_ref, t_ref, out):
    out_rows = out.shape[0]
    members = z_ref.shape[1] // (4 * WINDOW)
    for first in range(0, members, CHUNK):
        for member in range(first, first + CHUNK):
            weight = weight_at(member)
            parts = []
            for blurred, counts in zip(blurred_of(member), counts_of(member)):
                safe = jnp.where(weight > 0.0, blurred, 1.0)
                parts.append(weight * counts / safe)
            put_field(member, parts, z_ref, out_rows + 8)
        lanes = pl.ds(4 * WINDOW * first, 4 * WINDOW * CHUNK)
        part = dot_split(z_ref.at[:, lanes], wc_high[:, lanes], wc_low[:, lanes])
        t_ref[...] = part if first == 0 else t_ref[...] + part
    out[...] = model * gather_taps(t_ref, out_rows) / norm


def norm_field(first_row, tile_rows, tiles, received, norm):
    out_rows, width = norm.shape
    members = received.shape[0]
    table_row = received.shape[1] - 8
    tables = [
        received[:, pl.ds(table_row, 8), pl.ds(LANES * group, LANES)].reshape(8 * members, LANES) for group in range(2)
    ]
    entry = lax.broadcasted_iota(jnp.int32, (8 * members, 8 * members), 0)
    lane = lane_of((8 * members, 8 * members))
    covers = []
    for tile in range(tiles):
        column = jnp.broadcast_to(tables[tile // 8][:, 0:1], entry.shape)
        spot = entry == lane // 8 * 8 + tile % 8
        covers.append(jnp.sum(jnp.where(spot, column, 0.0), axis=0, keepdims=True))
    row = lax.broadcasted_iota(jnp.int32, (out_rows, 8 * members), 0) + lane_of((out_rows, 8 * members)) % 8
    total = None
    for index in range(4):
        group, half = divmod(index, 2)
        offset = lax.broadcasted_iota(jnp.int32, (LANES, width), 0) - WINDOW * half
        column = lane_of((LANES, width)) + offset - TAPS // 2
        inside = (offset >= 1) & (offset < TAPS) & (column >= 0) & (column < width)
        inside = inside.astype(jnp.bfloat16)
        high, low = split(tables[group])
        sums = jnp.dot(high, inside, preferred_element_type=jnp.float32)
        sums = sums + jnp.dot(low, inside, preferred_element_type=jnp.float32)
        place = row + (first_row - TAPS // 2 + 8 * index)
        weight = jnp.zeros(place.shape, jnp.float32)
        for tile in range(tiles):
            covered = (place >= tile * tile_rows) & (place < (tile + 1) * tile_rows)
            weight = jnp.where(covered, jnp.broadcast_to(covers[tile], place.shape), weight)
        weight = weight.astype(jnp.bfloat16)
        high, low = split(sums)
        part = jnp.dot(weight, high, preferred_element_type=jnp.float32)
        part = part + jnp.dot(weight, low, preferred_element_type=jnp.float32)
        total = part if total is None else total + part
    norm[...] = total


def put_model(refs, parity, wide):
    even_swap, own, odd_swap = refs
    rows = own.shape[0]
    wide[pl.ds(rows, rows), :] = own[...]
    wide[pl.ds(pl.multiple_of(2 * rows * (1 - parity), rows), rows), :] = even_swap[...]
    wide[pl.ds(pl.multiple_of(2 * rows * parity, rows), rows), :] = odd_swap[...]


def first_kernel(
    norm_at, at, received, even_swap, own, odd_swap, wb_high, wb_low, wc_high, wc_low, blurred, norm, wide, x_ref, g_ref
):
    members, rows, width = blurred.shape
    table_row = received.shape[1] - 8
    lane = lane_of((8, LANES)) % WINDOW
    used = (lane >= 1) & (lane < TAPS)

    def entry_of(member, group):
        return received[member, pl.ds(table_row, 8), pl.ds(LANES * group, LANES)]

    def band_of(base, s):
        band = jnp.broadcast_to(base[s : s + 1], (BLOCK, LANES))
        return split(pltpu.roll(band, 0, 1, stride=1, stride_axis=0))

    def blur_operator(chosen):
        for member in chosen:
            for group in range(2):
                flipped = jnp.where(used, pltpu.roll(entry_of(member, group), LANES - TAPS, 1), 0.0)
                for s in range(8):
                    spot = (pl.ds(BLOCK * member, BLOCK), pl.ds(LANES * (2 * s + group), LANES))
                    wb_high[spot], wb_low[spot] = band_of(flipped, s)

    put_model((even_swap, own, odd_swap), at[0, 2], wide)
    blur_all(blur_operator, wb_high, wb_low, wide, x_ref, g_ref)
    for member in range(members):
        for group in range(2):
            straight = jnp.where(used, entry_of(member, group), 0.0)
            for s in range(8):
                spot = (pl.ds(BLOCK * s, BLOCK), pl.ds((2 * member + group) * LANES, LANES))
                wc_high[spot], wc_low[spot] = band_of(straight, s)
    for member in range(members):
        for slab, part in enumerate(blurred_parts(g_ref, member, rows, width // LANES)):
            blurred[member, :, pl.ds(LANES * slab, LANES)] = part
    norm_at(at[0, 0], received=received, norm=norm)


def second_kernel(weight_at, group, at, wc_high, wc_low, received, blurred, model, norm, *refs):
    pair_refs, (out, data, z_ref, t_ref, window) = refs[:group], refs[group:]
    shard_rows = (received.shape[1] - 8) // 2
    out_rows, width = out.shape
    place = at[0, 1]
    slabs = [pl.ds(first, LANES) for first in range(0, width, LANES)]

    def blurred_of(member):
        return [blurred[member, :, slab] for slab in slabs]

    def counts_of(member):
        parts = []
        for slab in slabs:
            own, edge = ([ref[member, pl.ds(first, shard_rows), slab] for ref in pair_refs] for first in (0, shard_rows))
            own, edge = group_order(own, place), group_order(edge, place)
            parts.append(jnp.concatenate(edge[group // 2 :] + own + edge[: group // 2], axis=0))
            window[:, slab] = parts[-1]
        data[member] = window[pl.ds(pl.multiple_of(place * shard_rows, shard_rows), data.shape[1]), :]
        return parts

    weight_of_group = functools.partial(weight_at, first_row=at[0, 0], received=received, rows=out_rows + TAPS)
    update(blurred_of, weight_of_group, counts_of, model[...], norm[...], wc_high, wc_low, z_ref, t_ref, out)


def third_kernel(
    weight_at, at, wb_high, wb_low, wc_high, wc_low, received, norm, data, even_swap, own, odd_swap, out, tall, wide, x_ref, g_ref, z_ref, t_ref
):
    out_rows, width = out.shape
    rows = out_rows + TAPS
    first = pl.multiple_of(at[0, 1] * out_rows, out_rows)
    put_model((even_swap, own, odd_swap), at[0, 2], tall)
    wide[...] = tall[pl.ds(first, wide.shape[0]), :]
    blur_all(lambda chosen: None, wb_high, wb_low, wide, x_ref, g_ref)
    blurred_of = functools.partial(blurred_parts, g_ref, rows=rows, slabs=width // LANES)

    def counts_of(member):
        return [data[member, :, pl.ds(slab, LANES)] for slab in range(0, width, LANES)]

    weight_of_shard = functools.partial(weight_at, first_row=at[0, 0] + first, received=received, rows=rows)
    model, scale = own[pl.ds(first, out_rows), :], norm[pl.ds(first, out_rows), :]
    update(blurred_of, weight_of_shard, counts_of, model, scale, wc_high, wc_low, z_ref, t_ref, out)


def call(kernel, out_shape, scratch_shapes, flops, *operands, scalars=0):
    whole = pl.BlockSpec(memory_space=pltpu.VMEM)
    scalar = pl.BlockSpec(memory_space=pltpu.SMEM)
    return pl.pallas_call(
        kernel,
        out_shape=out_shape,
        in_specs=[scalar] * scalars + [whole] * (len(operands) - scalars),
        out_specs=jax.tree.map(lambda _: whole, out_shape),
        scratch_shapes=scratch_shapes,
        compiler_params=pltpu.CompilerParams(vmem_limit_bytes=VMEM_BYTES),
        cost_estimate=pl.CostEstimate(flops=flops, bytes_accessed=4 * 1024 * 1024, transcendentals=0),
    )(*operands)


def strip_permute(array, target):
    tiles, members = lax.axis_size("tile"), lax.axis_size("visit")
    count = tiles * members
    place = [i % members * tiles + i // members for i in range(count)]
    pairs = [(place[i], place[target(i)]) for i in range(count) if 0 <= target(i) < count]
    return lax.ppermute(array, ("visit", "tile"), pairs)


def group_gather(array, group):
    return [array] + [strip_permute(array, lambda i: i // group * group + (i + k) % group) for k in range(1, group)]


def group_order(arrays, place):
    ordered = []
    for slot in range(len(arrays)):
        back = (place - slot) % len(arrays)
        picked = arrays[0]
        for k in range(1, len(arrays)):
            picked = jnp.where(back == k, arrays[k], picked)
        ordered.append(picked)
    return ordered


def group_swaps(rows, group):
    def partner(first):
        return lambda i: i + group if i // group % 2 == first else i - group

    return [strip_permute(rows, partner(0)), rows, strip_permute(rows, partner(1))]


def body(exposures, sky_model, blur_kernels, coverage):
    tile_rows, width = exposures.shape[1:]
    shard_rows = sky_model.shape[0]
    members = lax.axis_size("visit")
    tiles = lax.axis_size("tile")
    group = TAPS // shard_rows
    place = lax.axis_index("visit") % group
    group_row = lax.axis_index("tile") * tile_rows + (lax.axis_index("visit") - place) * shard_rows
    parity = lax.axis_index("visit") // group % 2
    at = jnp.stack([group_row, place, parity]).reshape(1, 3)

    f32, bf16 = jnp.float32, jnp.bfloat16
    shape = jax.ShapeDtypeStruct
    blocks = width // BLOCK
    depth = TAPS * WINDOW

    halo = TAPS // 2
    first, last = exposures[0, :halo], exposures[0, tile_rows - halo :]
    if tiles == 2:
        above = below = lax.ppermute(jnp.where(lax.axis_index("tile") == 0, last, first), "tile", [(0, 1), (1, 0)])
    else:
        above = lax.ppermute(last, "tile", [(i, i + 1) for i in range(tiles - 1)])
        below = lax.ppermute(first, "tile", [(i + 1, i) for i in range(tiles - 1)])
    sent = call(
        functools.partial(send_kernel, group),
        shape((members, 2 * shard_rows + 8, width), f32),
        [pltpu.VMEM((TAPS, LANES), f32)],
        1 << 22,
        *(coverage, exposures, jnp.transpose(blur_kernels, (1, 0, 2)), above, below),
    )
    received = lax.all_to_all(sent, "visit", 0, 0)
    mine = jnp.concatenate(group_order(group_gather(sky_model, group), place), axis=0)
    near = group_swaps(mine, group)
    received, near = lax.optimization_barrier((received, near))
    pairs = group_gather(received, group)

    def blur_scratch(out_rows):
        rows = out_rows + TAPS
        return [
            pltpu.VMEM((rows + TAPS, width), f32),
            pltpu.VMEM((2 * blocks * rows, depth), bf16),
            pltpu.VMEM((blocks * rows, members * BLOCK), f32),
        ]

    def field(out_rows):
        return pltpu.VMEM((2 * blocks * (out_rows + 8), members * 4 * WINDOW), bf16)

    def product(out_rows):
        return pltpu.VMEM((blocks * (out_rows + 8), 8 * BLOCK), f32)

    blur_flops = 6 * blocks * (TAPS + shard_rows) * depth * members * BLOCK
    sum_flops = 6 * blocks * (shard_rows + 8) * members * 4 * WINDOW * 8 * BLOCK
    weight_at = functools.partial(weight_of, tile_rows=tile_rows, tiles=tiles)
    wb_high, wb_low, wc_high, wc_low, blurred, norm = call(
        functools.partial(first_kernel, functools.partial(norm_field, tile_rows=tile_rows, tiles=tiles)),
        (
            shape((members * BLOCK, depth), bf16),
            shape((members * BLOCK, depth), bf16),
            shape((8 * BLOCK, members * 4 * WINDOW), bf16),
            shape((8 * BLOCK, members * 4 * WINDOW), bf16),
            shape((members, 2 * TAPS, width), f32),
            shape((TAPS, width), f32),
        ),
        blur_scratch(TAPS),
        blur_flops + sum_flops,
        *(at, received, *near),
        scalars=1,
    )
    model, data = call(
        functools.partial(second_kernel, weight_at, group),
        (shape((TAPS, width), f32), shape((members, shard_rows + TAPS, width), f32)),
        [field(TAPS), product(TAPS), pltpu.VMEM((2 * TAPS, width), f32)],
        sum_flops,
        *(at, wc_high, wc_low, received, blurred, mine, norm, *pairs),
        scalars=1,
    )
    return call(
        functools.partial(third_kernel, weight_at),
        shape((shard_rows, width), f32),
        [pltpu.VMEM((3 * TAPS, width), f32)]
        + blur_scratch(shard_rows)
        + [field(shard_rows), product(shard_rows)],
        blur_flops + sum_flops,
        *(at, wb_high, wb_low, wc_high, wc_low, received, norm, data, *group_swaps(model, group)),
        scalars=1,
    )


def solution(mesh):
    return jax.shard_map(
        body,
        mesh=mesh,
        in_specs=(
            P("visit", "tile", None),
            P(("tile", "visit"), None),
            P("visit", None, None),
            P("visit", None),
        ),
        out_specs=P(("tile", "visit"), None),
        check_vma=False,
    )
```

```python
import functools

import jax
import jax.numpy as jnp
from jax import lax
from jax.experimental import pallas as pl
from jax.experimental.pallas import tpu as pltpu
from jax.sharding import PartitionSpec as P

LANES = 128
BLOCK = 32
WINDOW = 64
TAPS = 32
MARGIN = WINDOW // 4
CHUNK = 4
VMEM_BYTES = 20 * 1024 * 1024


def split(x):
    high = x.astype(jnp.bfloat16)
    low = (x - high.astype(jnp.float32)).astype(jnp.bfloat16)
    return high, low


def dot_t(x, w):
    return lax.dot_general(x, w, (((1,), (1,)), ((), ())), preferred_element_type=jnp.float32)


def dot_split(both, w_high, w_low):
    rows = both.shape[0] // 2
    wide = dot_t(both[...], w_high)
    return wide[:rows] + (wide[rows:] + dot_t(both[pl.ds(0, rows), :], w_low))


def lane_of(shape):
    return lax.broadcasted_iota(jnp.int32, shape, len(shape) - 1)


def column_windows(parts):
    rows = parts[0].shape[0] - 8
    lane = lane_of((rows, LANES))
    shifts = sorted({(MARGIN - BLOCK * j) % LANES for j in range(LANES // BLOCK)})
    rolled = [{shift: pltpu.roll(part, shift, 1) for shift in shifts} for part in parts]
    windows = []
    for j in range(len(parts) * LANES // BLOCK):
        start = BLOCK * j - MARGIN
        first = start // LANES
        cut = (first + 1) * LANES - start

        def piece(slab):
            if slab < 0 or slab >= len(parts):
                return jnp.zeros((rows, LANES), jnp.float32)
            near = rolled[slab][(-start) % LANES][:rows]
            far = rolled[slab][(WINDOW - start) % LANES][8:]
            return jnp.where(lane < WINDOW, near, far)

        window = piece(first)
        if cut < WINDOW:
            window = jnp.where(lane % WINDOW < cut, window, piece(first + 1))
        windows.append(window)
    return windows


def put_field(member, parts, z_ref, sum_rows):
    windows = column_windows(parts)
    for pair in range(len(windows) // 2):
        for group in range(2):
            rows = [window[16 * group : 16 * group + sum_rows] for window in windows[2 * pair : 2 * pair + 2]]
            high, low = split(jnp.concatenate(rows, axis=0))
            lanes = pl.ds((2 * member + group) * LANES, LANES)
            z_ref[pl.ds(2 * pair * sum_rows, 2 * sum_rows), lanes] = high
            z_ref[pl.ds((2 * pair + len(windows)) * sum_rows, 2 * sum_rows), lanes] = low


def gather_taps(t_ref, out_rows):
    sum_rows = out_rows + 8
    lane = lane_of((out_rows, LANES))
    halves = []
    for half in range(t_ref.shape[0] // sum_rows // 4):
        total = None
        for i in range(4):
            picked = None
            for jj in range(4):
                base = (4 * half + jj) * sum_rows + i
                near = t_ref[pl.ds(base, out_rows), pl.ds(0, LANES)]
                far = t_ref[pl.ds(base + 4, out_rows), pl.ds(LANES, LANES)]
                moved = pltpu.roll(near + far, (BLOCK * (jj - i)) % LANES, 1) if jj != i else near + far
                picked = moved if picked is None else jnp.where(lane >= BLOCK * jj, moved, picked)
            total = picked if total is None else total + picked
        halves.append(total)
    return jnp.concatenate(halves, axis=1)


def lay_model(wide, x_ref, shifts):
    slabs = wide.shape[1] // LANES
    blocks = wide.shape[1] // BLOCK
    half = x_ref.shape[0] // 2
    rows = half // blocks
    for s in shifts:
        parts = [wide[pl.ds(s, rows + 24), pl.ds(LANES * i, LANES)] for i in range(slabs)]
        windows = column_windows(parts)
        for j in range(blocks):
            high, low = split(windows[j])
            for group in range(2):
                lanes = pl.ds((2 * s + group) * LANES, LANES)
                x_ref[pl.ds(rows * j, rows), lanes] = high[16 * group : 16 * group + rows]
                x_ref[pl.ds(half + rows * j, rows), lanes] = low[16 * group : 16 * group + rows]


def blur_all(operator_for, wb_high, wb_low, wide, x_ref, g_ref):
    step = 2 * LANES
    depth = x_ref.shape[1] // 2
    for at in range(0, wb_high.shape[0], step):
        members = pl.ds(at, step)
        operator_for(range(at // BLOCK, (at + step) // BLOCK))
        if at == 0:
            for half in range(2):
                lay_model(wide, x_ref, range(4 * half, 4 * half + 4))
                lanes = pl.ds(depth * half, depth)
                part = dot_split(x_ref.at[:, lanes], wb_high[members, lanes], wb_low[members, lanes])
                g_ref[:, members] = part if half == 0 else g_ref[:, members] + part
        else:
            g_ref[:, members] = dot_split(x_ref, wb_high[members, :], wb_low[members, :])


def blurred_parts(g_ref, member, rows, slabs):
    lane = lane_of((rows, LANES))
    place = member % 4
    parts = []
    for slab in range(slabs):
        picked = None
        for jj in range(4):
            block = g_ref[pl.ds((4 * slab + jj) * rows, rows), pl.ds(member // 4 * LANES, LANES)]
            moved = pltpu.roll(block, (BLOCK * (jj - place)) % LANES, 1) if jj != place else block
            picked = moved if picked is None else jnp.where(lane >= BLOCK * jj, moved, picked)
        parts.append(picked)
    return parts


def table_of(kernel, cover, padded):
    size = kernel.shape[0]
    front = TAPS - size
    padded[...] = jnp.zeros(padded.shape, jnp.float32)
    for row in range(size):
        padded[pl.ds(front + row, 1), pl.ds(front, size)] = kernel[row]
    straight = padded[...]
    straight = straight / jnp.sum(straight)
    row = lax.broadcasted_iota(jnp.int32, (TAPS, TAPS), 0)
    turn_rows = (row + lane_of((TAPS, TAPS)) == TAPS).astype(jnp.float32)
    row = lax.broadcasted_iota(jnp.int32, (LANES, LANES), 0)
    turn_lanes = (row + lane_of((LANES, LANES)) == TAPS).astype(jnp.float32)
    exact = functools.partial(jnp.dot, precision=lax.Precision.HIGHEST, preferred_element_type=jnp.float32)
    flipped = exact(exact(turn_rows, straight), turn_lanes)
    both = straight + pltpu.roll(flipped, TAPS, 1)
    half = [both[8 * i : 8 * i + 8] for i in range(4)]
    groups = [half[2 * i] + pltpu.roll(half[2 * i + 1], WINDOW, 1) for i in range(2)]
    row = lax.broadcasted_iota(jnp.int32, groups[0].shape, 0)
    lane = lane_of(groups[0].shape)
    for tile in range(cover.shape[1]):
        spot = (row == tile % 8) & (lane == 0)
        entry = jnp.broadcast_to(cover[0:1, tile : tile + 1].astype(jnp.float32), spot.shape)
        groups[tile // 8] = jnp.where(spot, entry, groups[tile // 8])
    return groups


def send_kernel(cover, counts, kernels, out, padded):
    groups = table_of(kernels, cover, padded)
    own = out.shape[1] - 8
    for peer in range(out.shape[0]):
        out[peer, pl.ds(0, own), :] = counts[0, pl.ds(peer * own, own), :]
        for half in range(2):
            out[peer, pl.ds(own, 8), pl.ds(LANES * half, LANES)] = groups[half]


def weight_of(member, first_row, tile_rows, tiles, received, rows):
    own = received.shape[1] - 8
    row = first_row - TAPS // 2 + lax.broadcasted_iota(jnp.int32, (rows, LANES), 0)
    weight = jnp.zeros((rows, LANES), jnp.float32)
    for tile in range(tiles):
        entry = received[member, pl.ds(own + tile % 8, 1), pl.ds(tile // 8 * LANES, LANES)]
        inside = (row >= tile * tile_rows) & (row < (tile + 1) * tile_rows)
        weight = jnp.where(inside, jnp.broadcast_to(entry[:, 0:1], (rows, LANES)), weight)
    return weight


def update(blurred_of, weight_at, counts_of, model, norm, wc_high, wc_low, z_ref, t_ref, out):
    out_rows = out.shape[0]
    members = z_ref.shape[1] // (4 * WINDOW)
    for first in range(0, members, CHUNK):
        for member in range(first, first + CHUNK):
            weight = weight_at(member)
            parts = []
            for blurred, counts in zip(blurred_of(member), counts_of(member)):
                safe = jnp.where(weight > 0.0, blurred, 1.0)
                parts.append(weight * counts / safe)
            put_field(member, parts, z_ref, out_rows + 8)
        lanes = pl.ds(4 * WINDOW * first, 4 * WINDOW * CHUNK)
        part = dot_split(z_ref.at[:, lanes], wc_high[:, lanes], wc_low[:, lanes])
        t_ref[...] = part if first == 0 else t_ref[...] + part
    out[...] = model * gather_taps(t_ref, out_rows) / norm


def norm_field(first_row, tile_rows, tiles, received, norm):
    out_rows, width = norm.shape
    members = received.shape[0]
    table_row = received.shape[1] - 8
    tables = [
        received[:, pl.ds(table_row, 8), pl.ds(LANES * group, LANES)].reshape(8 * members, LANES) for group in range(2)
    ]
    entry = lax.broadcasted_iota(jnp.int32, (8 * members, 8 * members), 0)
    lane = lane_of((8 * members, 8 * members))
    covers = []
    for tile in range(tiles):
        column = jnp.broadcast_to(tables[tile // 8][:, 0:1], entry.shape)
        spot = entry == lane // 8 * 8 + tile % 8
        covers.append(jnp.sum(jnp.where(spot, column, 0.0), axis=0, keepdims=True))
    row = lax.broadcasted_iota(jnp.int32, (out_rows, 8 * members), 0) + lane_of((out_rows, 8 * members)) % 8
    total = None
    for index in range(4):
        group, half = divmod(index, 2)
        offset = lax.broadcasted_iota(jnp.int32, (LANES, width), 0) - WINDOW * half
        column = lane_of((LANES, width)) + offset - TAPS // 2
        inside = (offset >= 1) & (offset < TAPS) & (column >= 0) & (column < width)
        inside = inside.astype(jnp.bfloat16)
        high, low = split(tables[group])
        sums = jnp.dot(high, inside, preferred_element_type=jnp.float32)
        sums = sums + jnp.dot(low, inside, preferred_element_type=jnp.float32)
        place = row + (first_row - TAPS // 2 + 8 * index)
        weight = jnp.zeros(place.shape, jnp.float32)
        for tile in range(tiles):
            covered = (place >= tile * tile_rows) & (place < (tile + 1) * tile_rows)
            weight = jnp.where(covered, jnp.broadcast_to(covers[tile], place.shape), weight)
        weight = weight.astype(jnp.bfloat16)
        high, low = split(sums)
        part = jnp.dot(weight, high, preferred_element_type=jnp.float32)
        part = part + jnp.dot(weight, low, preferred_element_type=jnp.float32)
        total = part if total is None else total + part
    norm[...] = total


def put_model(refs, at, tall, wide):
    even_swap, own, odd_swap = refs
    rows = own.shape[0]
    tall[pl.ds(rows, rows), :] = own[...]
    tall[pl.ds(pl.multiple_of(2 * rows * (1 - at[0, 2]), rows), rows), :] = even_swap[...]
    tall[pl.ds(pl.multiple_of(2 * rows * at[0, 2], rows), rows), :] = odd_swap[...]
    wide[...] = tall[pl.ds(pl.multiple_of(at[0, 1], 8), wide.shape[0]), :]


def counts_window(at, received, swaps, rows):
    def window(member):
        parts = []
        for first in range(0, received.shape[2], LANES):
            slab = pl.ds(first, LANES)
            own = received[member, pl.ds(0, rows), slab]
            before, after = [], []
            for hop in range(len(swaps) // 2):
                even, odd = (ref[member, :, slab] for ref in swaps[2 * hop : 2 * hop + 2])
                is_even = at[0, 3 + hop] == 0
                before.insert(0, jnp.where(is_even, odd, even))
                after.append(jnp.where(is_even, even, odd))
            parts.append(jnp.concatenate(before + [own] + after, axis=0))
        return parts

    return window


def first_kernel(
    norm_at, at, received, even_swap, own, odd_swap, wb_high, wb_low, wc_high, wc_low, blurred, norm, tall, wide, x_ref, g_ref
):
    members, rows, width = blurred.shape
    table_row = received.shape[1] - 8
    lane = lane_of((8, LANES)) % WINDOW
    used = (lane >= 1) & (lane < TAPS)

    def entry_of(member, group):
        return received[member, pl.ds(table_row, 8), pl.ds(LANES * group, LANES)]

    def band_of(base, s):
        band = jnp.broadcast_to(base[s : s + 1], (BLOCK, LANES))
        return split(pltpu.roll(band, 0, 1, stride=1, stride_axis=0))

    def blur_operator(chosen):
        for member in chosen:
            for group in range(2):
                flipped = jnp.where(used, pltpu.roll(entry_of(member, group), LANES - TAPS, 1), 0.0)
                for s in range(8):
                    spot = (pl.ds(BLOCK * member, BLOCK), pl.ds(LANES * (2 * s + group), LANES))
                    wb_high[spot], wb_low[spot] = band_of(flipped, s)

    put_model((even_swap, own, odd_swap), at, tall, wide)
    blur_all(blur_operator, wb_high, wb_low, wide, x_ref, g_ref)
    for member in range(members):
        for group in range(2):
            straight = jnp.where(used, entry_of(member, group), 0.0)
            for s in range(8):
                spot = (pl.ds(BLOCK * s, BLOCK), pl.ds((2 * member + group) * LANES, LANES))
                wc_high[spot], wc_low[spot] = band_of(straight, s)
    for member in range(members):
        for slab, part in enumerate(blurred_parts(g_ref, member, rows, width // LANES)):
            blurred[member, :, pl.ds(LANES * slab, LANES)] = part
    norm_at(at[0, 0], received=received, norm=norm)


def second_kernel(weight_at, at, wc_high, wc_low, received, blurred, model, norm, *refs):
    swaps, (out, z_ref, t_ref) = refs[:-3], refs[-3:]
    out_rows, width = out.shape

    def blurred_of(member):
        return [blurred[member, :, pl.ds(first, LANES)] for first in range(0, width, LANES)]

    counts_of = counts_window(at, received, swaps, out_rows)
    weight_of_shard = functools.partial(weight_at, first_row=at[0, 0], received=received, rows=out_rows + TAPS)
    update(blurred_of, weight_of_shard, counts_of, model[...], norm[...], wc_high, wc_low, z_ref, t_ref, out)


def third_kernel(weight_at, at, wb_high, wb_low, wc_high, wc_low, received, model, norm, even_swap, own, odd_swap, *refs):
    swaps, (out, tall, wide, x_ref, g_ref, z_ref, t_ref) = refs[:-7], refs[-7:]
    out_rows, width = out.shape
    rows = out_rows + TAPS
    put_model((even_swap, own, odd_swap), at, tall, wide)
    blur_all(lambda chosen: None, wb_high, wb_low, wide, x_ref, g_ref)
    blurred_of = functools.partial(blurred_parts, g_ref, rows=rows, slabs=width // LANES)
    counts_of = counts_window(at, received, swaps, out_rows)
    weight_of_shard = functools.partial(weight_at, first_row=at[0, 0], received=received, rows=rows)
    update(blurred_of, weight_of_shard, counts_of, model[...], norm[...], wc_high, wc_low, z_ref, t_ref, out)


def call(kernel, out_shape, scratch_shapes, flops, *operands, scalars=0):
    whole = pl.BlockSpec(memory_space=pltpu.VMEM)
    scalar = pl.BlockSpec(memory_space=pltpu.SMEM)
    return pl.pallas_call(
        kernel,
        out_shape=out_shape,
        in_specs=[scalar] * scalars + [whole] * (len(operands) - scalars),
        out_specs=jax.tree.map(lambda _: whole, out_shape),
        scratch_shapes=scratch_shapes,
        compiler_params=pltpu.CompilerParams(vmem_limit_bytes=VMEM_BYTES),
        cost_estimate=pl.CostEstimate(flops=flops, bytes_accessed=4 * 1024 * 1024, transcendentals=0),
    )(*operands)


def strip_permute(array, target):
    tiles, members = lax.axis_size("tile"), lax.axis_size("visit")
    count = tiles * members
    place = [i % members * tiles + i // members for i in range(count)]
    pairs = [(place[i], place[target(i)]) for i in range(count) if 0 <= target(i) < count]
    return lax.ppermute(array, ("visit", "tile"), pairs)


def group_gather(array, group):
    return [array] + [strip_permute(array, lambda i: i // group * group + (i + k) % group) for k in range(1, group)]


def group_order(arrays, place):
    ordered = []
    for slot in range(len(arrays)):
        back = (place - slot) % len(arrays)
        picked = arrays[0]
        for k in range(1, len(arrays)):
            picked = jnp.where(back == k, arrays[k], picked)
        ordered.append(picked)
    return ordered


def group_swaps(rows, group):
    def partner(first):
        return lambda i: i + group if i // group % 2 == first else i - group

    return [strip_permute(rows, partner(0)), rows, strip_permute(rows, partner(1))]


def body(exposures, sky_model, blur_kernels, coverage):
    tile_rows, width = exposures.shape[1:]
    shard_rows = sky_model.shape[0]
    members = lax.axis_size("visit")
    tiles = lax.axis_size("tile")
    visit = lax.axis_index("visit")
    group = TAPS // shard_rows
    place = visit % group
    hops = TAPS // 2 // shard_rows
    first_row = lax.axis_index("tile") * tile_rows + visit * shard_rows
    parities = [visit // hop % 2 for hop in [group, *range(1, hops + 1)]]
    at = jnp.stack([first_row, place * shard_rows, *parities]).reshape(1, -1)

    f32, bf16 = jnp.float32, jnp.bfloat16
    shape = jax.ShapeDtypeStruct
    blocks = width // BLOCK
    depth = TAPS * WINDOW
    rows = shard_rows + TAPS

    def halo_of(model):
        mine = jnp.concatenate(group_order(group_gather(model, group), place), axis=0)
        return group_swaps(mine, group)

    sent = call(
        send_kernel,
        shape((members, shard_rows + 8, width), f32),
        [pltpu.VMEM((TAPS, LANES), f32)],
        1 << 22,
        *(coverage, exposures, jnp.transpose(blur_kernels, (1, 0, 2))),
    )
    received = lax.all_to_all(sent, "visit", 0, 0)
    received, near = lax.optimization_barrier((received, halo_of(sky_model)))
    swaps = []
    for hop in range(1, hops + 1):
        even, _, odd = group_swaps(received[:, :shard_rows], hop)
        swaps += [even, odd]

    blur_scratch = [
        pltpu.VMEM((3 * TAPS, width), f32),
        pltpu.VMEM((rows + TAPS, width), f32),
        pltpu.VMEM((2 * blocks * rows, depth), bf16),
        pltpu.VMEM((blocks * rows, members * BLOCK), f32),
    ]
    sum_scratch = [
        pltpu.VMEM((2 * blocks * (shard_rows + 8), members * 4 * WINDOW), bf16),
        pltpu.VMEM((blocks * (shard_rows + 8), 8 * BLOCK), f32),
    ]
    blur_flops = 6 * blocks * rows * depth * members * BLOCK
    sum_flops = 6 * blocks * (shard_rows + 8) * members * 4 * WINDOW * 8 * BLOCK
    weight_at = functools.partial(weight_of, tile_rows=tile_rows, tiles=tiles)
    wb_high, wb_low, wc_high, wc_low, blurred, norm = call(
        functools.partial(first_kernel, functools.partial(norm_field, tile_rows=tile_rows, tiles=tiles)),
        (
            shape((members * BLOCK, depth), bf16),
            shape((members * BLOCK, depth), bf16),
            shape((8 * BLOCK, members * 4 * WINDOW), bf16),
            shape((8 * BLOCK, members * 4 * WINDOW), bf16),
            shape((members, rows, width), f32),
            shape((shard_rows, width), f32),
        ),
        blur_scratch,
        blur_flops + sum_flops,
        *(at, received, *near),
        scalars=1,
    )
    model = call(
        functools.partial(second_kernel, weight_at),
        shape((shard_rows, width), f32),
        sum_scratch,
        sum_flops,
        *(at, wc_high, wc_low, received, blurred, sky_model, norm, *swaps),
        scalars=1,
    )
    return call(
        functools.partial(third_kernel, weight_at),
        shape((shard_rows, width), f32),
        blur_scratch + sum_scratch,
        blur_flops + sum_flops,
        *(at, wb_high, wb_low, wc_high, wc_low, received, model, norm, *halo_of(model), *swaps),
        scalars=1,
    )


def solution(mesh):
    return jax.shard_map(
        body,
        mesh=mesh,
        in_specs=(
            P("visit", "tile", None),
            P(("tile", "visit"), None),
            P("visit", None, None),
            P("visit", None),
        ),
        out_specs=P(("tile", "visit"), None),
        check_vma=False,
    )
```

```python
import functools

import jax
import jax.numpy as jnp
from jax import lax
from jax.experimental import pallas as pl
from jax.experimental.pallas import tpu as pltpu
from jax.sharding import PartitionSpec as P

LANES = 128
BLOCK = 32
WINDOW = 64
TAPS = 32
MARGIN = WINDOW // 4
CHUNK = 4
VMEM_BYTES = 20 * 1024 * 1024


def split(x):
    high = x.astype(jnp.bfloat16)
    low = (x - high.astype(jnp.float32)).astype(jnp.bfloat16)
    return high, low


def dot_t(x, w):
    return lax.dot_general(x, w, (((1,), (1,)), ((), ())), preferred_element_type=jnp.float32)


def dot_split(both, w_high, w_low):
    rows = both.shape[0] // 2
    wide = dot_t(both[...], w_high)
    return wide[:rows] + (wide[rows:] + dot_t(both[pl.ds(0, rows), :], w_low))


def lane_of(shape):
    return lax.broadcasted_iota(jnp.int32, shape, len(shape) - 1)


def column_windows(parts):
    rows = parts[0].shape[0] - 8
    lane = lane_of((rows, LANES))
    shifts = sorted({(MARGIN - BLOCK * j) % LANES for j in range(LANES // BLOCK)})
    rolled = [{shift: pltpu.roll(part, shift, 1) for shift in shifts} for part in parts]
    windows = []
    for j in range(len(parts) * LANES // BLOCK):
        start = BLOCK * j - MARGIN
        first = start // LANES
        cut = (first + 1) * LANES - start

        def piece(slab):
            if slab < 0 or slab >= len(parts):
                return jnp.zeros((rows, LANES), jnp.float32)
            near = rolled[slab][(-start) % LANES][:rows]
            far = rolled[slab][(WINDOW - start) % LANES][8:]
            return jnp.where(lane < WINDOW, near, far)

        window = piece(first)
        if cut < WINDOW:
            window = jnp.where(lane % WINDOW < cut, window, piece(first + 1))
        windows.append(window)
    return windows


def put_field(member, parts, z_ref, sum_rows):
    windows = column_windows(parts)
    for pair in range(len(windows) // 2):
        for group in range(2):
            rows = [window[16 * group : 16 * group + sum_rows] for window in windows[2 * pair : 2 * pair + 2]]
            high, low = split(jnp.concatenate(rows, axis=0))
            lanes = pl.ds((2 * member + group) * LANES, LANES)
            z_ref[pl.ds(2 * pair * sum_rows, 2 * sum_rows), lanes] = high
            z_ref[pl.ds((2 * pair + len(windows)) * sum_rows, 2 * sum_rows), lanes] = low


def gather_taps(t_ref, out_rows):
    sum_rows = out_rows + 8
    lane = lane_of((out_rows, LANES))
    halves = []
    for half in range(t_ref.shape[0] // sum_rows // 4):
        total = None
        for i in range(4):
            picked = None
            for jj in range(4):
                base = (4 * half + jj) * sum_rows + i
                near = t_ref[pl.ds(base, out_rows), pl.ds(0, LANES)]
                far = t_ref[pl.ds(base + 4, out_rows), pl.ds(LANES, LANES)]
                moved = pltpu.roll(near + far, (BLOCK * (jj - i)) % LANES, 1) if jj != i else near + far
                picked = moved if picked is None else jnp.where(lane >= BLOCK * jj, moved, picked)
            total = picked if total is None else total + picked
        halves.append(total)
    return jnp.concatenate(halves, axis=1)


def lay_model(wide, x_ref, shifts):
    slabs = wide.shape[1] // LANES
    blocks = wide.shape[1] // BLOCK
    half = x_ref.shape[0] // 2
    rows = half // blocks
    for s in shifts:
        parts = [wide[pl.ds(s, rows + 24), pl.ds(LANES * i, LANES)] for i in range(slabs)]
        windows = column_windows(parts)
        for j in range(blocks):
            high, low = split(windows[j])
            for group in range(2):
                lanes = pl.ds((2 * s + group) * LANES, LANES)
                x_ref[pl.ds(rows * j, rows), lanes] = high[16 * group : 16 * group + rows]
                x_ref[pl.ds(half + rows * j, rows), lanes] = low[16 * group : 16 * group + rows]


def blur_all(operator_for, wb_high, wb_low, wide, x_ref, g_ref):
    step = 2 * LANES
    depth = x_ref.shape[1] // 2
    for at in range(0, wb_high.shape[0], step):
        members = pl.ds(at, step)
        operator_for(range(at // BLOCK, (at + step) // BLOCK))
        if at == 0:
            for half in range(2):
                lay_model(wide, x_ref, range(4 * half, 4 * half + 4))
                lanes = pl.ds(depth * half, depth)
                part = dot_split(x_ref.at[:, lanes], wb_high[members, lanes], wb_low[members, lanes])
                g_ref[:, members] = part if half == 0 else g_ref[:, members] + part
        else:
            g_ref[:, members] = dot_split(x_ref, wb_high[members, :], wb_low[members, :])


def blurred_parts(g_ref, member, rows, slabs):
    lane = lane_of((rows, LANES))
    place = member % 4
    parts = []
    for slab in range(slabs):
        picked = None
        for jj in range(4):
            block = g_ref[pl.ds((4 * slab + jj) * rows, rows), pl.ds(member // 4 * LANES, LANES)]
            moved = pltpu.roll(block, (BLOCK * (jj - place)) % LANES, 1) if jj != place else block
            picked = moved if picked is None else jnp.where(lane >= BLOCK * jj, moved, picked)
        parts.append(picked)
    return parts


def send_kernel(cover, kernel, counts, out, padded):
    size = kernel.shape[0]
    front = TAPS - size
    padded[...] = jnp.zeros(padded.shape, jnp.float32)
    for row in range(size):
        padded[pl.ds(front + row, 1), pl.ds(front, size)] = kernel[row]
    straight = padded[...]
    straight = straight / jnp.sum(straight)
    table = straight[0:8]
    for q in range(1, TAPS // 8):
        table = table + pltpu.roll(straight[8 * q : 8 * q + 8], TAPS * q, 1)
    row = lax.broadcasted_iota(jnp.int32, table.shape, 0)
    lane = lane_of(table.shape)
    for tile in range(cover.shape[1]):
        spot = (row == tile % 8) & (lane == tile // 8 * TAPS)
        entry = jnp.broadcast_to(cover[0:1, tile : tile + 1].astype(jnp.float32), table.shape)
        table = jnp.where(spot, entry, table)
    slabs = counts.shape[2] // LANES
    own = (out.shape[1] - 8) // slabs
    for peer in range(out.shape[0]):
        for slab in range(slabs):
            out[peer, pl.ds(slab * own, own), :] = counts[0, pl.ds(peer * own, own), pl.ds(slab * LANES, LANES)]
        out[peer, pl.ds(slabs * own, 8), :] = table


def weight_of(member, first_row, tile_rows, tiles, received, rows):
    table_row = received.shape[1] - 8
    row = first_row - TAPS // 2 + lax.broadcasted_iota(jnp.int32, (rows, LANES), 0)
    weight = jnp.zeros((rows, LANES), jnp.float32)
    for tile in range(tiles):
        entry = received[member, pl.ds(table_row + tile % 8, 1), :]
        inside = (row >= tile * tile_rows) & (row < (tile + 1) * tile_rows)
        weight = jnp.where(inside, jnp.broadcast_to(entry[:, tile // 8 * TAPS :][:, 0:1], (rows, LANES)), weight)
    return weight


def update(blurred_of, weight_at, counts_of, model, norm, wc_high, wc_low, z_ref, t_ref, out):
    out_rows = out.shape[0]
    members = z_ref.shape[1] // (4 * WINDOW)
    for first in range(0, members, CHUNK):
        for member in range(first, first + CHUNK):
            weight = weight_at(member)
            parts = []
            for blurred, counts in zip(blurred_of(member), counts_of(member)):
                safe = jnp.where(weight > 0.0, blurred, 1.0)
                parts.append(weight * counts / safe)
            put_field(member, parts, z_ref, out_rows + 8)
        lanes = pl.ds(4 * WINDOW * first, 4 * WINDOW * CHUNK)
        part = dot_split(z_ref.at[:, lanes], wc_high[:, lanes], wc_low[:, lanes])
        t_ref[...] = part if first == 0 else t_ref[...] + part
    out[...] = model * gather_taps(t_ref, out_rows) / norm


def norm_field(first_row, tile_rows, tiles, received, norm):
    out_rows, width = norm.shape
    members = received.shape[0]
    table_row = received.shape[1] - 8
    table = received[:, pl.ds(table_row, 8), :].reshape(8 * members, LANES)
    entry = lax.broadcasted_iota(jnp.int32, (8 * members, 8 * members), 0)
    lane = lane_of((8 * members, 8 * members))
    covers = []
    for tile in range(tiles):
        column = jnp.broadcast_to(table[:, tile // 8 * TAPS :][:, 0:1], entry.shape)
        spot = entry == lane // 8 * 8 + tile % 8
        covers.append(jnp.sum(jnp.where(spot, column, 0.0), axis=0, keepdims=True))
    row = lax.broadcasted_iota(jnp.int32, (out_rows, 8 * members), 0) + lane_of((out_rows, 8 * members)) % 8
    total = None
    for index in range(4):
        offset = lax.broadcasted_iota(jnp.int32, (LANES, width), 0) - TAPS * index
        column = lane_of((LANES, width)) + offset - TAPS // 2
        inside = (offset >= 1) & (offset < TAPS) & (column >= 0) & (column < width)
        inside = inside.astype(jnp.bfloat16)
        high, low = split(table)
        sums = jnp.dot(high, inside, preferred_element_type=jnp.float32)
        sums = sums + jnp.dot(low, inside, preferred_element_type=jnp.float32)
        place = row + (first_row - TAPS // 2 + 8 * index)
        weight = jnp.zeros(place.shape, jnp.float32)
        for tile in range(tiles):
            covered = (place >= tile * tile_rows) & (place < (tile + 1) * tile_rows)
            weight = jnp.where(covered, jnp.broadcast_to(covers[tile], place.shape), weight)
        weight = weight.astype(jnp.bfloat16)
        high, low = split(sums)
        part = jnp.dot(weight, high, preferred_element_type=jnp.float32)
        part = part + jnp.dot(weight, low, preferred_element_type=jnp.float32)
        total = part if total is None else total + part
    norm[...] = total


def put_model(refs, at, tall, wide):
    even_swap, own, odd_swap = refs
    rows = own.shape[0]
    tall[pl.ds(rows, rows), :] = own[...]
    tall[pl.ds(pl.multiple_of(2 * rows * (1 - at[0, 2]), rows), rows), :] = even_swap[...]
    tall[pl.ds(pl.multiple_of(2 * rows * at[0, 2], rows), rows), :] = odd_swap[...]
    wide[...] = tall[pl.ds(pl.multiple_of(at[0, 1], 8), wide.shape[0]), :]


def counts_window(at, received, swaps, rows):
    def window(member):
        parts = []
        for first in range(0, received.shape[1] - 8, rows):
            slab = pl.ds(first, rows)
            own = received[member, slab, :]
            before, after = [], []
            for hop in range(len(swaps) // 2):
                even, odd = (ref[member, slab, :] for ref in swaps[2 * hop : 2 * hop + 2])
                is_even = at[0, 3 + hop] == 0
                before.insert(0, jnp.where(is_even, odd, even))
                after.append(jnp.where(is_even, even, odd))
            parts.append(jnp.concatenate(before + [own] + after, axis=0))
        return parts

    return window


def first_kernel(
    norm_at, at, received, even_swap, own, odd_swap, wb_high, wb_low, wc_high, wc_low, blurred, norm, tall, wide, x_ref, g_ref
):
    members, rows, width = blurred.shape
    table_row = received.shape[1] - 8
    table = received[:, pl.ds(table_row, 8), :].reshape(8 * members, LANES)
    source = lax.broadcasted_iota(jnp.int32, (LANES, LANES), 0)
    target = lane_of((LANES, LANES))
    tap = target % WINDOW
    used = (tap >= 1) & (tap < TAPS)
    mirrored = []
    for group in range(2):
        slot = 2 * group + target // WINDOW
        for last in (4, 3):
            pick = used & (source == TAPS * (last - slot) + TAPS - tap)
            mirrored.append(
                jnp.dot(table, pick.astype(jnp.float32), precision=lax.Precision.HIGHEST, preferred_element_type=jnp.float32)
            )
    lane = lane_of((8, LANES))
    used = (lane % WINDOW >= 1) & (lane % WINDOW < TAPS)

    def band_of(base, s):
        band = jnp.broadcast_to(base[s : s + 1], (BLOCK, LANES))
        return split(pltpu.roll(band, 0, 1, stride=1, stride_axis=0))

    def blur_operator(chosen):
        for member in chosen:
            for group in range(2):
                for s in range(8):
                    spot = (pl.ds(BLOCK * member, BLOCK), pl.ds(LANES * (2 * s + group), LANES))
                    base = mirrored[2 * group + (s > 0)]
                    wb_high[spot], wb_low[spot] = band_of(base, 8 * member + (8 - s) % 8)

    put_model((even_swap, own, odd_swap), at, tall, wide)
    blur_all(blur_operator, wb_high, wb_low, wide, x_ref, g_ref)
    for member in range(members):
        for group in range(2):
            entry = table[8 * member : 8 * member + 8]
            near = pltpu.roll(entry, WINDOW, 1) if group else entry
            straight = jnp.where(used, jnp.where(lane < WINDOW, near, pltpu.roll(near, TAPS, 1)), 0.0)
            for s in range(8):
                spot = (pl.ds(BLOCK * s, BLOCK), pl.ds((2 * member + group) * LANES, LANES))
                wc_high[spot], wc_low[spot] = band_of(straight, s)
    for member in range(members):
        for slab, part in enumerate(blurred_parts(g_ref, member, rows, width // LANES)):
            blurred[member, :, pl.ds(LANES * slab, LANES)] = part
    norm_at(at[0, 0], received=received, norm=norm)


def second_kernel(weight_at, at, wc_high, wc_low, received, blurred, model, norm, *refs):
    swaps, (out, z_ref, t_ref) = refs[:-3], refs[-3:]
    out_rows, width = out.shape

    def blurred_of(member):
        return [blurred[member, :, pl.ds(first, LANES)] for first in range(0, width, LANES)]

    counts_of = counts_window(at, received, swaps, out_rows)
    weight_of_shard = functools.partial(weight_at, first_row=at[0, 0], received=received, rows=out_rows + TAPS)
    update(blurred_of, weight_of_shard, counts_of, model[...], norm[...], wc_high, wc_low, z_ref, t_ref, out)


def third_kernel(weight_at, at, wb_high, wb_low, wc_high, wc_low, received, model, norm, even_swap, own, odd_swap, *refs):
    swaps, (out, tall, wide, x_ref, g_ref, z_ref, t_ref) = refs[:-7], refs[-7:]
    out_rows, width = out.shape
    rows = out_rows + TAPS
    put_model((even_swap, own, odd_swap), at, tall, wide)
    blur_all(lambda chosen: None, wb_high, wb_low, wide, x_ref, g_ref)
    blurred_of = functools.partial(blurred_parts, g_ref, rows=rows, slabs=width // LANES)
    counts_of = counts_window(at, received, swaps, out_rows)
    weight_of_shard = functools.partial(weight_at, first_row=at[0, 0], received=received, rows=rows)
    update(blurred_of, weight_of_shard, counts_of, model[...], norm[...], wc_high, wc_low, z_ref, t_ref, out)


def call(kernel, out_shape, scratch_shapes, flops, *operands, scalars=0):
    whole = pl.BlockSpec(memory_space=pltpu.VMEM)
    scalar = pl.BlockSpec(memory_space=pltpu.SMEM)
    return pl.pallas_call(
        kernel,
        out_shape=out_shape,
        in_specs=[scalar] * scalars + [whole] * (len(operands) - scalars),
        out_specs=jax.tree.map(lambda _: whole, out_shape),
        scratch_shapes=scratch_shapes,
        compiler_params=pltpu.CompilerParams(vmem_limit_bytes=VMEM_BYTES),
        cost_estimate=pl.CostEstimate(flops=flops, bytes_accessed=4 * 1024 * 1024, transcendentals=0),
    )(*operands)


def strip_permute(array, target):
    tiles, members = lax.axis_size("tile"), lax.axis_size("visit")
    count = tiles * members
    place = [i % members * tiles + i // members for i in range(count)]
    pairs = [(place[i], place[target(i)]) for i in range(count) if 0 <= target(i) < count]
    return lax.ppermute(array, ("visit", "tile"), pairs)


def group_gather(array, group):
    return [array] + [strip_permute(array, lambda i: i // group * group + (i + k) % group) for k in range(1, group)]


def group_order(arrays, place):
    ordered = []
    for slot in range(len(arrays)):
        back = (place - slot) % len(arrays)
        picked = arrays[0]
        for k in range(1, len(arrays)):
            picked = jnp.where(back == k, arrays[k], picked)
        ordered.append(picked)
    return ordered


def group_swaps(rows, group):
    def partner(first):
        return lambda i: i + group if i // group % 2 == first else i - group

    return [strip_permute(rows, partner(0)), rows, strip_permute(rows, partner(1))]


def body(exposures, sky_model, blur_kernels, coverage):
    tile_rows, width = exposures.shape[1:]
    shard_rows = sky_model.shape[0]
    members = lax.axis_size("visit")
    tiles = lax.axis_size("tile")
    visit = lax.axis_index("visit")
    group = TAPS // shard_rows
    place = visit % group
    hops = TAPS // 2 // shard_rows
    first_row = lax.axis_index("tile") * tile_rows + visit * shard_rows
    parities = [visit // hop % 2 for hop in [group, *range(1, hops + 1)]]
    at = jnp.stack([first_row, place * shard_rows, *parities]).reshape(1, -1)

    f32, bf16 = jnp.float32, jnp.bfloat16
    shape = jax.ShapeDtypeStruct
    blocks = width // BLOCK
    depth = TAPS * WINDOW
    rows = shard_rows + TAPS

    def halo_of(model):
        mine = jnp.concatenate(group_order(group_gather(model, group), place), axis=0)
        return group_swaps(mine, group)

    sent = call(
        send_kernel,
        shape((members, width // LANES * shard_rows + 8, LANES), f32),
        [pltpu.VMEM((TAPS, LANES), f32)],
        1 << 22,
        *(coverage, jnp.transpose(blur_kernels, (1, 0, 2)), exposures),
    )
    received = lax.all_to_all(sent, "visit", 0, 0)
    received, near = lax.optimization_barrier((received, halo_of(sky_model)))
    swaps = []
    for hop in range(1, hops + 1):
        even, _, odd = group_swaps(received[:, : width // LANES * shard_rows], hop)
        swaps += [even, odd]

    blur_scratch = [
        pltpu.VMEM((3 * TAPS, width), f32),
        pltpu.VMEM((rows + TAPS, width), f32),
        pltpu.VMEM((2 * blocks * rows, depth), bf16),
        pltpu.VMEM((blocks * rows, members * BLOCK), f32),
    ]
    sum_scratch = [
        pltpu.VMEM((2 * blocks * (shard_rows + 8), members * 4 * WINDOW), bf16),
        pltpu.VMEM((blocks * (shard_rows + 8), 8 * BLOCK), f32),
    ]
    blur_flops = 6 * blocks * rows * depth * members * BLOCK
    sum_flops = 6 * blocks * (shard_rows + 8) * members * 4 * WINDOW * 8 * BLOCK
    weight_at = functools.partial(weight_of, tile_rows=tile_rows, tiles=tiles)
    wb_high, wb_low, wc_high, wc_low, blurred, norm = call(
        functools.partial(first_kernel, functools.partial(norm_field, tile_rows=tile_rows, tiles=tiles)),
        (
            shape((members * BLOCK, depth), bf16),
            shape((members * BLOCK, depth), bf16),
            shape((8 * BLOCK, members * 4 * WINDOW), bf16),
            shape((8 * BLOCK, members * 4 * WINDOW), bf16),
            shape((members, rows, width), f32),
            shape((shard_rows, width), f32),
        ),
        blur_scratch,
        blur_flops + sum_flops,
        *(at, received, *near),
        scalars=1,
    )
    model = call(
        functools.partial(second_kernel, weight_at),
        shape((shard_rows, width), f32),
        sum_scratch,
        sum_flops,
        *(at, wc_high, wc_low, received, blurred, sky_model, norm, *swaps),
        scalars=1,
    )
    return call(
        functools.partial(third_kernel, weight_at),
        shape((shard_rows, width), f32),
        blur_scratch + sum_scratch,
        blur_flops + sum_flops,
        *(at, wb_high, wb_low, wc_high, wc_low, received, model, norm, *halo_of(model), *swaps),
        scalars=1,
    )


def solution(mesh):
    return jax.shard_map(
        body,
        mesh=mesh,
        in_specs=(
            P("visit", "tile", None),
            P(("tile", "visit"), None),
            P("visit", None, None),
            P("visit", None),
        ),
        out_specs=P(("tile", "visit"), None),
        check_vma=False,
    )
```

```python
import functools

import jax
import jax.numpy as jnp
from jax import lax
from jax.experimental import pallas as pl
from jax.experimental.pallas import tpu as pltpu
from jax.sharding import PartitionSpec as P

LANES = 128
BLOCK = 32
WINDOW = 64
TAPS = 32
MARGIN = WINDOW // 4
CHUNK = 4
VMEM_BYTES = 20 * 1024 * 1024


def split(x):
    high = x.astype(jnp.bfloat16)
    low = (x - high.astype(jnp.float32)).astype(jnp.bfloat16)
    return high, low


def dot_t(x, w):
    return lax.dot_general(x, w, (((1,), (1,)), ((), ())), preferred_element_type=jnp.float32)


def dot_split(both, w_high, w_low):
    rows = both.shape[0] // 2
    wide = dot_t(both[...], w_high)
    return wide[:rows] + (wide[rows:] + dot_t(both[pl.ds(0, rows), :], w_low))


def lane_of(shape):
    return lax.broadcasted_iota(jnp.int32, shape, len(shape) - 1)


def column_windows(parts):
    rows = parts[0].shape[0] - 8
    lane = lane_of((rows, LANES))
    shifts = sorted({(MARGIN - BLOCK * j) % LANES for j in range(LANES // BLOCK)})
    rolled = [{shift: pltpu.roll(part, shift, 1) for shift in shifts} for part in parts]
    windows = []
    for j in range(len(parts) * LANES // BLOCK):
        start = BLOCK * j - MARGIN
        first = start // LANES
        cut = (first + 1) * LANES - start

        def piece(slab):
            if slab < 0 or slab >= len(parts):
                return jnp.zeros((rows, LANES), jnp.float32)
            near = rolled[slab][(-start) % LANES][:rows]
            far = rolled[slab][(WINDOW - start) % LANES][8:]
            return jnp.where(lane < WINDOW, near, far)

        window = piece(first)
        if cut < WINDOW:
            window = jnp.where(lane % WINDOW < cut, window, piece(first + 1))
        windows.append(window)
    return windows


def put_field(member, parts, z_ref, sum_rows):
    windows = column_windows(parts)
    for pair in range(len(windows) // 2):
        for group in range(2):
            rows = [window[16 * group : 16 * group + sum_rows] for window in windows[2 * pair : 2 * pair + 2]]
            high, low = split(jnp.concatenate(rows, axis=0))
            lanes = pl.ds((2 * member + group) * LANES, LANES)
            z_ref[pl.ds(2 * pair * sum_rows, 2 * sum_rows), lanes] = high
            z_ref[pl.ds((2 * pair + len(windows)) * sum_rows, 2 * sum_rows), lanes] = low


def gather_taps(t_ref, out_rows):
    sum_rows = out_rows + 8
    lane = lane_of((out_rows, LANES))
    halves = []
    for half in range(t_ref.shape[0] // sum_rows // 4):
        total = None
        for i in range(4):
            picked = None
            for jj in range(4):
                base = (4 * half + jj) * sum_rows + i
                near = t_ref[pl.ds(base, out_rows), pl.ds(0, LANES)]
                far = t_ref[pl.ds(base + 4, out_rows), pl.ds(LANES, LANES)]
                moved = pltpu.roll(near + far, (BLOCK * (jj - i)) % LANES, 1) if jj != i else near + far
                picked = moved if picked is None else jnp.where(lane >= BLOCK * jj, moved, picked)
            total = picked if total is None else total + picked
        halves.append(total)
    return jnp.concatenate(halves, axis=1)


def lay_model(wide, x_ref, shifts):
    slabs = wide.shape[1] // LANES
    blocks = wide.shape[1] // BLOCK
    half = x_ref.shape[0] // 2
    rows = half // blocks
    for s in shifts:
        parts = [wide[pl.ds(s, rows + 24), pl.ds(LANES * i, LANES)] for i in range(slabs)]
        windows = column_windows(parts)
        for j in range(blocks):
            high, low = split(windows[j])
            for group in range(2):
                lanes = pl.ds((2 * s + group) * LANES, LANES)
                x_ref[pl.ds(rows * j, rows), lanes] = high[16 * group : 16 * group + rows]
                x_ref[pl.ds(half + rows * j, rows), lanes] = low[16 * group : 16 * group + rows]


def blur_all(operator_for, wb_high, wb_low, wide, x_ref, g_ref):
    step = 2 * LANES
    depth = x_ref.shape[1] // 2
    for at in range(0, wb_high.shape[0], step):
        members = pl.ds(at, step)
        if at == 0:
            lay_model(wide, x_ref, range(4))
        operator_for(range(at // BLOCK, (at + step) // BLOCK))
        if at == 0:
            for half in range(2):
                if half == 1:
                    lay_model(wide, x_ref, range(4, 8))
                lanes = pl.ds(depth * half, depth)
                part = dot_split(x_ref.at[:, lanes], wb_high[members, lanes], wb_low[members, lanes])
                g_ref[:, members] = part if half == 0 else g_ref[:, members] + part
        else:
            g_ref[:, members] = dot_split(x_ref, wb_high[members, :], wb_low[members, :])


def blurred_parts(g_ref, member, rows, slabs):
    lane = lane_of((rows, LANES))
    place = member % 4
    parts = []
    for slab in range(slabs):
        picked = None
        for jj in range(4):
            block = g_ref[pl.ds((4 * slab + jj) * rows, rows), pl.ds(member // 4 * LANES, LANES)]
            moved = pltpu.roll(block, (BLOCK * (jj - place)) % LANES, 1) if jj != place else block
            picked = moved if picked is None else jnp.where(lane >= BLOCK * jj, moved, picked)
        parts.append(picked)
    return parts


def send_kernel(cover, kernel, counts, out, padded):
    size = kernel.shape[0]
    front = TAPS - size
    padded[...] = jnp.zeros(padded.shape, jnp.float32)
    for row in range(size):
        padded[pl.ds(front + row, 1), pl.ds(front, size)] = kernel[row]
    straight = padded[...]
    straight = straight / jnp.sum(straight)
    table = straight[0:8]
    for q in range(1, TAPS // 8):
        table = table + pltpu.roll(straight[8 * q : 8 * q + 8], TAPS * q, 1)
    row = lax.broadcasted_iota(jnp.int32, table.shape, 0)
    lane = lane_of(table.shape)
    for tile in range(cover.shape[1]):
        spot = (row == tile % 8) & (lane == tile // 8 * TAPS)
        entry = jnp.broadcast_to(cover[0:1, tile : tile + 1].astype(jnp.float32), table.shape)
        table = jnp.where(spot, entry, table)
    slabs = counts.shape[2] // LANES
    own = (out.shape[1] - 8) // slabs
    for peer in range(out.shape[0]):
        for slab in range(slabs):
            out[peer, pl.ds(slab * own, own), :] = counts[0, pl.ds(peer * own, own), pl.ds(slab * LANES, LANES)]
        out[peer, pl.ds(slabs * own, 8), :] = table


def weight_of(member, first_row, tile_rows, tiles, received, rows):
    table_row = received.shape[1] - 8
    row = first_row - TAPS // 2 + lax.broadcasted_iota(jnp.int32, (rows, LANES), 0)
    weight = jnp.zeros((rows, LANES), jnp.float32)
    for tile in range(tiles):
        entry = received[member, pl.ds(table_row + tile % 8, 1), :]
        inside = (row >= tile * tile_rows) & (row < (tile + 1) * tile_rows)
        weight = jnp.where(inside, jnp.broadcast_to(entry[:, tile // 8 * TAPS :][:, 0:1], (rows, LANES)), weight)
    return weight


def update(blurred_of, weight_at, counts_of, model, norm, wc_high, wc_low, z_ref, t_ref, out):
    out_rows = out.shape[0]
    members = z_ref.shape[1] // (4 * WINDOW)
    for first in range(0, members, CHUNK):
        for member in range(first, first + CHUNK):
            weight = weight_at(member)
            parts = []
            for blurred, counts in zip(blurred_of(member), counts_of(member)):
                safe = jnp.where(weight > 0.0, blurred, 1.0)
                parts.append(weight * counts / safe)
            put_field(member, parts, z_ref, out_rows + 8)
        lanes = pl.ds(4 * WINDOW * first, 4 * WINDOW * CHUNK)
        part = dot_split(z_ref.at[:, lanes], wc_high[:, lanes], wc_low[:, lanes])
        t_ref[...] = part if first == 0 else t_ref[...] + part
    out[...] = model * gather_taps(t_ref, out_rows) / norm


def norm_field(first_row, tile_rows, tiles, received, norm):
    out_rows, width = norm.shape
    members = received.shape[0]
    table_row = received.shape[1] - 8
    table = received[:, pl.ds(table_row, 8), :].reshape(8 * members, LANES)
    entry = lax.broadcasted_iota(jnp.int32, (8 * members, 8 * members), 0)
    lane = lane_of((8 * members, 8 * members))
    covers = []
    for tile in range(tiles):
        column = jnp.broadcast_to(table[:, tile // 8 * TAPS :][:, 0:1], entry.shape)
        spot = entry == lane // 8 * 8 + tile % 8
        covers.append(jnp.sum(jnp.where(spot, column, 0.0), axis=0, keepdims=True))
    row = lax.broadcasted_iota(jnp.int32, (out_rows, 8 * members), 0) + lane_of((out_rows, 8 * members)) % 8
    total = None
    for index in range(4):
        offset = lax.broadcasted_iota(jnp.int32, (LANES, width), 0) - TAPS * index
        column = lane_of((LANES, width)) + offset - TAPS // 2
        inside = (offset >= 1) & (offset < TAPS) & (column >= 0) & (column < width)
        inside = inside.astype(jnp.bfloat16)
        high, low = split(table)
        sums = jnp.dot(high, inside, preferred_element_type=jnp.float32)
        sums = sums + jnp.dot(low, inside, preferred_element_type=jnp.float32)
        place = row + (first_row - TAPS // 2 + 8 * index)
        weight = jnp.zeros(place.shape, jnp.float32)
        for tile in range(tiles):
            covered = (place >= tile * tile_rows) & (place < (tile + 1) * tile_rows)
            weight = jnp.where(covered, jnp.broadcast_to(covers[tile], place.shape), weight)
        weight = weight.astype(jnp.bfloat16)
        high, low = split(sums)
        part = jnp.dot(weight, high, preferred_element_type=jnp.float32)
        part = part + jnp.dot(weight, low, preferred_element_type=jnp.float32)
        total = part if total is None else total + part
    norm[...] = total


def put_model(refs, at, tall, wide):
    even_swap, own, odd_swap = refs
    rows = own.shape[0]
    tall[pl.ds(rows, rows), :] = own[...]
    tall[pl.ds(pl.multiple_of(2 * rows * (1 - at[0, 2]), rows), rows), :] = even_swap[...]
    tall[pl.ds(pl.multiple_of(2 * rows * at[0, 2], rows), rows), :] = odd_swap[...]
    wide[...] = tall[pl.ds(pl.multiple_of(at[0, 1], 8), wide.shape[0]), :]


def counts_window(at, received, swaps, rows):
    def window(member):
        parts = []
        for first in range(0, received.shape[1] - 8, rows):
            slab = pl.ds(first, rows)
            own = received[member, slab, :]
            before, after = [], []
            for hop in range(len(swaps) // 2):
                even, odd = (ref[member, slab, :] for ref in swaps[2 * hop : 2 * hop + 2])
                is_even = at[0, 3 + hop] == 0
                before.insert(0, jnp.where(is_even, odd, even))
                after.append(jnp.where(is_even, even, odd))
            parts.append(jnp.concatenate(before + [own] + after, axis=0))
        return parts

    return window


def first_kernel(
    norm_at, at, received, even_swap, own, odd_swap, wb_high, wb_low, wc_high, wc_low, blurred, norm, tall, wide, x_ref, g_ref
):
    members, rows, width = blurred.shape
    table_row = received.shape[1] - 8
    table = received[:, pl.ds(table_row, 8), :].reshape(8 * members, LANES)
    source = lax.broadcasted_iota(jnp.int32, (LANES, LANES), 0)
    target = lane_of((LANES, LANES))
    tap = target % WINDOW
    used = (tap >= 1) & (tap < TAPS)
    picks = []
    for group in range(2):
        slot = 2 * group + target // WINDOW
        for last in (4, 3):
            picks.append(used & (source == TAPS * (last - slot) + TAPS - tap))
    picks = jnp.concatenate([pick.astype(jnp.bfloat16) for pick in picks], axis=1)
    high, low = split(table)
    mirrored = jnp.dot(jnp.concatenate([high, low], axis=0), picks, preferred_element_type=jnp.float32)
    mirrored = mirrored[: 8 * members] + mirrored[8 * members :]
    lane = lane_of((8, LANES))
    used = (lane % WINDOW >= 1) & (lane % WINDOW < TAPS)

    def band_of(base, s):
        band = jnp.broadcast_to(base[s : s + 1], (BLOCK, LANES))
        return split(pltpu.roll(band, 0, 1, stride=1, stride_axis=0))

    def blur_operator(chosen):
        for member in chosen:
            for group in range(2):
                for s in range(8):
                    spot = (pl.ds(BLOCK * member, BLOCK), pl.ds(LANES * (2 * s + group), LANES))
                    first = (2 * group + (s > 0)) * LANES
                    base = mirrored[8 * member : 8 * member + 8, first : first + LANES]
                    wb_high[spot], wb_low[spot] = band_of(base, (8 - s) % 8)

    put_model((even_swap, own, odd_swap), at, tall, wide)
    blur_all(blur_operator, wb_high, wb_low, wide, x_ref, g_ref)
    for member in range(members):
        for group in range(2):
            entry = table[8 * member : 8 * member + 8]
            near = pltpu.roll(entry, WINDOW, 1) if group else entry
            straight = jnp.where(used, jnp.where(lane < WINDOW, near, pltpu.roll(near, TAPS, 1)), 0.0)
            for s in range(8):
                spot = (pl.ds(BLOCK * s, BLOCK), pl.ds((2 * member + group) * LANES, LANES))
                wc_high[spot], wc_low[spot] = band_of(straight, s)
    for member in range(members):
        for slab, part in enumerate(blurred_parts(g_ref, member, rows, width // LANES)):
            blurred[member, :, pl.ds(LANES * slab, LANES)] = part
    norm_at(at[0, 0], received=received, norm=norm)


def second_kernel(weight_at, at, wc_high, wc_low, received, blurred, model, norm, *refs):
    swaps, (out, z_ref, t_ref) = refs[:-3], refs[-3:]
    out_rows, width = out.shape

    def blurred_of(member):
        return [blurred[member, :, pl.ds(first, LANES)] for first in range(0, width, LANES)]

    counts_of = counts_window(at, received, swaps, out_rows)
    weight_of_shard = functools.partial(weight_at, first_row=at[0, 0], received=received, rows=out_rows + TAPS)
    update(blurred_of, weight_of_shard, counts_of, model[...], norm[...], wc_high, wc_low, z_ref, t_ref, out)


def third_kernel(weight_at, at, wb_high, wb_low, wc_high, wc_low, received, model, norm, even_swap, own, odd_swap, *refs):
    swaps, (out, tall, wide, x_ref, g_ref, z_ref, t_ref) = refs[:-7], refs[-7:]
    out_rows, width = out.shape
    rows = out_rows + TAPS
    put_model((even_swap, own, odd_swap), at, tall, wide)
    blur_all(lambda chosen: None, wb_high, wb_low, wide, x_ref, g_ref)
    blurred_of = functools.partial(blurred_parts, g_ref, rows=rows, slabs=width // LANES)
    counts_of = counts_window(at, received, swaps, out_rows)
    weight_of_shard = functools.partial(weight_at, first_row=at[0, 0], received=received, rows=rows)
    update(blurred_of, weight_of_shard, counts_of, model[...], norm[...], wc_high, wc_low, z_ref, t_ref, out)


def call(kernel, out_shape, scratch_shapes, flops, *operands, scalars=0):
    whole = pl.BlockSpec(memory_space=pltpu.VMEM)
    scalar = pl.BlockSpec(memory_space=pltpu.SMEM)
    return pl.pallas_call(
        kernel,
        out_shape=out_shape,
        in_specs=[scalar] * scalars + [whole] * (len(operands) - scalars),
        out_specs=jax.tree.map(lambda _: whole, out_shape),
        scratch_shapes=scratch_shapes,
        compiler_params=pltpu.CompilerParams(vmem_limit_bytes=VMEM_BYTES),
        cost_estimate=pl.CostEstimate(flops=flops, bytes_accessed=4 * 1024 * 1024, transcendentals=0),
    )(*operands)


def strip_permute(array, target):
    tiles, members = lax.axis_size("tile"), lax.axis_size("visit")
    count = tiles * members
    place = [i % members * tiles + i // members for i in range(count)]
    pairs = [(place[i], place[target(i)]) for i in range(count) if 0 <= target(i) < count]
    return lax.ppermute(array, ("visit", "tile"), pairs)


def group_gather(array, group):
    return [array] + [strip_permute(array, lambda i: i // group * group + (i + k) % group) for k in range(1, group)]


def group_order(arrays, place):
    ordered = []
    for slot in range(len(arrays)):
        back = (place - slot) % len(arrays)
        picked = arrays[0]
        for k in range(1, len(arrays)):
            picked = jnp.where(back == k, arrays[k], picked)
        ordered.append(picked)
    return ordered


def group_swaps(rows, group):
    def partner(first):
        return lambda i: i + group if i // group % 2 == first else i - group

    return [strip_permute(rows, partner(0)), rows, strip_permute(rows, partner(1))]


def body(exposures, sky_model, blur_kernels, coverage):
    tile_rows, width = exposures.shape[1:]
    shard_rows = sky_model.shape[0]
    members = lax.axis_size("visit")
    tiles = lax.axis_size("tile")
    visit = lax.axis_index("visit")
    group = TAPS // shard_rows
    place = visit % group
    hops = TAPS // 2 // shard_rows
    first_row = lax.axis_index("tile") * tile_rows + visit * shard_rows
    parities = [visit // hop % 2 for hop in [group, *range(1, hops + 1)]]
    at = jnp.stack([first_row, place * shard_rows, *parities]).reshape(1, -1)

    f32, bf16 = jnp.float32, jnp.bfloat16
    shape = jax.ShapeDtypeStruct
    blocks = width // BLOCK
    depth = TAPS * WINDOW
    rows = shard_rows + TAPS

    def halo_of(model):
        mine = jnp.concatenate(group_order(group_gather(model, group), place), axis=0)
        return group_swaps(mine, group)

    sent = call(
        send_kernel,
        shape((members, width // LANES * shard_rows + 8, LANES), f32),
        [pltpu.VMEM((TAPS, LANES), f32)],
        1 << 22,
        *(coverage, jnp.transpose(blur_kernels, (1, 0, 2)), exposures),
    )
    received = lax.all_to_all(sent, "visit", 0, 0)
    received, near = lax.optimization_barrier((received, halo_of(sky_model)))
    swaps = []
    for hop in range(1, hops + 1):
        even, _, odd = group_swaps(received[:, : width // LANES * shard_rows], hop)
        swaps += [even, odd]

    blur_scratch = [
        pltpu.VMEM((3 * TAPS, width), f32),
        pltpu.VMEM((rows + TAPS, width), f32),
        pltpu.VMEM((2 * blocks * rows, depth), bf16),
        pltpu.VMEM((blocks * rows, members * BLOCK), f32),
    ]
    sum_scratch = [
        pltpu.VMEM((2 * blocks * (shard_rows + 8), members * 4 * WINDOW), bf16),
        pltpu.VMEM((blocks * (shard_rows + 8), 8 * BLOCK), f32),
    ]
    blur_flops = 6 * blocks * rows * depth * members * BLOCK
    sum_flops = 6 * blocks * (shard_rows + 8) * members * 4 * WINDOW * 8 * BLOCK
    weight_at = functools.partial(weight_of, tile_rows=tile_rows, tiles=tiles)
    wb_high, wb_low, wc_high, wc_low, blurred, norm = call(
        functools.partial(first_kernel, functools.partial(norm_field, tile_rows=tile_rows, tiles=tiles)),
        (
            shape((members * BLOCK, depth), bf16),
            shape((members * BLOCK, depth), bf16),
            shape((8 * BLOCK, members * 4 * WINDOW), bf16),
            shape((8 * BLOCK, members * 4 * WINDOW), bf16),
            shape((members, rows, width), f32),
            shape((shard_rows, width), f32),
        ),
        blur_scratch,
        blur_flops + sum_flops,
        *(at, received, *near),
        scalars=1,
    )
    model = call(
        functools.partial(second_kernel, weight_at),
        shape((shard_rows, width), f32),
        sum_scratch,
        sum_flops,
        *(at, wc_high, wc_low, received, blurred, sky_model, norm, *swaps),
        scalars=1,
    )
    return call(
        functools.partial(third_kernel, weight_at),
        shape((shard_rows, width), f32),
        blur_scratch + sum_scratch,
        blur_flops + sum_flops,
        *(at, wb_high, wb_low, wc_high, wc_low, received, model, norm, *halo_of(model), *swaps),
        scalars=1,
    )


def solution(mesh):
    return jax.shard_map(
        body,
        mesh=mesh,
        in_specs=(
            P("visit", "tile", None),
            P(("tile", "visit"), None),
            P("visit", None, None),
            P("visit", None),
        ),
        out_specs=P(("tile", "visit"), None),
        check_vma=False,
    )
```

```python
import functools

import jax
import jax.numpy as jnp
from jax import lax
from jax.experimental import pallas as pl
from jax.experimental.pallas import tpu as pltpu
from jax.sharding import PartitionSpec as P

LANES = 128
BLOCK = 32
WINDOW = 64
TAPS = 32
MARGIN = WINDOW // 4
CHUNK = 4
VMEM_BYTES = 20 * 1024 * 1024


def split(x):
    high = x.astype(jnp.bfloat16)
    low = (x - high.astype(jnp.float32)).astype(jnp.bfloat16)
    return high, low


def dot_t(x, w):
    return lax.dot_general(x, w, (((1,), (1,)), ((), ())), preferred_element_type=jnp.float32)


def dot_split(both, w_high, w_low):
    rows = both.shape[0] // 2
    wide = dot_t(both[...], w_high)
    return wide[:rows] + (wide[rows:] + dot_t(both[pl.ds(0, rows), :], w_low))


def lane_of(shape):
    return lax.broadcasted_iota(jnp.int32, shape, len(shape) - 1)


def column_windows(parts):
    rows = parts[0].shape[0] - 8
    lane = lane_of((rows, LANES))
    shifts = sorted({(MARGIN - BLOCK * j) % LANES for j in range(LANES // BLOCK)})
    rolled = [{shift: pltpu.roll(part, shift, 1) for shift in shifts} for part in parts]
    windows = []
    for j in range(len(parts) * LANES // BLOCK):
        start = BLOCK * j - MARGIN
        first = start // LANES
        cut = (first + 1) * LANES - start

        def piece(slab):
            if slab < 0 or slab >= len(parts):
                return jnp.zeros((rows, LANES), jnp.float32)
            near = rolled[slab][(-start) % LANES][:rows]
            far = rolled[slab][(WINDOW - start) % LANES][8:]
            return jnp.where(lane < WINDOW, near, far)

        window = piece(first)
        if cut < WINDOW:
            window = jnp.where(lane % WINDOW < cut, window, piece(first + 1))
        windows.append(window)
    return windows


def put_field(member, parts, z_ref, sum_rows):
    windows = column_windows(parts)
    for pair in range(len(windows) // 2):
        for group in range(2):
            rows = [window[16 * group : 16 * group + sum_rows] for window in windows[2 * pair : 2 * pair + 2]]
            high, low = split(jnp.concatenate(rows, axis=0))
            lanes = pl.ds((2 * member + group) * LANES, LANES)
            z_ref[pl.ds(2 * pair * sum_rows, 2 * sum_rows), lanes] = high
            z_ref[pl.ds((2 * pair + len(windows)) * sum_rows, 2 * sum_rows), lanes] = low


def gather_taps(t_ref, out_rows):
    sum_rows = out_rows + 8
    lane = lane_of((out_rows, LANES))
    halves = []
    for half in range(t_ref.shape[0] // sum_rows // 4):
        total = None
        for i in range(4):
            picked = None
            for jj in range(4):
                base = (4 * half + jj) * sum_rows + i
                near = t_ref[pl.ds(base, out_rows), pl.ds(0, LANES)]
                far = t_ref[pl.ds(base + 4, out_rows), pl.ds(LANES, LANES)]
                moved = pltpu.roll(near + far, (BLOCK * (jj - i)) % LANES, 1) if jj != i else near + far
                picked = moved if picked is None else jnp.where(lane >= BLOCK * jj, moved, picked)
            total = picked if total is None else total + picked
        halves.append(total)
    return jnp.concatenate(halves, axis=1)


def lay_model(wide, x_ref, shifts):
    slabs = wide.shape[1] // LANES
    blocks = wide.shape[1] // BLOCK
    half = x_ref.shape[0] // 2
    rows = half // blocks
    for s in shifts:
        parts = [wide[pl.ds(s, rows + 24), pl.ds(LANES * i, LANES)] for i in range(slabs)]
        windows = column_windows(parts)
        for j in range(blocks):
            high, low = split(windows[j])
            for group in range(2):
                lanes = pl.ds((2 * s + group) * LANES, LANES)
                x_ref[pl.ds(rows * j, rows), lanes] = high[16 * group : 16 * group + rows]
                x_ref[pl.ds(half + rows * j, rows), lanes] = low[16 * group : 16 * group + rows]


def blur_all(operator_for, wb_high, wb_low, wide, x_ref, g_ref):
    step = 2 * LANES
    depth = x_ref.shape[1] // 2
    for at in range(0, wb_high.shape[0], step):
        members = pl.ds(at, step)
        if at == 0:
            lay_model(wide, x_ref, range(4))
        operator_for(range(at // BLOCK, (at + step) // BLOCK))
        if at == 0:
            for half in range(2):
                if half == 1:
                    lay_model(wide, x_ref, range(4, 8))
                lanes = pl.ds(depth * half, depth)
                part = dot_split(x_ref.at[:, lanes], wb_high[members, lanes], wb_low[members, lanes])
                g_ref[:, members] = part if half == 0 else g_ref[:, members] + part
        else:
            g_ref[:, members] = dot_split(x_ref, wb_high[members, :], wb_low[members, :])


def blurred_parts(g_ref, member, rows, slabs):
    lane = lane_of((rows, LANES))
    place = member % 4
    parts = []
    for slab in range(slabs):
        picked = None
        for jj in range(4):
            block = g_ref[pl.ds((4 * slab + jj) * rows, rows), pl.ds(member // 4 * LANES, LANES)]
            moved = pltpu.roll(block, (BLOCK * (jj - place)) % LANES, 1) if jj != place else block
            picked = moved if picked is None else jnp.where(lane >= BLOCK * jj, moved, picked)
        parts.append(picked)
    return parts


def send_kernel(cover, kernel, counts, out, padded):
    size = kernel.shape[0]
    front = TAPS - size
    padded[...] = jnp.zeros(padded.shape, jnp.float32)
    for row in range(size):
        padded[pl.ds(front + row, 1), pl.ds(front, size)] = kernel[row]
    straight = padded[...]
    straight = straight / jnp.sum(straight)
    table = straight[0:8]
    for q in range(1, TAPS // 8):
        table = table + pltpu.roll(straight[8 * q : 8 * q + 8], TAPS * q, 1)
    row = lax.broadcasted_iota(jnp.int32, table.shape, 0)
    lane = lane_of(table.shape)
    for tile in range(cover.shape[1]):
        spot = (row == tile % 8) & (lane == tile // 8 * TAPS)
        entry = jnp.broadcast_to(cover[0:1, tile : tile + 1].astype(jnp.float32), table.shape)
        table = jnp.where(spot, entry, table)
    slabs = counts.shape[2] // LANES
    own = (out.shape[1] - 8) // slabs
    for peer in range(out.shape[0]):
        for slab in range(slabs):
            out[peer, pl.ds(slab * own, own), :] = counts[0, pl.ds(peer * own, own), pl.ds(slab * LANES, LANES)]
        out[peer, pl.ds(slabs * own, 8), :] = table


def weight_of(member, first_row, tile_rows, tiles, received, rows):
    table_row = received.shape[1] - 8
    row = first_row - TAPS // 2 + lax.broadcasted_iota(jnp.int32, (rows, LANES), 0)
    weight = jnp.zeros((rows, LANES), jnp.float32)
    for tile in range(tiles):
        entry = received[member, pl.ds(table_row + tile % 8, 1), :]
        inside = (row >= tile * tile_rows) & (row < (tile + 1) * tile_rows)
        weight = jnp.where(inside, jnp.broadcast_to(entry[:, tile // 8 * TAPS :][:, 0:1], (rows, LANES)), weight)
    return weight


def update(blurred_of, weight_at, counts_of, model, norm, wc_high, wc_low, z_ref, t_ref, out):
    out_rows = out.shape[0]
    members = z_ref.shape[1] // (4 * WINDOW)
    for first in range(0, members, CHUNK):
        for member in range(first, first + CHUNK):
            weight = weight_at(member)
            parts = []
            for blurred, counts in zip(blurred_of(member), counts_of(member)):
                safe = jnp.where(weight > 0.0, blurred, 1.0)
                parts.append(weight * counts / safe)
            put_field(member, parts, z_ref, out_rows + 8)
        lanes = pl.ds(4 * WINDOW * first, 4 * WINDOW * CHUNK)
        part = dot_split(z_ref.at[:, lanes], wc_high[:, lanes], wc_low[:, lanes])
        t_ref[...] = part if first == 0 else t_ref[...] + part
    out[...] = model * gather_taps(t_ref, out_rows) / norm


def norm_field(first_row, tile_rows, tiles, received, norm):
    out_rows, width = norm.shape
    members = received.shape[0]
    table_row = received.shape[1] - 8
    table = received[:, pl.ds(table_row, 8), :].reshape(8 * members, LANES)
    entry = lax.broadcasted_iota(jnp.int32, (8 * members, 8 * members), 0)
    lane = lane_of((8 * members, 8 * members))
    covers = []
    for tile in range(tiles):
        column = jnp.broadcast_to(table[:, tile // 8 * TAPS :][:, 0:1], entry.shape)
        spot = entry == lane // 8 * 8 + tile % 8
        covers.append(jnp.sum(jnp.where(spot, column, 0.0), axis=0, keepdims=True))
    row = lax.broadcasted_iota(jnp.int32, (out_rows, 8 * members), 0) + lane_of((out_rows, 8 * members)) % 8
    total = None
    for index in range(4):
        offset = lax.broadcasted_iota(jnp.int32, (LANES, width), 0) - TAPS * index
        column = lane_of((LANES, width)) + offset - TAPS // 2
        inside = (offset >= 1) & (offset < TAPS) & (column >= 0) & (column < width)
        inside = inside.astype(jnp.bfloat16)
        high, low = split(table)
        sums = jnp.dot(high, inside, preferred_element_type=jnp.float32)
        sums = sums + jnp.dot(low, inside, preferred_element_type=jnp.float32)
        place = row + (first_row - TAPS // 2 + 8 * index)
        weight = jnp.zeros(place.shape, jnp.float32)
        for tile in range(tiles):
            covered = (place >= tile * tile_rows) & (place < (tile + 1) * tile_rows)
            weight = jnp.where(covered, jnp.broadcast_to(covers[tile], place.shape), weight)
        weight = weight.astype(jnp.bfloat16)
        high, low = split(sums)
        part = jnp.dot(weight, high, preferred_element_type=jnp.float32)
        part = part + jnp.dot(weight, low, preferred_element_type=jnp.float32)
        total = part if total is None else total + part
    norm[...] = total


def put_model(refs, at, tall, wide):
    even_swap, own, odd_swap = refs
    rows = own.shape[0]
    tall[pl.ds(rows, rows), :] = own[...]
    tall[pl.ds(pl.multiple_of(2 * rows * (1 - at[0, 2]), rows), rows), :] = even_swap[...]
    tall[pl.ds(pl.multiple_of(2 * rows * at[0, 2], rows), rows), :] = odd_swap[...]
    wide[...] = tall[pl.ds(pl.multiple_of(at[0, 1], 8), wide.shape[0]), :]


def counts_window(at, received, swaps, rows):
    def window(member):
        parts = []
        for first in range(0, received.shape[1] - 8, rows):
            slab = pl.ds(first, rows)
            own = received[member, slab, :]
            before, after = [], []
            for hop in range(len(swaps) // 2):
                even, odd = (ref[member, slab, :] for ref in swaps[2 * hop : 2 * hop + 2])
                is_even = at[0, 3 + hop] == 0
                before.insert(0, jnp.where(is_even, odd, even))
                after.append(jnp.where(is_even, even, odd))
            parts.append(jnp.concatenate(before + [own] + after, axis=0))
        return parts

    return window


def first_kernel(
    norm_at, at, received, even_swap, own, odd_swap, wb_high, wb_low, wc_high, wc_low, blurred, norm, tall, wide, x_ref, g_ref, flips
):
    members, rows, width = blurred.shape
    table_row = received.shape[1] - 8
    table = received[:, pl.ds(table_row, 8), :].reshape(8 * members, LANES)
    source = lax.broadcasted_iota(jnp.int32, (LANES, LANES), 0)
    target = lane_of((LANES, LANES))
    tap = target % WINDOW
    used = (tap >= 1) & (tap < TAPS)
    picks = []
    for group in range(2):
        slot = 2 * group + target // WINDOW
        for last in (4, 3):
            picks.append(used & (source == TAPS * (last - slot) + TAPS - tap))
    picks = jnp.concatenate([pick.astype(jnp.bfloat16) for pick in picks], axis=1)
    high, low = split(table)
    mirrored = jnp.dot(jnp.concatenate([high, low], axis=0), picks, preferred_element_type=jnp.float32)
    flips[...] = mirrored[: 8 * members] + mirrored[8 * members :]
    lane = lane_of((8, LANES))
    used = (lane % WINDOW >= 1) & (lane % WINDOW < TAPS)

    def band_of(base, s):
        band = jnp.broadcast_to(base[s : s + 1], (BLOCK, LANES))
        return split(pltpu.roll(band, 0, 1, stride=1, stride_axis=0))

    def blur_operator(chosen):
        for member in chosen:
            for group in range(2):
                for s in range(8):
                    spot = (pl.ds(BLOCK * member, BLOCK), pl.ds(LANES * (2 * s + group), LANES))
                    first = (2 * group + (s > 0)) * LANES
                    base = flips[pl.ds(8 * member, 8), pl.ds(first, LANES)]
                    wb_high[spot], wb_low[spot] = band_of(base, (8 - s) % 8)

    put_model((even_swap, own, odd_swap), at, tall, wide)
    blur_all(blur_operator, wb_high, wb_low, wide, x_ref, g_ref)
    for member in range(members):
        for group in range(2):
            entry = received[member, pl.ds(table_row, 8), :]
            near = pltpu.roll(entry, WINDOW, 1) if group else entry
            straight = jnp.where(used, jnp.where(lane < WINDOW, near, pltpu.roll(near, TAPS, 1)), 0.0)
            for s in range(8):
                spot = (pl.ds(BLOCK * s, BLOCK), pl.ds((2 * member + group) * LANES, LANES))
                wc_high[spot], wc_low[spot] = band_of(straight, s)
    for member in range(members):
        for slab, part in enumerate(blurred_parts(g_ref, member, rows, width // LANES)):
            blurred[member, :, pl.ds(LANES * slab, LANES)] = part
    norm_at(at[0, 0], received=received, norm=norm)


def second_kernel(weight_at, at, wc_high, wc_low, received, blurred, model, norm, *refs):
    swaps, (out, z_ref, t_ref) = refs[:-3], refs[-3:]
    out_rows, width = out.shape

    def blurred_of(member):
        return [blurred[member, :, pl.ds(first, LANES)] for first in range(0, width, LANES)]

    counts_of = counts_window(at, received, swaps, out_rows)
    weight_of_shard = functools.partial(weight_at, first_row=at[0, 0], received=received, rows=out_rows + TAPS)
    update(blurred_of, weight_of_shard, counts_of, model[...], norm[...], wc_high, wc_low, z_ref, t_ref, out)


def third_kernel(weight_at, at, wb_high, wb_low, wc_high, wc_low, received, model, norm, even_swap, own, odd_swap, *refs):
    swaps, (out, tall, wide, x_ref, g_ref, z_ref, t_ref) = refs[:-7], refs[-7:]
    out_rows, width = out.shape
    rows = out_rows + TAPS
    put_model((even_swap, own, odd_swap), at, tall, wide)
    blur_all(lambda chosen: None, wb_high, wb_low, wide, x_ref, g_ref)
    blurred_of = functools.partial(blurred_parts, g_ref, rows=rows, slabs=width // LANES)
    counts_of = counts_window(at, received, swaps, out_rows)
    weight_of_shard = functools.partial(weight_at, first_row=at[0, 0], received=received, rows=rows)
    update(blurred_of, weight_of_shard, counts_of, model[...], norm[...], wc_high, wc_low, z_ref, t_ref, out)


def call(kernel, out_shape, scratch_shapes, flops, *operands, scalars=0):
    whole = pl.BlockSpec(memory_space=pltpu.VMEM)
    scalar = pl.BlockSpec(memory_space=pltpu.SMEM)
    return pl.pallas_call(
        kernel,
        out_shape=out_shape,
        in_specs=[scalar] * scalars + [whole] * (len(operands) - scalars),
        out_specs=jax.tree.map(lambda _: whole, out_shape),
        scratch_shapes=scratch_shapes,
        compiler_params=pltpu.CompilerParams(vmem_limit_bytes=VMEM_BYTES),
        cost_estimate=pl.CostEstimate(flops=flops, bytes_accessed=4 * 1024 * 1024, transcendentals=0),
    )(*operands)


def strip_permute(array, target):
    tiles, members = lax.axis_size("tile"), lax.axis_size("visit")
    count = tiles * members
    place = [i % members * tiles + i // members for i in range(count)]
    pairs = [(place[i], place[target(i)]) for i in range(count) if 0 <= target(i) < count]
    return lax.ppermute(array, ("visit", "tile"), pairs)


def group_gather(array, group):
    return [array] + [strip_permute(array, lambda i: i // group * group + (i + k) % group) for k in range(1, group)]


def group_order(arrays, place):
    ordered = []
    for slot in range(len(arrays)):
        back = (place - slot) % len(arrays)
        picked = arrays[0]
        for k in range(1, len(arrays)):
            picked = jnp.where(back == k, arrays[k], picked)
        ordered.append(picked)
    return ordered


def group_swaps(rows, group):
    def partner(first):
        return lambda i: i + group if i // group % 2 == first else i - group

    return [strip_permute(rows, partner(0)), rows, strip_permute(rows, partner(1))]


def body(exposures, sky_model, blur_kernels, coverage):
    tile_rows, width = exposures.shape[1:]
    shard_rows = sky_model.shape[0]
    members = lax.axis_size("visit")
    tiles = lax.axis_size("tile")
    visit = lax.axis_index("visit")
    group = TAPS // shard_rows
    place = visit % group
    hops = TAPS // 2 // shard_rows
    first_row = lax.axis_index("tile") * tile_rows + visit * shard_rows
    parities = [visit // hop % 2 for hop in [group, *range(1, hops + 1)]]
    at = jnp.stack([first_row, place * shard_rows, *parities]).reshape(1, -1)

    f32, bf16 = jnp.float32, jnp.bfloat16
    shape = jax.ShapeDtypeStruct
    blocks = width // BLOCK
    depth = TAPS * WINDOW
    rows = shard_rows + TAPS

    def halo_of(model):
        mine = jnp.concatenate(group_order(group_gather(model, group), place), axis=0)
        return group_swaps(mine, group)

    sent = call(
        send_kernel,
        shape((members, width // LANES * shard_rows + 8, LANES), f32),
        [pltpu.VMEM((TAPS, LANES), f32)],
        1 << 22,
        *(coverage, jnp.transpose(blur_kernels, (1, 0, 2)), exposures),
    )
    received = lax.all_to_all(sent, "visit", 0, 0)
    received, near = lax.optimization_barrier((received, halo_of(sky_model)))
    swaps = []
    for hop in range(1, hops + 1):
        even, _, odd = group_swaps(received[:, : width // LANES * shard_rows], hop)
        swaps += [even, odd]

    blur_scratch = [
        pltpu.VMEM((3 * TAPS, width), f32),
        pltpu.VMEM((rows + TAPS, width), f32),
        pltpu.VMEM((2 * blocks * rows, depth), bf16),
        pltpu.VMEM((blocks * rows, members * BLOCK), f32),
    ]
    sum_scratch = [
        pltpu.VMEM((2 * blocks * (shard_rows + 8), members * 4 * WINDOW), bf16),
        pltpu.VMEM((blocks * (shard_rows + 8), 8 * BLOCK), f32),
    ]
    blur_flops = 6 * blocks * rows * depth * members * BLOCK
    sum_flops = 6 * blocks * (shard_rows + 8) * members * 4 * WINDOW * 8 * BLOCK
    weight_at = functools.partial(weight_of, tile_rows=tile_rows, tiles=tiles)
    wb_high, wb_low, wc_high, wc_low, blurred, norm = call(
        functools.partial(first_kernel, functools.partial(norm_field, tile_rows=tile_rows, tiles=tiles)),
        (
            shape((members * BLOCK, depth), bf16),
            shape((members * BLOCK, depth), bf16),
            shape((8 * BLOCK, members * 4 * WINDOW), bf16),
            shape((8 * BLOCK, members * 4 * WINDOW), bf16),
            shape((members, rows, width), f32),
            shape((shard_rows, width), f32),
        ),
        blur_scratch + [pltpu.VMEM((8 * members, 4 * LANES), f32)],
        blur_flops + sum_flops,
        *(at, received, *near),
        scalars=1,
    )
    model = call(
        functools.partial(second_kernel, weight_at),
        shape((shard_rows, width), f32),
        sum_scratch,
        sum_flops,
        *(at, wc_high, wc_low, received, blurred, sky_model, norm, *swaps),
        scalars=1,
    )
    return call(
        functools.partial(third_kernel, weight_at),
        shape((shard_rows, width), f32),
        blur_scratch + sum_scratch,
        blur_flops + sum_flops,
        *(at, wb_high, wb_low, wc_high, wc_low, received, model, norm, *halo_of(model), *swaps),
        scalars=1,
    )


def solution(mesh):
    return jax.shard_map(
        body,
        mesh=mesh,
        in_specs=(
            P("visit", "tile", None),
            P(("tile", "visit"), None),
            P("visit", None, None),
            P("visit", None),
        ),
        out_specs=P(("tile", "visit"), None),
        check_vma=False,
    )
```

```python
import functools

import jax
import jax.numpy as jnp
from jax import lax
from jax.experimental import pallas as pl
from jax.experimental.pallas import tpu as pltpu
from jax.sharding import PartitionSpec as P

LANES = 128
BLOCK = 32
WINDOW = 64
TAPS = 32
MARGIN = WINDOW // 4
CHUNK = 4
VMEM_BYTES = 20 * 1024 * 1024


def split(x):
    high = x.astype(jnp.bfloat16)
    low = (x - high.astype(jnp.float32)).astype(jnp.bfloat16)
    return high, low


def dot_t(x, w):
    return lax.dot_general(x, w, (((1,), (1,)), ((), ())), preferred_element_type=jnp.float32)


def dot_split(both, w_high, w_low):
    rows = both.shape[0] // 2
    wide = dot_t(both[...], w_high)
    return wide[:rows] + (wide[rows:] + dot_t(both[pl.ds(0, rows), :], w_low))


def lane_of(shape):
    return lax.broadcasted_iota(jnp.int32, shape, len(shape) - 1)


def column_windows(parts):
    rows = parts[0].shape[0] - 8
    lane = lane_of((rows, LANES))
    shifts = sorted({(MARGIN - BLOCK * j) % LANES for j in range(LANES // BLOCK)})
    rolled = [{shift: pltpu.roll(part, shift, 1) for shift in shifts} for part in parts]
    windows = []
    for j in range(len(parts) * LANES // BLOCK):
        start = BLOCK * j - MARGIN
        first = start // LANES
        cut = (first + 1) * LANES - start

        def piece(slab):
            if slab < 0 or slab >= len(parts):
                return jnp.zeros((rows, LANES), jnp.float32)
            near = rolled[slab][(-start) % LANES][:rows]
            far = rolled[slab][(WINDOW - start) % LANES][8:]
            return jnp.where(lane < WINDOW, near, far)

        window = piece(first)
        if cut < WINDOW:
            window = jnp.where(lane % WINDOW < cut, window, piece(first + 1))
        windows.append(window)
    return windows


def put_field(member, parts, z_ref, sum_rows):
    windows = column_windows(parts)
    for pair in range(len(windows) // 2):
        for group in range(2):
            rows = [window[16 * group : 16 * group + sum_rows] for window in windows[2 * pair : 2 * pair + 2]]
            high, low = split(jnp.concatenate(rows, axis=0))
            lanes = pl.ds((2 * member + group) * LANES, LANES)
            z_ref[pl.ds(2 * pair * sum_rows, 2 * sum_rows), lanes] = high
            z_ref[pl.ds((2 * pair + len(windows)) * sum_rows, 2 * sum_rows), lanes] = low


def gather_taps(t_ref, out_rows):
    sum_rows = out_rows + 8
    lane = lane_of((out_rows, LANES))
    halves = []
    for half in range(t_ref.shape[0] // sum_rows // 4):
        total = None
        for i in range(4):
            picked = None
            for jj in range(4):
                base = (4 * half + jj) * sum_rows + i
                near = t_ref[pl.ds(base, out_rows), pl.ds(0, LANES)]
                far = t_ref[pl.ds(base + 4, out_rows), pl.ds(LANES, LANES)]
                moved = pltpu.roll(near + far, (BLOCK * (jj - i)) % LANES, 1) if jj != i else near + far
                picked = moved if picked is None else jnp.where(lane >= BLOCK * jj, moved, picked)
            total = picked if total is None else total + picked
        halves.append(total)
    return jnp.concatenate(halves, axis=1)


def lay_model(wide, x_ref, shifts):
    slabs = wide.shape[1] // LANES
    blocks = wide.shape[1] // BLOCK
    half = x_ref.shape[0] // 2
    rows = half // blocks
    for s in shifts:
        parts = [wide[pl.ds(s, rows + 24), pl.ds(LANES * i, LANES)] for i in range(slabs)]
        windows = column_windows(parts)
        for j in range(blocks):
            high, low = split(windows[j])
            for group in range(2):
                lanes = pl.ds((2 * s + group) * LANES, LANES)
                x_ref[pl.ds(rows * j, rows), lanes] = high[16 * group : 16 * group + rows]
                x_ref[pl.ds(half + rows * j, rows), lanes] = low[16 * group : 16 * group + rows]


def blur_all(operator_for, wb_high, wb_low, wide, x_ref, g_ref):
    step = 2 * LANES
    depth = x_ref.shape[1] // 2
    for at in range(0, wb_high.shape[0], step):
        members = pl.ds(at, step)
        if at == 0:
            lay_model(wide, x_ref, range(4))
        operator_for(range(at // BLOCK, (at + step) // BLOCK))
        if at == 0:
            for half in range(2):
                if half == 1:
                    lay_model(wide, x_ref, range(4, 8))
                lanes = pl.ds(depth * half, depth)
                part = dot_split(x_ref.at[:, lanes], wb_high[members, lanes], wb_low[members, lanes])
                g_ref[:, members] = part if half == 0 else g_ref[:, members] + part
        else:
            g_ref[:, members] = dot_split(x_ref, wb_high[members, :], wb_low[members, :])


def blurred_parts(g_ref, member, rows, slabs):
    lane = lane_of((rows, LANES))
    place = member % 4
    parts = []
    for slab in range(slabs):
        picked = None
        for jj in range(4):
            block = g_ref[pl.ds((4 * slab + jj) * rows, rows), pl.ds(member // 4 * LANES, LANES)]
            moved = pltpu.roll(block, (BLOCK * (jj - place)) % LANES, 1) if jj != place else block
            picked = moved if picked is None else jnp.where(lane >= BLOCK * jj, moved, picked)
        parts.append(picked)
    return parts


def send_kernel(cover, kernel, counts, out, padded):
    size = kernel.shape[0]
    front = TAPS - size
    padded[...] = jnp.zeros(padded.shape, jnp.float32)
    for row in range(size):
        padded[pl.ds(front + row, 1), pl.ds(front, size)] = kernel[row]
    straight = padded[...]
    straight = straight / jnp.sum(straight)
    table = straight[0:8]
    for q in range(1, TAPS // 8):
        table = table + pltpu.roll(straight[8 * q : 8 * q + 8], TAPS * q, 1)
    row = lax.broadcasted_iota(jnp.int32, table.shape, 0)
    lane = lane_of(table.shape)
    for tile in range(cover.shape[1]):
        spot = (row == tile % 8) & (lane == tile // 8 * TAPS)
        entry = jnp.broadcast_to(cover[0:1, tile : tile + 1].astype(jnp.float32), table.shape)
        table = jnp.where(spot, entry, table)
    slabs = counts.shape[2] // LANES
    own = (out.shape[1] - 8) // slabs
    for peer in range(out.shape[0]):
        for slab in range(slabs):
            out[peer, pl.ds(slab * own, own), :] = counts[0, pl.ds(peer * own, own), pl.ds(slab * LANES, LANES)]
        out[peer, pl.ds(slabs * own, 8), :] = table


def weight_of(member, first_row, tile_rows, tiles, received, rows):
    table_row = received.shape[1] - 8
    row = first_row - TAPS // 2 + lax.broadcasted_iota(jnp.int32, (rows, LANES), 0)
    weight = jnp.zeros((rows, LANES), jnp.float32)
    for tile in range(tiles):
        entry = received[member, pl.ds(table_row + tile % 8, 1), :]
        inside = (row >= tile * tile_rows) & (row < (tile + 1) * tile_rows)
        weight = jnp.where(inside, jnp.broadcast_to(entry[:, tile // 8 * TAPS :][:, 0:1], (rows, LANES)), weight)
    return weight


def update(blurred_of, weight_at, counts_of, model, norm, wc_high, wc_low, z_ref, t_ref, out):
    out_rows = out.shape[0]
    members = z_ref.shape[1] // (4 * WINDOW)
    for first in range(0, members, CHUNK):
        for member in range(first, first + CHUNK):
            weight = weight_at(member)
            parts = []
            for blurred, counts in zip(blurred_of(member), counts_of(member)):
                safe = jnp.where(weight > 0.0, blurred, 1.0)
                parts.append(weight * counts / safe)
            put_field(member, parts, z_ref, out_rows + 8)
        lanes = pl.ds(4 * WINDOW * first, 4 * WINDOW * CHUNK)
        part = dot_split(z_ref.at[:, lanes], wc_high[:, lanes], wc_low[:, lanes])
        t_ref[...] = part if first == 0 else t_ref[...] + part
    out[...] = model * gather_taps(t_ref, out_rows) / norm


def norm_field(first_row, tile_rows, tiles, received, norm):
    out_rows, width = norm.shape
    members = received.shape[0]
    table_row = received.shape[1] - 8
    table = received[:, pl.ds(table_row, 8), :].reshape(8 * members, LANES)
    entry = lax.broadcasted_iota(jnp.int32, (8 * members, 8 * members), 0)
    lane = lane_of((8 * members, 8 * members))
    covers = []
    for tile in range(tiles):
        column = jnp.broadcast_to(table[:, tile // 8 * TAPS :][:, 0:1], entry.shape)
        spot = entry == lane // 8 * 8 + tile % 8
        covers.append(jnp.sum(jnp.where(spot, column, 0.0), axis=0, keepdims=True))
    row = lax.broadcasted_iota(jnp.int32, (out_rows, 8 * members), 0) + lane_of((out_rows, 8 * members)) % 8
    total = None
    for index in range(4):
        offset = lax.broadcasted_iota(jnp.int32, (LANES, width), 0) - TAPS * index
        column = lane_of((LANES, width)) + offset - TAPS // 2
        inside = (offset >= 1) & (offset < TAPS) & (column >= 0) & (column < width)
        inside = inside.astype(jnp.bfloat16)
        high, low = split(table)
        sums = jnp.dot(high, inside, preferred_element_type=jnp.float32)
        sums = sums + jnp.dot(low, inside, preferred_element_type=jnp.float32)
        place = row + (first_row - TAPS // 2 + 8 * index)
        weight = jnp.zeros(place.shape, jnp.float32)
        for tile in range(tiles):
            covered = (place >= tile * tile_rows) & (place < (tile + 1) * tile_rows)
            weight = jnp.where(covered, jnp.broadcast_to(covers[tile], place.shape), weight)
        weight = weight.astype(jnp.bfloat16)
        high, low = split(sums)
        part = jnp.dot(weight, high, preferred_element_type=jnp.float32)
        part = part + jnp.dot(weight, low, preferred_element_type=jnp.float32)
        total = part if total is None else total + part
    norm[...] = total


def put_model(refs, at, tall, wide):
    even_swap, own, odd_swap = refs
    rows = own.shape[0]
    tall[pl.ds(rows, rows), :] = own[...]
    tall[pl.ds(pl.multiple_of(2 * rows * (1 - at[0, 2]), rows), rows), :] = even_swap[...]
    tall[pl.ds(pl.multiple_of(2 * rows * at[0, 2], rows), rows), :] = odd_swap[...]
    wide[...] = tall[pl.ds(pl.multiple_of(at[0, 1], 8), wide.shape[0]), :]


def counts_window(at, received, swaps, rows):
    def window(member):
        parts = []
        for first in range(0, received.shape[1] - 8, rows):
            slab = pl.ds(first, rows)
            own = received[member, slab, :]
            before, after = [], []
            for hop in range(len(swaps) // 2):
                even, odd = (ref[member, slab, :] for ref in swaps[2 * hop : 2 * hop + 2])
                is_even = at[0, 3 + hop] == 0
                before.insert(0, jnp.where(is_even, odd, even))
                after.append(jnp.where(is_even, even, odd))
            parts.append(jnp.concatenate(before + [own] + after, axis=0))
        return parts

    return window


def mirror_kernel(received, flips):
    members = received.shape[0]
    table_row = received.shape[1] - 8
    table = received[:, pl.ds(table_row, 8), :].reshape(8 * members, LANES)
    source = lax.broadcasted_iota(jnp.int32, (LANES, LANES), 0)
    target = lane_of((LANES, LANES))
    tap = target % WINDOW
    used = (tap >= 1) & (tap < TAPS)
    picks = []
    for group in range(2):
        slot = 2 * group + target // WINDOW
        for last in (4, 3):
            picks.append(used & (source == TAPS * (last - slot) + TAPS - tap))
    picks = jnp.concatenate([pick.astype(jnp.bfloat16) for pick in picks], axis=1)
    high, low = split(table)
    mirrored = jnp.dot(jnp.concatenate([high, low], axis=0), picks, preferred_element_type=jnp.float32)
    flips[...] = mirrored[: 8 * members] + mirrored[8 * members :]


def first_kernel(
    norm_at, at, received, flips, even_swap, own, odd_swap, wb_high, wb_low, wc_high, wc_low, blurred, norm, tall, wide, x_ref, g_ref
):
    members, rows, width = blurred.shape
    table_row = received.shape[1] - 8
    lane = lane_of((8, LANES))
    used = (lane % WINDOW >= 1) & (lane % WINDOW < TAPS)

    def band_of(base, s):
        band = jnp.broadcast_to(base[s : s + 1], (BLOCK, LANES))
        return split(pltpu.roll(band, 0, 1, stride=1, stride_axis=0))

    def blur_operator(chosen):
        for member in chosen:
            for group in range(2):
                for s in range(8):
                    spot = (pl.ds(BLOCK * member, BLOCK), pl.ds(LANES * (2 * s + group), LANES))
                    first = (2 * group + (s > 0)) * LANES
                    base = flips[pl.ds(8 * member, 8), pl.ds(first, LANES)]
                    wb_high[spot], wb_low[spot] = band_of(base, (8 - s) % 8)

    put_model((even_swap, own, odd_swap), at, tall, wide)
    blur_all(blur_operator, wb_high, wb_low, wide, x_ref, g_ref)
    for member in range(members):
        for group in range(2):
            entry = received[member, pl.ds(table_row, 8), :]
            near = pltpu.roll(entry, WINDOW, 1) if group else entry
            straight = jnp.where(used, jnp.where(lane < WINDOW, near, pltpu.roll(near, TAPS, 1)), 0.0)
            for s in range(8):
                spot = (pl.ds(BLOCK * s, BLOCK), pl.ds((2 * member + group) * LANES, LANES))
                wc_high[spot], wc_low[spot] = band_of(straight, s)
    for member in range(members):
        for slab, part in enumerate(blurred_parts(g_ref, member, rows, width // LANES)):
            blurred[member, :, pl.ds(LANES * slab, LANES)] = part
    norm_at(at[0, 0], received=received, norm=norm)


def second_kernel(weight_at, at, wc_high, wc_low, received, blurred, model, norm, *refs):
    swaps, (out, z_ref, t_ref) = refs[:-3], refs[-3:]
    out_rows, width = out.shape

    def blurred_of(member):
        return [blurred[member, :, pl.ds(first, LANES)] for first in range(0, width, LANES)]

    counts_of = counts_window(at, received, swaps, out_rows)
    weight_of_shard = functools.partial(weight_at, first_row=at[0, 0], received=received, rows=out_rows + TAPS)
    update(blurred_of, weight_of_shard, counts_of, model[...], norm[...], wc_high, wc_low, z_ref, t_ref, out)


def third_kernel(weight_at, at, wb_high, wb_low, wc_high, wc_low, received, model, norm, even_swap, own, odd_swap, *refs):
    swaps, (out, tall, wide, x_ref, g_ref, z_ref, t_ref) = refs[:-7], refs[-7:]
    out_rows, width = out.shape
    rows = out_rows + TAPS
    put_model((even_swap, own, odd_swap), at, tall, wide)
    blur_all(lambda chosen: None, wb_high, wb_low, wide, x_ref, g_ref)
    blurred_of = functools.partial(blurred_parts, g_ref, rows=rows, slabs=width // LANES)
    counts_of = counts_window(at, received, swaps, out_rows)
    weight_of_shard = functools.partial(weight_at, first_row=at[0, 0], received=received, rows=rows)
    update(blurred_of, weight_of_shard, counts_of, model[...], norm[...], wc_high, wc_low, z_ref, t_ref, out)


def call(kernel, out_shape, scratch_shapes, flops, *operands, scalars=0):
    whole = pl.BlockSpec(memory_space=pltpu.VMEM)
    scalar = pl.BlockSpec(memory_space=pltpu.SMEM)
    return pl.pallas_call(
        kernel,
        out_shape=out_shape,
        in_specs=[scalar] * scalars + [whole] * (len(operands) - scalars),
        out_specs=jax.tree.map(lambda _: whole, out_shape),
        scratch_shapes=scratch_shapes,
        compiler_params=pltpu.CompilerParams(vmem_limit_bytes=VMEM_BYTES),
        cost_estimate=pl.CostEstimate(flops=flops, bytes_accessed=4 * 1024 * 1024, transcendentals=0),
    )(*operands)


def strip_permute(array, target):
    tiles, members = lax.axis_size("tile"), lax.axis_size("visit")
    count = tiles * members
    place = [i % members * tiles + i // members for i in range(count)]
    pairs = [(place[i], place[target(i)]) for i in range(count) if 0 <= target(i) < count]
    return lax.ppermute(array, ("visit", "tile"), pairs)


def group_gather(array, group):
    return [array] + [strip_permute(array, lambda i: i // group * group + (i + k) % group) for k in range(1, group)]


def group_order(arrays, place):
    ordered = []
    for slot in range(len(arrays)):
        back = (place - slot) % len(arrays)
        picked = arrays[0]
        for k in range(1, len(arrays)):
            picked = jnp.where(back == k, arrays[k], picked)
        ordered.append(picked)
    return ordered


def group_swaps(rows, group):
    def partner(first):
        return lambda i: i + group if i // group % 2 == first else i - group

    return [strip_permute(rows, partner(0)), rows, strip_permute(rows, partner(1))]


def body(exposures, sky_model, blur_kernels, coverage):
    tile_rows, width = exposures.shape[1:]
    shard_rows = sky_model.shape[0]
    members = lax.axis_size("visit")
    tiles = lax.axis_size("tile")
    visit = lax.axis_index("visit")
    group = TAPS // shard_rows
    place = visit % group
    hops = TAPS // 2 // shard_rows
    first_row = lax.axis_index("tile") * tile_rows + visit * shard_rows
    parities = [visit // hop % 2 for hop in [group, *range(1, hops + 1)]]
    at = jnp.stack([first_row, place * shard_rows, *parities]).reshape(1, -1)

    f32, bf16 = jnp.float32, jnp.bfloat16
    shape = jax.ShapeDtypeStruct
    blocks = width // BLOCK
    depth = TAPS * WINDOW
    rows = shard_rows + TAPS

    def halo_of(model):
        mine = jnp.concatenate(group_order(group_gather(model, group), place), axis=0)
        return group_swaps(mine, group)

    sent = call(
        send_kernel,
        shape((members, width // LANES * shard_rows + 8, LANES), f32),
        [pltpu.VMEM((TAPS, LANES), f32)],
        1 << 22,
        *(coverage, jnp.transpose(blur_kernels, (1, 0, 2)), exposures),
    )
    received = lax.all_to_all(sent, "visit", 0, 0)
    received, near = lax.optimization_barrier((received, halo_of(sky_model)))
    swaps = []
    for hop in range(1, hops + 1):
        even, _, odd = group_swaps(received[:, : width // LANES * shard_rows], hop)
        swaps += [even, odd]

    blur_scratch = [
        pltpu.VMEM((3 * TAPS, width), f32),
        pltpu.VMEM((rows + TAPS, width), f32),
        pltpu.VMEM((2 * blocks * rows, depth), bf16),
        pltpu.VMEM((blocks * rows, members * BLOCK), f32),
    ]
    sum_scratch = [
        pltpu.VMEM((2 * blocks * (shard_rows + 8), members * 4 * WINDOW), bf16),
        pltpu.VMEM((blocks * (shard_rows + 8), 8 * BLOCK), f32),
    ]
    blur_flops = 6 * blocks * rows * depth * members * BLOCK
    sum_flops = 6 * blocks * (shard_rows + 8) * members * 4 * WINDOW * 8 * BLOCK
    weight_at = functools.partial(weight_of, tile_rows=tile_rows, tiles=tiles)
    flips = call(mirror_kernel, shape((8 * members, 4 * LANES), f32), [], 1 << 22, received)
    wb_high, wb_low, wc_high, wc_low, blurred, norm = call(
        functools.partial(first_kernel, functools.partial(norm_field, tile_rows=tile_rows, tiles=tiles)),
        (
            shape((members * BLOCK, depth), bf16),
            shape((members * BLOCK, depth), bf16),
            shape((8 * BLOCK, members * 4 * WINDOW), bf16),
            shape((8 * BLOCK, members * 4 * WINDOW), bf16),
            shape((members, rows, width), f32),
            shape((shard_rows, width), f32),
        ),
        blur_scratch,
        blur_flops + sum_flops,
        *(at, received, flips, *near),
        scalars=1,
    )
    model = call(
        functools.partial(second_kernel, weight_at),
        shape((shard_rows, width), f32),
        sum_scratch,
        sum_flops,
        *(at, wc_high, wc_low, received, blurred, sky_model, norm, *swaps),
        scalars=1,
    )
    return call(
        functools.partial(third_kernel, weight_at),
        shape((shard_rows, width), f32),
        blur_scratch + sum_scratch,
        blur_flops + sum_flops,
        *(at, wb_high, wb_low, wc_high, wc_low, received, model, norm, *halo_of(model), *swaps),
        scalars=1,
    )


def solution(mesh):
    return jax.shard_map(
        body,
        mesh=mesh,
        in_specs=(
            P("visit", "tile", None),
            P(("tile", "visit"), None),
            P("visit", None, None),
            P("visit", None),
        ),
        out_specs=P(("tile", "visit"), None),
        check_vma=False,
    )
```

```python
import functools

import jax
import jax.numpy as jnp
from jax import lax
from jax.experimental import pallas as pl
from jax.experimental.pallas import tpu as pltpu
from jax.sharding import PartitionSpec as P

LANES = 128
BLOCK = 32
WINDOW = 64
TAPS = 32
MARGIN = WINDOW // 4
CHUNK = 4
VMEM_BYTES = 20 * 1024 * 1024


def split(x):
    high = x.astype(jnp.bfloat16)
    low = (x - high.astype(jnp.float32)).astype(jnp.bfloat16)
    return high, low


def dot_t(x, w):
    return lax.dot_general(x, w, (((1,), (1,)), ((), ())), preferred_element_type=jnp.float32)


def dot_split(both, w_high, w_low):
    rows = both.shape[0] // 2
    wide = dot_t(both[...], w_high)
    return wide[:rows] + (wide[rows:] + dot_t(both[pl.ds(0, rows), :], w_low))


def lane_of(shape):
    return lax.broadcasted_iota(jnp.int32, shape, len(shape) - 1)


def column_windows(parts):
    rows = parts[0].shape[0] - 8
    lane = lane_of((rows, LANES))
    shifts = sorted({(MARGIN - BLOCK * j) % LANES for j in range(LANES // BLOCK)})
    rolled = [{shift: pltpu.roll(part, shift, 1) for shift in shifts} for part in parts]
    windows = []
    for j in range(len(parts) * LANES // BLOCK):
        start = BLOCK * j - MARGIN
        first = start // LANES
        cut = (first + 1) * LANES - start

        def piece(slab):
            if slab < 0 or slab >= len(parts):
                return jnp.zeros((rows, LANES), jnp.float32)
            near = rolled[slab][(-start) % LANES][:rows]
            far = rolled[slab][(WINDOW - start) % LANES][8:]
            return jnp.where(lane < WINDOW, near, far)

        window = piece(first)
        if cut < WINDOW:
            window = jnp.where(lane % WINDOW < cut, window, piece(first + 1))
        windows.append(window)
    return windows


def put_field(member, parts, z_ref, sum_rows):
    windows = column_windows(parts)
    for pair in range(len(windows) // 2):
        for group in range(2):
            rows = [window[16 * group : 16 * group + sum_rows] for window in windows[2 * pair : 2 * pair + 2]]
            high, low = split(jnp.concatenate(rows, axis=0))
            lanes = pl.ds((2 * member + group) * LANES, LANES)
            z_ref[pl.ds(2 * pair * sum_rows, 2 * sum_rows), lanes] = high
            z_ref[pl.ds((2 * pair + len(windows)) * sum_rows, 2 * sum_rows), lanes] = low


def gather_taps(t_ref, out_rows):
    sum_rows = out_rows + 8
    lane = lane_of((out_rows, LANES))
    halves = []
    for half in range(t_ref.shape[0] // sum_rows // 4):
        total = None
        for i in range(4):
            picked = None
            for jj in range(4):
                base = (4 * half + jj) * sum_rows + i
                near = t_ref[pl.ds(base, out_rows), pl.ds(0, LANES)]
                far = t_ref[pl.ds(base + 4, out_rows), pl.ds(LANES, LANES)]
                moved = pltpu.roll(near + far, (BLOCK * (jj - i)) % LANES, 1) if jj != i else near + far
                picked = moved if picked is None else jnp.where(lane >= BLOCK * jj, moved, picked)
            total = picked if total is None else total + picked
        halves.append(total)
    return jnp.concatenate(halves, axis=1)


def lay_model(wide, x_ref, shifts):
    slabs = wide.shape[1] // LANES
    blocks = wide.shape[1] // BLOCK
    half = x_ref.shape[0] // 2
    rows = half // blocks
    for s in shifts:
        parts = [wide[pl.ds(s, rows + 24), pl.ds(LANES * i, LANES)] for i in range(slabs)]
        windows = column_windows(parts)
        for j in range(blocks):
            high, low = split(windows[j])
            for group in range(2):
                lanes = pl.ds((2 * s + group) * LANES, LANES)
                x_ref[pl.ds(rows * j, rows), lanes] = high[16 * group : 16 * group + rows]
                x_ref[pl.ds(half + rows * j, rows), lanes] = low[16 * group : 16 * group + rows]


def blur_all(operator_for, wb_high, wb_low, wide, x_ref, g_ref):
    step = 2 * LANES
    depth = x_ref.shape[1] // 2
    for at in range(0, wb_high.shape[0], step):
        members = pl.ds(at, step)
        operator_for(range(at // BLOCK, (at + step) // BLOCK))
        if at == 0:
            for half in range(2):
                lay_model(wide, x_ref, range(4 * half, 4 * half + 4))
                lanes = pl.ds(depth * half, depth)
                part = dot_split(x_ref.at[:, lanes], wb_high[members, lanes], wb_low[members, lanes])
                g_ref[:, members] = part if half == 0 else g_ref[:, members] + part
        else:
            g_ref[:, members] = dot_split(x_ref, wb_high[members, :], wb_low[members, :])


def blurred_parts(g_ref, member, rows, slabs):
    lane = lane_of((rows, LANES))
    place = member % 4
    parts = []
    for slab in range(slabs):
        picked = None
        for jj in range(4):
            block = g_ref[pl.ds((4 * slab + jj) * rows, rows), pl.ds(member // 4 * LANES, LANES)]
            moved = pltpu.roll(block, (BLOCK * (jj - place)) % LANES, 1) if jj != place else block
            picked = moved if picked is None else jnp.where(lane >= BLOCK * jj, moved, picked)
        parts.append(picked)
    return parts


def send_kernel(cover, kernel, counts, out, padded):
    size = kernel.shape[0]
    front = TAPS - size
    padded[...] = jnp.zeros(padded.shape, jnp.float32)
    for row in range(size):
        padded[pl.ds(front + row, 1), pl.ds(front, size)] = kernel[row]
    straight = padded[...]
    straight = straight / jnp.sum(straight)
    table = straight[0:8]
    for q in range(1, TAPS // 8):
        table = table + pltpu.roll(straight[8 * q : 8 * q + 8], TAPS * q, 1)
    row = lax.broadcasted_iota(jnp.int32, table.shape, 0)
    lane = lane_of(table.shape)
    for tile in range(cover.shape[1]):
        spot = (row == tile % 8) & (lane == tile // 8 * TAPS)
        entry = jnp.broadcast_to(cover[0:1, tile : tile + 1].astype(jnp.float32), table.shape)
        table = jnp.where(spot, entry, table)
    slabs = counts.shape[2] // LANES
    own = (out.shape[1] - 8) // slabs
    for peer in range(out.shape[0]):
        for slab in range(slabs):
            out[peer, pl.ds(slab * own, own), :] = counts[0, pl.ds(peer * own, own), pl.ds(slab * LANES, LANES)]
        out[peer, pl.ds(slabs * own, 8), :] = table


def weight_of(member, first_row, tile_rows, tiles, received, rows):
    table_row = received.shape[1] - 8
    row = first_row - TAPS // 2 + lax.broadcasted_iota(jnp.int32, (rows, LANES), 0)
    weight = jnp.zeros((rows, LANES), jnp.float32)
    for tile in range(tiles):
        entry = received[member, pl.ds(table_row + tile % 8, 1), :]
        inside = (row >= tile * tile_rows) & (row < (tile + 1) * tile_rows)
        weight = jnp.where(inside, jnp.broadcast_to(entry[:, tile // 8 * TAPS :][:, 0:1], (rows, LANES)), weight)
    return weight


def update(blurred_of, weight_at, counts_of, model, norm, wc_high, wc_low, z_ref, t_ref, out):
    out_rows = out.shape[0]
    members = z_ref.shape[1] // (4 * WINDOW)
    for first in range(0, members, CHUNK):
        for member in range(first, first + CHUNK):
            weight = weight_at(member)
            parts = []
            for blurred, counts in zip(blurred_of(member), counts_of(member)):
                safe = jnp.where(weight > 0.0, blurred, 1.0)
                parts.append(weight * counts / safe)
            put_field(member, parts, z_ref, out_rows + 8)
        lanes = pl.ds(4 * WINDOW * first, 4 * WINDOW * CHUNK)
        part = dot_split(z_ref.at[:, lanes], wc_high[:, lanes], wc_low[:, lanes])
        t_ref[...] = part if first == 0 else t_ref[...] + part
    out[...] = model * gather_taps(t_ref, out_rows) / norm


def norm_field(first_row, tile_rows, tiles, received, norm):
    out_rows, width = norm.shape
    members = received.shape[0]
    table_row = received.shape[1] - 8
    tables = [
        received[:, pl.ds(table_row, 8), pl.ds(LANES * group, LANES)].reshape(8 * members, LANES) for group in range(2)
    ]
    entry = lax.broadcasted_iota(jnp.int32, (8 * members, 8 * members), 0)
    lane = lane_of((8 * members, 8 * members))
    covers = []
    for tile in range(tiles):
        column = jnp.broadcast_to(tables[tile // 8][:, 0:1], entry.shape)
        spot = entry == lane // 8 * 8 + tile % 8
        covers.append(jnp.sum(jnp.where(spot, column, 0.0), axis=0, keepdims=True))
    row = lax.broadcasted_iota(jnp.int32, (out_rows, 8 * members), 0) + lane_of((out_rows, 8 * members)) % 8
    total = None
    for index in range(4):
        group, half = divmod(index, 2)
        offset = lax.broadcasted_iota(jnp.int32, (LANES, width), 0) - WINDOW * half
        column = lane_of((LANES, width)) + offset - TAPS // 2
        inside = (offset >= 1) & (offset < TAPS) & (column >= 0) & (column < width)
        inside = inside.astype(jnp.bfloat16)
        high, low = split(tables[group])
        sums = jnp.dot(high, inside, preferred_element_type=jnp.float32)
        sums = sums + jnp.dot(low, inside, preferred_element_type=jnp.float32)
        place = row + (first_row - TAPS // 2 + 8 * index)
        weight = jnp.zeros(place.shape, jnp.float32)
        for tile in range(tiles):
            covered = (place >= tile * tile_rows) & (place < (tile + 1) * tile_rows)
            weight = jnp.where(covered, jnp.broadcast_to(covers[tile], place.shape), weight)
        weight = weight.astype(jnp.bfloat16)
        high, low = split(sums)
        part = jnp.dot(weight, high, preferred_element_type=jnp.float32)
        part = part + jnp.dot(weight, low, preferred_element_type=jnp.float32)
        total = part if total is None else total + part
    norm[...] = total


def put_model(refs, at, tall, wide):
    even_swap, own, odd_swap = refs
    rows = own.shape[0]
    tall[pl.ds(rows, rows), :] = own[...]
    tall[pl.ds(pl.multiple_of(2 * rows * (1 - at[0, 2]), rows), rows), :] = even_swap[...]
    tall[pl.ds(pl.multiple_of(2 * rows * at[0, 2], rows), rows), :] = odd_swap[...]
    wide[...] = tall[pl.ds(pl.multiple_of(at[0, 1], 8), wide.shape[0]), :]


def counts_window(at, received, swaps, rows):
    def window(member):
        parts = []
        for first in range(0, received.shape[1] - 8, rows):
            slab = pl.ds(first, rows)
            own = received[member, slab, :]
            before, after = [], []
            for hop in range(len(swaps) // 2):
                even, odd = (ref[member, slab, :] for ref in swaps[2 * hop : 2 * hop + 2])
                is_even = at[0, 3 + hop] == 0
                before.insert(0, jnp.where(is_even, odd, even))
                after.append(jnp.where(is_even, even, odd))
            parts.append(jnp.concatenate(before + [own] + after, axis=0))
        return parts

    return window


def mirror_kernel(received, out):
    members = received.shape[0]
    count = 8 * members
    table = received[:, pl.ds(received.shape[1] - 8, 8), :].reshape(count, LANES)
    high, low = split(table)
    row = lax.broadcasted_iota(jnp.int32, (count, count), 0)
    turn = (lane_of((count, count)) == row // 8 * 8 + (8 - row % 8) % 8).astype(jnp.bfloat16)
    move = functools.partial(jnp.dot, preferred_element_type=jnp.float32)
    turned = [move(turn, part).astype(jnp.bfloat16) for part in (high, low)]
    source = lax.broadcasted_iota(jnp.int32, (LANES, 2 * LANES), 0)
    target = lane_of((LANES, 2 * LANES))
    slot, tap = target // WINDOW, target % TAPS
    mirror = target % WINDOW >= TAPS
    covers = (target % LANES == 0) & (source == target // LANES * TAPS)
    straight = (~mirror & (tap >= 1) & (source == TAPS * slot + tap)) | covers
    mirrored = [mirror & (tap >= 1) & (source == TAPS * (last - slot) + TAPS - tap) for last in (3, 4)]
    picks = [pick.astype(jnp.bfloat16) for pick in (straight, *mirrored)]
    parts = [move(high, picks[0]) + move(low, picks[0])]
    parts += [move(turned[0], pick) + move(turned[1], pick) for pick in picks[1:]]
    first = lax.broadcasted_iota(jnp.int32, parts[0].shape, 0) % 8 == 0
    out[...] = (parts[0] + jnp.where(first, parts[2], parts[1])).reshape(out.shape)


def first_kernel(
    norm_at, at, received, even_swap, own, odd_swap, wb_high, wb_low, wc_high, wc_low, blurred, norm, tall, wide, x_ref, g_ref
):
    members, rows, width = blurred.shape
    table_row = received.shape[1] - 8
    lane = lane_of((8, LANES)) % WINDOW
    used = (lane >= 1) & (lane < TAPS)

    def entry_of(member, group):
        return received[member, pl.ds(table_row, 8), pl.ds(LANES * group, LANES)]

    def band_of(base, s):
        band = jnp.broadcast_to(base[s : s + 1], (BLOCK, LANES))
        return split(pltpu.roll(band, 0, 1, stride=1, stride_axis=0))

    def blur_operator(chosen):
        for member in chosen:
            for group in range(2):
                flipped = jnp.where(used, pltpu.roll(entry_of(member, group), LANES - TAPS, 1), 0.0)
                for s in range(8):
                    spot = (pl.ds(BLOCK * member, BLOCK), pl.ds(LANES * (2 * s + group), LANES))
                    wb_high[spot], wb_low[spot] = band_of(flipped, s)

    put_model((even_swap, own, odd_swap), at, tall, wide)
    blur_all(blur_operator, wb_high, wb_low, wide, x_ref, g_ref)
    for member in range(members):
        for group in range(2):
            straight = jnp.where(used, entry_of(member, group), 0.0)
            for s in range(8):
                spot = (pl.ds(BLOCK * s, BLOCK), pl.ds((2 * member + group) * LANES, LANES))
                wc_high[spot], wc_low[spot] = band_of(straight, s)
    for member in range(members):
        for slab, part in enumerate(blurred_parts(g_ref, member, rows, width // LANES)):
            blurred[member, :, pl.ds(LANES * slab, LANES)] = part
    norm_at(at[0, 0], received=received, norm=norm)


def second_kernel(weight_at, at, wc_high, wc_low, received, blurred, model, norm, *refs):
    swaps, (out, z_ref, t_ref) = refs[:-3], refs[-3:]
    out_rows, width = out.shape

    def blurred_of(member):
        return [blurred[member, :, pl.ds(first, LANES)] for first in range(0, width, LANES)]

    counts_of = counts_window(at, received, swaps, out_rows)
    weight_of_shard = functools.partial(weight_at, first_row=at[0, 0], received=received, rows=out_rows + TAPS)
    update(blurred_of, weight_of_shard, counts_of, model[...], norm[...], wc_high, wc_low, z_ref, t_ref, out)


def third_kernel(weight_at, at, wb_high, wb_low, wc_high, wc_low, received, model, norm, even_swap, own, odd_swap, *refs):
    swaps, (out, tall, wide, x_ref, g_ref, z_ref, t_ref) = refs[:-7], refs[-7:]
    out_rows, width = out.shape
    rows = out_rows + TAPS
    put_model((even_swap, own, odd_swap), at, tall, wide)
    blur_all(lambda chosen: None, wb_high, wb_low, wide, x_ref, g_ref)
    blurred_of = functools.partial(blurred_parts, g_ref, rows=rows, slabs=width // LANES)
    counts_of = counts_window(at, received, swaps, out_rows)
    weight_of_shard = functools.partial(weight_at, first_row=at[0, 0], received=received, rows=rows)
    update(blurred_of, weight_of_shard, counts_of, model[...], norm[...], wc_high, wc_low, z_ref, t_ref, out)


def call(kernel, out_shape, scratch_shapes, flops, *operands, scalars=0):
    whole = pl.BlockSpec(memory_space=pltpu.VMEM)
    scalar = pl.BlockSpec(memory_space=pltpu.SMEM)
    return pl.pallas_call(
        kernel,
        out_shape=out_shape,
        in_specs=[scalar] * scalars + [whole] * (len(operands) - scalars),
        out_specs=jax.tree.map(lambda _: whole, out_shape),
        scratch_shapes=scratch_shapes,
        compiler_params=pltpu.CompilerParams(vmem_limit_bytes=VMEM_BYTES),
        cost_estimate=pl.CostEstimate(flops=flops, bytes_accessed=4 * 1024 * 1024, transcendentals=0),
    )(*operands)


def strip_permute(array, target):
    tiles, members = lax.axis_size("tile"), lax.axis_size("visit")
    count = tiles * members
    place = [i % members * tiles + i // members for i in range(count)]
    pairs = [(place[i], place[target(i)]) for i in range(count) if 0 <= target(i) < count]
    return lax.ppermute(array, ("visit", "tile"), pairs)


def group_gather(array, group):
    return [array] + [strip_permute(array, lambda i: i // group * group + (i + k) % group) for k in range(1, group)]


def group_order(arrays, place):
    ordered = []
    for slot in range(len(arrays)):
        back = (place - slot) % len(arrays)
        picked = arrays[0]
        for k in range(1, len(arrays)):
            picked = jnp.where(back == k, arrays[k], picked)
        ordered.append(picked)
    return ordered


def group_swaps(rows, group):
    def partner(first):
        return lambda i: i + group if i // group % 2 == first else i - group

    return [strip_permute(rows, partner(0)), rows, strip_permute(rows, partner(1))]


def body(exposures, sky_model, blur_kernels, coverage):
    tile_rows, width = exposures.shape[1:]
    shard_rows = sky_model.shape[0]
    members = lax.axis_size("visit")
    tiles = lax.axis_size("tile")
    visit = lax.axis_index("visit")
    group = TAPS // shard_rows
    place = visit % group
    hops = TAPS // 2 // shard_rows
    first_row = lax.axis_index("tile") * tile_rows + visit * shard_rows
    parities = [visit // hop % 2 for hop in [group, *range(1, hops + 1)]]
    at = jnp.stack([first_row, place * shard_rows, *parities]).reshape(1, -1)

    f32, bf16 = jnp.float32, jnp.bfloat16
    shape = jax.ShapeDtypeStruct
    blocks = width // BLOCK
    depth = TAPS * WINDOW
    rows = shard_rows + TAPS

    def halo_of(model):
        mine = jnp.concatenate(group_order(group_gather(model, group), place), axis=0)
        return group_swaps(mine, group)

    sent = call(
        send_kernel,
        shape((members, width // LANES * shard_rows + 8, LANES), f32),
        [pltpu.VMEM((TAPS, LANES), f32)],
        1 << 22,
        *(coverage, jnp.transpose(blur_kernels, (1, 0, 2)), exposures),
    )
    received = lax.all_to_all(sent, "visit", 0, 0)
    received, near = lax.optimization_barrier((received, halo_of(sky_model)))
    swaps = []
    for hop in range(1, hops + 1):
        even, _, odd = group_swaps(received[:, : width // LANES * shard_rows], hop)
        swaps += [even, odd]

    blur_scratch = [
        pltpu.VMEM((3 * TAPS, width), f32),
        pltpu.VMEM((rows + TAPS, width), f32),
        pltpu.VMEM((2 * blocks * rows, depth), bf16),
        pltpu.VMEM((blocks * rows, members * BLOCK), f32),
    ]
    sum_scratch = [
        pltpu.VMEM((2 * blocks * (shard_rows + 8), members * 4 * WINDOW), bf16),
        pltpu.VMEM((blocks * (shard_rows + 8), 8 * BLOCK), f32),
    ]
    blur_flops = 6 * blocks * rows * depth * members * BLOCK
    sum_flops = 6 * blocks * (shard_rows + 8) * members * 4 * WINDOW * 8 * BLOCK
    weight_at = functools.partial(weight_of, tile_rows=tile_rows, tiles=tiles)
    tables = call(mirror_kernel, shape((members, 8, 2 * LANES), f32), [], 1 << 22, received)
    wb_high, wb_low, wc_high, wc_low, blurred, norm = call(
        functools.partial(first_kernel, functools.partial(norm_field, tile_rows=tile_rows, tiles=tiles)),
        (
            shape((members * BLOCK, depth), bf16),
            shape((members * BLOCK, depth), bf16),
            shape((8 * BLOCK, members * 4 * WINDOW), bf16),
            shape((8 * BLOCK, members * 4 * WINDOW), bf16),
            shape((members, rows, width), f32),
            shape((shard_rows, width), f32),
        ),
        blur_scratch,
        blur_flops + sum_flops,
        *(at, tables, *near),
        scalars=1,
    )
    model = call(
        functools.partial(second_kernel, weight_at),
        shape((shard_rows, width), f32),
        sum_scratch,
        sum_flops,
        *(at, wc_high, wc_low, received, blurred, sky_model, norm, *swaps),
        scalars=1,
    )
    return call(
        functools.partial(third_kernel, weight_at),
        shape((shard_rows, width), f32),
        blur_scratch + sum_scratch,
        blur_flops + sum_flops,
        *(at, wb_high, wb_low, wc_high, wc_low, received, model, norm, *halo_of(model), *swaps),
        scalars=1,
    )


def solution(mesh):
    return jax.shard_map(
        body,
        mesh=mesh,
        in_specs=(
            P("visit", "tile", None),
            P(("tile", "visit"), None),
            P("visit", None, None),
            P("visit", None),
        ),
        out_specs=P(("tile", "visit"), None),
        check_vma=False,
    )
```

```python
import functools

import jax
import jax.numpy as jnp
from jax import lax
from jax.experimental import pallas as pl
from jax.experimental.pallas import tpu as pltpu
from jax.sharding import PartitionSpec as P

LANES = 128
BLOCK = 32
WINDOW = 64
TAPS = 32
MARGIN = WINDOW // 4
CHUNK = 2
VMEM_BYTES = 20 * 1024 * 1024


def split(x):
    high = x.astype(jnp.bfloat16)
    low = (x - high.astype(jnp.float32)).astype(jnp.bfloat16)
    return high, low


def dot_t(x, w):
    return lax.dot_general(x, w, (((1,), (1,)), ((), ())), preferred_element_type=jnp.float32)


def dot_split(both, w_high, w_low):
    rows = both.shape[0] // 2
    wide = dot_t(both[...], w_high)
    return wide[:rows] + (wide[rows:] + dot_t(both[pl.ds(0, rows), :], w_low))


def lane_of(shape):
    return lax.broadcasted_iota(jnp.int32, shape, len(shape) - 1)


def column_windows(parts):
    rows = parts[0].shape[0] - 8
    lane = lane_of((rows, LANES))
    shifts = sorted({(MARGIN - BLOCK * j) % LANES for j in range(LANES // BLOCK)})
    rolled = [{shift: pltpu.roll(part, shift, 1) for shift in shifts} for part in parts]
    windows = []
    for j in range(len(parts) * LANES // BLOCK):
        start = BLOCK * j - MARGIN
        first = start // LANES
        cut = (first + 1) * LANES - start

        def piece(slab):
            if slab < 0 or slab >= len(parts):
                return jnp.zeros((rows, LANES), jnp.float32)
            near = rolled[slab][(-start) % LANES][:rows]
            far = rolled[slab][(WINDOW - start) % LANES][8:]
            return jnp.where(lane < WINDOW, near, far)

        window = piece(first)
        if cut < WINDOW:
            window = jnp.where(lane % WINDOW < cut, window, piece(first + 1))
        windows.append(window)
    return windows


def put_field(member, parts, z_ref, sum_rows):
    windows = column_windows(parts)
    for pair in range(len(windows) // 2):
        for group in range(2):
            rows = [window[16 * group : 16 * group + sum_rows] for window in windows[2 * pair : 2 * pair + 2]]
            high, low = split(jnp.concatenate(rows, axis=0))
            lanes = pl.ds((2 * member + group) * LANES, LANES)
            z_ref[pl.ds(2 * pair * sum_rows, 2 * sum_rows), lanes] = high
            z_ref[pl.ds((2 * pair + len(windows)) * sum_rows, 2 * sum_rows), lanes] = low


def gather_taps(t_ref, out_rows):
    sum_rows = out_rows + 8
    lane = lane_of((out_rows, LANES))
    halves = []
    for half in range(t_ref.shape[0] // sum_rows // 4):
        total = None
        for i in range(4):
            picked = None
            for jj in range(4):
                base = (4 * half + jj) * sum_rows + i
                near = t_ref[pl.ds(base, out_rows), pl.ds(0, LANES)]
                far = t_ref[pl.ds(base + 4, out_rows), pl.ds(LANES, LANES)]
                moved = pltpu.roll(near + far, (BLOCK * (jj - i)) % LANES, 1) if jj != i else near + far
                picked = moved if picked is None else jnp.where(lane >= BLOCK * jj, moved, picked)
            total = picked if total is None else total + picked
        halves.append(total)
    return jnp.concatenate(halves, axis=1)


def lay_model(wide, x_ref, shifts):
    slabs = wide.shape[1] // LANES
    blocks = wide.shape[1] // BLOCK
    half = x_ref.shape[0] // 2
    rows = half // blocks
    for s in shifts:
        parts = [wide[pl.ds(s, rows + 24), pl.ds(LANES * i, LANES)] for i in range(slabs)]
        windows = column_windows(parts)
        for j in range(blocks):
            high, low = split(windows[j])
            for group in range(2):
                lanes = pl.ds((2 * s + group) * LANES, LANES)
                x_ref[pl.ds(rows * j, rows), lanes] = high[16 * group : 16 * group + rows]
                x_ref[pl.ds(half + rows * j, rows), lanes] = low[16 * group : 16 * group + rows]


def blur_all(operator_for, wb_high, wb_low, wide, x_ref, g_ref):
    step = 2 * LANES
    depth = x_ref.shape[1] // 4
    for at in range(0, wb_high.shape[0], step):
        members = pl.ds(at, step)
        operator_for(range(at // BLOCK, (at + step) // BLOCK))
        if at == 0:
            for part in range(4):
                lay_model(wide, x_ref, range(2 * part, 2 * part + 2))
                lanes = pl.ds(depth * part, depth)
                product = dot_split(x_ref.at[:, lanes], wb_high[members, lanes], wb_low[members, lanes])
                g_ref[:, members] = product if part == 0 else g_ref[:, members] + product
        else:
            g_ref[:, members] = dot_split(x_ref, wb_high[members, :], wb_low[members, :])


def blurred_parts(g_ref, member, rows, slabs):
    lane = lane_of((rows, LANES))
    place = member % 4
    parts = []
    for slab in range(slabs):
        picked = None
        for jj in range(4):
            block = g_ref[pl.ds((4 * slab + jj) * rows, rows), pl.ds(member // 4 * LANES, LANES)]
            moved = pltpu.roll(block, (BLOCK * (jj - place)) % LANES, 1) if jj != place else block
            picked = moved if picked is None else jnp.where(lane >= BLOCK * jj, moved, picked)
        parts.append(picked)
    return parts


def send_kernel(cover, kernel, counts, out, padded):
    size = kernel.shape[0]
    front = TAPS - size
    padded[...] = jnp.zeros(padded.shape, jnp.float32)
    for row in range(size):
        padded[pl.ds(front + row, 1), pl.ds(front, size)] = kernel[row]
    straight = padded[...]
    straight = straight / jnp.sum(straight)
    table = straight[0:8]
    for q in range(1, TAPS // 8):
        table = table + pltpu.roll(straight[8 * q : 8 * q + 8], TAPS * q, 1)
    row = lax.broadcasted_iota(jnp.int32, table.shape, 0)
    lane = lane_of(table.shape)
    for tile in range(cover.shape[1]):
        spot = (row == tile % 8) & (lane == tile // 8 * TAPS)
        entry = jnp.broadcast_to(cover[0:1, tile : tile + 1].astype(jnp.float32), table.shape)
        table = jnp.where(spot, entry, table)
    slabs = counts.shape[2] // LANES
    own = (out.shape[1] - 8) // slabs
    for peer in range(out.shape[0]):
        for slab in range(slabs):
            out[peer, pl.ds(slab * own, own), :] = counts[0, pl.ds(peer * own, own), pl.ds(slab * LANES, LANES)]
        out[peer, pl.ds(slabs * own, 8), :] = table


def weight_of(member, first_row, tile_rows, tiles, received, rows):
    table_row = received.shape[1] - 8
    row = first_row - TAPS // 2 + lax.broadcasted_iota(jnp.int32, (rows, LANES), 0)
    weight = jnp.zeros((rows, LANES), jnp.float32)
    for tile in range(tiles):
        entry = received[member, pl.ds(table_row + tile % 8, 1), :]
        inside = (row >= tile * tile_rows) & (row < (tile + 1) * tile_rows)
        weight = jnp.where(inside, jnp.broadcast_to(entry[:, tile // 8 * TAPS :][:, 0:1], (rows, LANES)), weight)
    return weight


def update(blurred_of, weight_at, counts_of, model, norm, wc_high, wc_low, z_ref, t_ref, out):
    out_rows = out.shape[0]
    members = z_ref.shape[1] // (4 * WINDOW)
    for first in range(0, members, CHUNK):
        for member in range(first, first + CHUNK):
            weight = weight_at(member)
            parts = []
            for blurred, counts in zip(blurred_of(member), counts_of(member)):
                safe = jnp.where(weight > 0.0, blurred, 1.0)
                parts.append(weight * counts / safe)
            put_field(member, parts, z_ref, out_rows + 8)
        lanes = pl.ds(4 * WINDOW * first, 4 * WINDOW * CHUNK)
        part = dot_split(z_ref.at[:, lanes], wc_high[:, lanes], wc_low[:, lanes])
        t_ref[...] = part if first == 0 else t_ref[...] + part
    out[...] = model * gather_taps(t_ref, out_rows) / norm


def norm_field(first_row, tile_rows, tiles, received, norm):
    out_rows, width = norm.shape
    members = received.shape[0]
    table_row = received.shape[1] - 8
    tables = [
        received[:, pl.ds(table_row, 8), pl.ds(LANES * group, LANES)].reshape(8 * members, LANES) for group in range(2)
    ]
    entry = lax.broadcasted_iota(jnp.int32, (8 * members, 8 * members), 0)
    lane = lane_of((8 * members, 8 * members))
    covers = []
    for tile in range(tiles):
        column = jnp.broadcast_to(tables[tile // 8][:, 0:1], entry.shape)
        spot = entry == lane // 8 * 8 + tile % 8
        covers.append(jnp.sum(jnp.where(spot, column, 0.0), axis=0, keepdims=True))
    row = lax.broadcasted_iota(jnp.int32, (out_rows, 8 * members), 0) + lane_of((out_rows, 8 * members)) % 8
    total = None
    for index in range(4):
        group, half = divmod(index, 2)
        offset = lax.broadcasted_iota(jnp.int32, (LANES, width), 0) - WINDOW * half
        column = lane_of((LANES, width)) + offset - TAPS // 2
        inside = (offset >= 1) & (offset < TAPS) & (column >= 0) & (column < width)
        inside = inside.astype(jnp.bfloat16)
        high, low = split(tables[group])
        sums = jnp.dot(high, inside, preferred_element_type=jnp.float32)
        sums = sums + jnp.dot(low, inside, preferred_element_type=jnp.float32)
        place = row + (first_row - TAPS // 2 + 8 * index)
        weight = jnp.zeros(place.shape, jnp.float32)
        for tile in range(tiles):
            covered = (place >= tile * tile_rows) & (place < (tile + 1) * tile_rows)
            weight = jnp.where(covered, jnp.broadcast_to(covers[tile], place.shape), weight)
        weight = weight.astype(jnp.bfloat16)
        high, low = split(sums)
        part = jnp.dot(weight, high, preferred_element_type=jnp.float32)
        part = part + jnp.dot(weight, low, preferred_element_type=jnp.float32)
        total = part if total is None else total + part
    norm[...] = total


def put_model(refs, at, tall, wide):
    even_swap, own, odd_swap = refs
    rows = own.shape[0]
    tall[pl.ds(rows, rows), :] = own[...]
    tall[pl.ds(pl.multiple_of(2 * rows * (1 - at[0, 2]), rows), rows), :] = even_swap[...]
    tall[pl.ds(pl.multiple_of(2 * rows * at[0, 2], rows), rows), :] = odd_swap[...]
    wide[...] = tall[pl.ds(pl.multiple_of(at[0, 1], 8), wide.shape[0]), :]


def counts_window(at, received, swaps, rows):
    def window(member):
        parts = []
        for first in range(0, received.shape[1] - 8, rows):
            slab = pl.ds(first, rows)
            own = received[member, slab, :]
            before, after = [], []
            for hop in range(len(swaps) // 2):
                even, odd = (ref[member, slab, :] for ref in swaps[2 * hop : 2 * hop + 2])
                is_even = at[0, 3 + hop] == 0
                before.insert(0, jnp.where(is_even, odd, even))
                after.append(jnp.where(is_even, even, odd))
            parts.append(jnp.concatenate(before + [own] + after, axis=0))
        return parts

    return window


def mirror_kernel(received, out):
    members = received.shape[0]
    count = 8 * members
    table = received[:, pl.ds(received.shape[1] - 8, 8), :].reshape(count, LANES)
    high, low = split(table)
    row = lax.broadcasted_iota(jnp.int32, (count, count), 0)
    turn = (lane_of((count, count)) == row // 8 * 8 + (8 - row % 8) % 8).astype(jnp.bfloat16)
    move = functools.partial(jnp.dot, preferred_element_type=jnp.float32)
    turned = [move(turn, part).astype(jnp.bfloat16) for part in (high, low)]
    source = lax.broadcasted_iota(jnp.int32, (LANES, 2 * LANES), 0)
    target = lane_of((LANES, 2 * LANES))
    slot, tap = target // WINDOW, target % TAPS
    mirror = target % WINDOW >= TAPS
    covers = (target % LANES == 0) & (source == target // LANES * TAPS)
    straight = (~mirror & (tap >= 1) & (source == TAPS * slot + tap)) | covers
    mirrored = [mirror & (tap >= 1) & (source == TAPS * (last - slot) + TAPS - tap) for last in (3, 4)]
    picks = [pick.astype(jnp.bfloat16) for pick in (straight, *mirrored)]
    parts = [move(high, picks[0]) + move(low, picks[0])]
    parts += [move(turned[0], pick) + move(turned[1], pick) for pick in picks[1:]]
    first = lax.broadcasted_iota(jnp.int32, parts[0].shape, 0) % 8 == 0
    out[...] = (parts[0] + jnp.where(first, parts[2], parts[1])).reshape(out.shape)


def first_kernel(
    norm_at, at, received, even_swap, own, odd_swap, wb_high, wb_low, wc_high, wc_low, blurred, norm, tall, wide, x_ref, g_ref
):
    members, rows, width = blurred.shape
    table_row = received.shape[1] - 8
    lane = lane_of((8, LANES)) % WINDOW
    used = (lane >= 1) & (lane < TAPS)

    def entry_of(member, group):
        return received[member, pl.ds(table_row, 8), pl.ds(LANES * group, LANES)]

    def band_of(base, s):
        band = jnp.broadcast_to(base[s : s + 1], (BLOCK, LANES))
        return split(pltpu.roll(band, 0, 1, stride=1, stride_axis=0))

    def blur_operator(chosen):
        for member in chosen:
            for group in range(2):
                flipped = jnp.where(used, pltpu.roll(entry_of(member, group), LANES - TAPS, 1), 0.0)
                for s in range(8):
                    spot = (pl.ds(BLOCK * member, BLOCK), pl.ds(LANES * (2 * s + group), LANES))
                    wb_high[spot], wb_low[spot] = band_of(flipped, s)

    put_model((even_swap, own, odd_swap), at, tall, wide)
    blur_all(blur_operator, wb_high, wb_low, wide, x_ref, g_ref)
    for member in range(members):
        for group in range(2):
            straight = jnp.where(used, entry_of(member, group), 0.0)
            for s in range(8):
                spot = (pl.ds(BLOCK * s, BLOCK), pl.ds((2 * member + group) * LANES, LANES))
                wc_high[spot], wc_low[spot] = band_of(straight, s)
    for member in range(members):
        for slab, part in enumerate(blurred_parts(g_ref, member, rows, width // LANES)):
            blurred[member, :, pl.ds(LANES * slab, LANES)] = part
    norm_at(at[0, 0], received=received, norm=norm)


def second_kernel(weight_at, at, wc_high, wc_low, received, blurred, model, norm, *refs):
    swaps, (out, z_ref, t_ref) = refs[:-3], refs[-3:]
    out_rows, width = out.shape

    def blurred_of(member):
        return [blurred[member, :, pl.ds(first, LANES)] for first in range(0, width, LANES)]

    counts_of = counts_window(at, received, swaps, out_rows)
    weight_of_shard = functools.partial(weight_at, first_row=at[0, 0], received=received, rows=out_rows + TAPS)
    update(blurred_of, weight_of_shard, counts_of, model[...], norm[...], wc_high, wc_low, z_ref, t_ref, out)


def third_kernel(weight_at, at, wb_high, wb_low, wc_high, wc_low, received, model, norm, even_swap, own, odd_swap, *refs):
    swaps, (out, tall, wide, x_ref, g_ref, z_ref, t_ref) = refs[:-7], refs[-7:]
    out_rows, width = out.shape
    rows = out_rows + TAPS
    put_model((even_swap, own, odd_swap), at, tall, wide)
    blur_all(lambda chosen: None, wb_high, wb_low, wide, x_ref, g_ref)
    blurred_of = functools.partial(blurred_parts, g_ref, rows=rows, slabs=width // LANES)
    counts_of = counts_window(at, received, swaps, out_rows)
    weight_of_shard = functools.partial(weight_at, first_row=at[0, 0], received=received, rows=rows)
    update(blurred_of, weight_of_shard, counts_of, model[...], norm[...], wc_high, wc_low, z_ref, t_ref, out)


def call(kernel, out_shape, scratch_shapes, flops, *operands, scalars=0):
    whole = pl.BlockSpec(memory_space=pltpu.VMEM)
    scalar = pl.BlockSpec(memory_space=pltpu.SMEM)
    return pl.pallas_call(
        kernel,
        out_shape=out_shape,
        in_specs=[scalar] * scalars + [whole] * (len(operands) - scalars),
        out_specs=jax.tree.map(lambda _: whole, out_shape),
        scratch_shapes=scratch_shapes,
        compiler_params=pltpu.CompilerParams(vmem_limit_bytes=VMEM_BYTES),
        cost_estimate=pl.CostEstimate(flops=flops, bytes_accessed=4 * 1024 * 1024, transcendentals=0),
    )(*operands)


def strip_permute(array, target):
    tiles, members = lax.axis_size("tile"), lax.axis_size("visit")
    count = tiles * members
    place = [i % members * tiles + i // members for i in range(count)]
    pairs = [(place[i], place[target(i)]) for i in range(count) if 0 <= target(i) < count]
    return lax.ppermute(array, ("visit", "tile"), pairs)


def group_gather(array, group):
    return [array] + [strip_permute(array, lambda i: i // group * group + (i + k) % group) for k in range(1, group)]


def group_order(arrays, place):
    ordered = []
    for slot in range(len(arrays)):
        back = (place - slot) % len(arrays)
        picked = arrays[0]
        for k in range(1, len(arrays)):
            picked = jnp.where(back == k, arrays[k], picked)
        ordered.append(picked)
    return ordered


def group_swaps(rows, group):
    def partner(first):
        return lambda i: i + group if i // group % 2 == first else i - group

    return [strip_permute(rows, partner(0)), rows, strip_permute(rows, partner(1))]


def body(exposures, sky_model, blur_kernels, coverage):
    tile_rows, width = exposures.shape[1:]
    shard_rows = sky_model.shape[0]
    members = lax.axis_size("visit")
    tiles = lax.axis_size("tile")
    visit = lax.axis_index("visit")
    group = TAPS // shard_rows
    place = visit % group
    hops = TAPS // 2 // shard_rows
    first_row = lax.axis_index("tile") * tile_rows + visit * shard_rows
    parities = [visit // hop % 2 for hop in [group, *range(1, hops + 1)]]
    at = jnp.stack([first_row, place * shard_rows, *parities]).reshape(1, -1)

    f32, bf16 = jnp.float32, jnp.bfloat16
    shape = jax.ShapeDtypeStruct
    blocks = width // BLOCK
    depth = TAPS * WINDOW
    rows = shard_rows + TAPS

    def halo_of(model):
        mine = jnp.concatenate(group_order(group_gather(model, group), place), axis=0)
        return group_swaps(mine, group)

    sent = call(
        send_kernel,
        shape((members, width // LANES * shard_rows + 8, LANES), f32),
        [pltpu.VMEM((TAPS, LANES), f32)],
        1 << 22,
        *(coverage, jnp.transpose(blur_kernels, (1, 0, 2)), exposures),
    )
    received = lax.all_to_all(sent, "visit", 0, 0)
    received, near = lax.optimization_barrier((received, halo_of(sky_model)))
    swaps = []
    for hop in range(1, hops + 1):
        even, _, odd = group_swaps(received[:, : width // LANES * shard_rows], hop)
        swaps += [even, odd]

    blur_scratch = [
        pltpu.VMEM((3 * TAPS, width), f32),
        pltpu.VMEM((rows + TAPS, width), f32),
        pltpu.VMEM((2 * blocks * rows, depth), bf16),
        pltpu.VMEM((blocks * rows, members * BLOCK), f32),
    ]
    sum_scratch = [
        pltpu.VMEM((2 * blocks * (shard_rows + 8), members * 4 * WINDOW), bf16),
        pltpu.VMEM((blocks * (shard_rows + 8), 8 * BLOCK), f32),
    ]
    blur_flops = 6 * blocks * rows * depth * members * BLOCK
    sum_flops = 6 * blocks * (shard_rows + 8) * members * 4 * WINDOW * 8 * BLOCK
    weight_at = functools.partial(weight_of, tile_rows=tile_rows, tiles=tiles)
    tables = call(mirror_kernel, shape((members, 8, 2 * LANES), f32), [], 1 << 22, received)
    wb_high, wb_low, wc_high, wc_low, blurred, norm = call(
        functools.partial(first_kernel, functools.partial(norm_field, tile_rows=tile_rows, tiles=tiles)),
        (
            shape((members * BLOCK, depth), bf16),
            shape((members * BLOCK, depth), bf16),
            shape((8 * BLOCK, members * 4 * WINDOW), bf16),
            shape((8 * BLOCK, members * 4 * WINDOW), bf16),
            shape((members, rows, width), f32),
            shape((shard_rows, width), f32),
        ),
        blur_scratch,
        blur_flops + sum_flops,
        *(at, tables, *near),
        scalars=1,
    )
    model = call(
        functools.partial(second_kernel, weight_at),
        shape((shard_rows, width), f32),
        sum_scratch,
        sum_flops,
        *(at, wc_high, wc_low, received, blurred, sky_model, norm, *swaps),
        scalars=1,
    )
    return call(
        functools.partial(third_kernel, weight_at),
        shape((shard_rows, width), f32),
        blur_scratch + sum_scratch,
        blur_flops + sum_flops,
        *(at, wb_high, wb_low, wc_high, wc_low, received, model, norm, *halo_of(model), *swaps),
        scalars=1,
    )


def solution(mesh):
    return jax.shard_map(
        body,
        mesh=mesh,
        in_specs=(
            P("visit", "tile", None),
            P(("tile", "visit"), None),
            P("visit", None, None),
            P("visit", None),
        ),
        out_specs=P(("tile", "visit"), None),
        check_vma=False,
    )
```

```python
import functools

import jax
import jax.numpy as jnp
from jax import lax
from jax.experimental import pallas as pl
from jax.experimental.pallas import tpu as pltpu
from jax.sharding import PartitionSpec as P

LANES = 128
BLOCK = 32
WINDOW = 64
TAPS = 32
MARGIN = WINDOW // 4
CHUNK = 4
VMEM_BYTES = 20 * 1024 * 1024


def split(x):
    high = x.astype(jnp.bfloat16)
    low = (x - high.astype(jnp.float32)).astype(jnp.bfloat16)
    return high, low


def dot_t(x, w):
    return lax.dot_general(x, w, (((1,), (1,)), ((), ())), preferred_element_type=jnp.float32)


def dot_split(both, w_high, w_low):
    rows = both.shape[0] // 2
    wide = dot_t(both[...], w_high)
    return wide[:rows] + (wide[rows:] + dot_t(both[pl.ds(0, rows), :], w_low))


def lane_of(shape):
    return lax.broadcasted_iota(jnp.int32, shape, len(shape) - 1)


def column_windows(parts):
    rows = parts[0].shape[0] - 8
    lane = lane_of((rows, LANES))
    shifts = sorted({(MARGIN - BLOCK * j) % LANES for j in range(LANES // BLOCK)})
    rolled = [{shift: pltpu.roll(part, shift, 1) for shift in shifts} for part in parts]
    windows = []
    for j in range(len(parts) * LANES // BLOCK):
        start = BLOCK * j - MARGIN
        first = start // LANES
        cut = (first + 1) * LANES - start

        def piece(slab):
            if slab < 0 or slab >= len(parts):
                return jnp.zeros((rows, LANES), jnp.float32)
            near = rolled[slab][(-start) % LANES][:rows]
            far = rolled[slab][(WINDOW - start) % LANES][8:]
            return jnp.where(lane < WINDOW, near, far)

        window = piece(first)
        if cut < WINDOW:
            window = jnp.where(lane % WINDOW < cut, window, piece(first + 1))
        windows.append(window)
    return windows


def put_field(member, parts, z_ref, sum_rows):
    windows = column_windows(parts)
    for pair in range(len(windows) // 2):
        for group in range(2):
            rows = [window[16 * group : 16 * group + sum_rows] for window in windows[2 * pair : 2 * pair + 2]]
            high, low = split(jnp.concatenate(rows, axis=0))
            lanes = pl.ds((2 * member + group) * LANES, LANES)
            z_ref[pl.ds(2 * pair * sum_rows, 2 * sum_rows), lanes] = high
            z_ref[pl.ds((2 * pair + len(windows)) * sum_rows, 2 * sum_rows), lanes] = low


def gather_taps(t_ref, out_rows):
    sum_rows = out_rows + 8
    lane = lane_of((out_rows, LANES))
    halves = []
    for half in range(t_ref.shape[0] // sum_rows // 4):
        total = None
        for i in range(4):
            picked = None
            for jj in range(4):
                base = (4 * half + jj) * sum_rows + i
                near = t_ref[pl.ds(base, out_rows), pl.ds(0, LANES)]
                far = t_ref[pl.ds(base + 4, out_rows), pl.ds(LANES, LANES)]
                moved = pltpu.roll(near + far, (BLOCK * (jj - i)) % LANES, 1) if jj != i else near + far
                picked = moved if picked is None else jnp.where(lane >= BLOCK * jj, moved, picked)
            total = picked if total is None else total + picked
        halves.append(total)
    return jnp.concatenate(halves, axis=1)


def lay_model(wide, x_ref, shifts):
    slabs = wide.shape[1] // LANES
    blocks = wide.shape[1] // BLOCK
    half = x_ref.shape[0] // 2
    rows = half // blocks
    for s in shifts:
        parts = [wide[pl.ds(s, rows + 24), pl.ds(LANES * i, LANES)] for i in range(slabs)]
        windows = column_windows(parts)
        for j in range(blocks):
            high, low = split(windows[j])
            for group in range(2):
                lanes = pl.ds((2 * s + group) * LANES, LANES)
                x_ref[pl.ds(rows * j, rows), lanes] = high[16 * group : 16 * group + rows]
                x_ref[pl.ds(half + rows * j, rows), lanes] = low[16 * group : 16 * group + rows]


def blur_all(operator_for, wb_high, wb_low, wide, x_ref, g_ref):
    step = 2 * LANES
    depth = x_ref.shape[1] // 2
    for at in range(0, wb_high.shape[0], step):
        members = pl.ds(at, step)
        operator_for(range(at // BLOCK, (at + step) // BLOCK))
        if at == 0:
            for half in range(2):
                lay_model(wide, x_ref, range(4 * half, 4 * half + 4))
                lanes = pl.ds(depth * half, depth)
                part = dot_split(x_ref.at[:, lanes], wb_high[members, lanes], wb_low[members, lanes])
                g_ref[:, members] = part if half == 0 else g_ref[:, members] + part
        else:
            g_ref[:, members] = dot_split(x_ref, wb_high[members, :], wb_low[members, :])


def blurred_parts(g_ref, member, rows, slabs):
    lane = lane_of((rows, LANES))
    place = member % 4
    parts = []
    for slab in range(slabs):
        picked = None
        for jj in range(4):
            block = g_ref[pl.ds((4 * slab + jj) * rows, rows), pl.ds(member // 4 * LANES, LANES)]
            moved = pltpu.roll(block, (BLOCK * (jj - place)) % LANES, 1) if jj != place else block
            picked = moved if picked is None else jnp.where(lane >= BLOCK * jj, moved, picked)
        parts.append(picked)
    return parts


def send_kernel(cover, kernel, counts, out, padded):
    size = kernel.shape[0]
    front = TAPS - size
    padded[...] = jnp.zeros(padded.shape, jnp.float32)
    for row in range(size):
        padded[pl.ds(front + row, 1), pl.ds(front, size)] = kernel[row]
    straight = padded[...]
    straight = straight / jnp.sum(straight)
    table = straight[0:8]
    for q in range(1, TAPS // 8):
        table = table + pltpu.roll(straight[8 * q : 8 * q + 8], TAPS * q, 1)
    row = lax.broadcasted_iota(jnp.int32, table.shape, 0)
    lane = lane_of(table.shape)
    for tile in range(cover.shape[1]):
        spot = (row == tile % 8) & (lane == tile // 8 * TAPS)
        entry = jnp.broadcast_to(cover[0:1, tile : tile + 1].astype(jnp.float32), table.shape)
        table = jnp.where(spot, entry, table)
    slabs = counts.shape[2] // LANES
    own = (out.shape[1] - 8) // slabs
    for peer in range(out.shape[0]):
        for slab in range(slabs):
            out[peer, pl.ds(slab * own, own), :] = counts[0, pl.ds(peer * own, own), pl.ds(slab * LANES, LANES)]
        out[peer, pl.ds(slabs * own, 8), :] = table


def weight_of(member, first_row, tile_rows, tiles, received, rows):
    table_row = received.shape[1] - 8
    row = first_row - TAPS // 2 + lax.broadcasted_iota(jnp.int32, (rows, LANES), 0)
    weight = jnp.zeros((rows, LANES), jnp.float32)
    for tile in range(tiles):
        entry = received[member, pl.ds(table_row + tile % 8, 1), :]
        inside = (row >= tile * tile_rows) & (row < (tile + 1) * tile_rows)
        weight = jnp.where(inside, jnp.broadcast_to(entry[:, tile // 8 * TAPS :][:, 0:1], (rows, LANES)), weight)
    return weight


def update(blurred_of, weight_at, counts_of, model, norm, wc_high, wc_low, z_ref, t_ref, out):
    out_rows = out.shape[0]
    members = z_ref.shape[1] // (4 * WINDOW)
    for first in range(0, members, CHUNK):
        for member in range(first, first + CHUNK):
            weight = weight_at(member)
            parts = []
            for blurred, counts in zip(blurred_of(member), counts_of(member)):
                safe = jnp.where(weight > 0.0, blurred, 1.0)
                parts.append(weight * counts / safe)
            put_field(member, parts, z_ref, out_rows + 8)
        lanes = pl.ds(4 * WINDOW * first, 4 * WINDOW * CHUNK)
        part = dot_split(z_ref.at[:, lanes], wc_high[:, lanes], wc_low[:, lanes])
        t_ref[...] = part if first == 0 else t_ref[...] + part
    out[...] = model * gather_taps(t_ref, out_rows) / norm


def norm_field(first_row, tile_rows, tiles, received, norm):
    out_rows, width = norm.shape
    members = received.shape[0]
    table_row = received.shape[1] - 8
    tables = [
        received[:, pl.ds(table_row, 8), pl.ds(LANES * group, LANES)].reshape(8 * members, LANES) for group in range(2)
    ]
    entry = lax.broadcasted_iota(jnp.int32, (8 * members, 8 * members), 0)
    lane = lane_of((8 * members, 8 * members))
    covers = []
    for tile in range(tiles):
        column = jnp.broadcast_to(tables[tile // 8][:, 0:1], entry.shape)
        spot = entry == lane // 8 * 8 + tile % 8
        covers.append(jnp.sum(jnp.where(spot, column, 0.0), axis=0, keepdims=True))
    row = lax.broadcasted_iota(jnp.int32, (out_rows, 8 * members), 0) + lane_of((out_rows, 8 * members)) % 8
    total = None
    for index in range(4):
        group, half = divmod(index, 2)
        offset = lax.broadcasted_iota(jnp.int32, (LANES, width), 0) - WINDOW * half
        column = lane_of((LANES, width)) + offset - TAPS // 2
        inside = (offset >= 1) & (offset < TAPS) & (column >= 0) & (column < width)
        inside = inside.astype(jnp.bfloat16)
        high, low = split(tables[group])
        sums = jnp.dot(high, inside, preferred_element_type=jnp.float32)
        sums = sums + jnp.dot(low, inside, preferred_element_type=jnp.float32)
        place = row + (first_row - TAPS // 2 + 8 * index)
        weight = jnp.zeros(place.shape, jnp.float32)
        for tile in range(tiles):
            covered = (place >= tile * tile_rows) & (place < (tile + 1) * tile_rows)
            weight = jnp.where(covered, jnp.broadcast_to(covers[tile], place.shape), weight)
        weight = weight.astype(jnp.bfloat16)
        high, low = split(sums)
        part = jnp.dot(weight, high, preferred_element_type=jnp.float32)
        part = part + jnp.dot(weight, low, preferred_element_type=jnp.float32)
        total = part if total is None else total + part
    norm[...] = total


def put_model(refs, at, tall, wide):
    even_swap, own, odd_swap = refs
    rows = own.shape[0]
    tall[pl.ds(rows, rows), :] = own[...]
    tall[pl.ds(pl.multiple_of(2 * rows * (1 - at[0, 2]), rows), rows), :] = even_swap[...]
    tall[pl.ds(pl.multiple_of(2 * rows * at[0, 2], rows), rows), :] = odd_swap[...]
    wide[...] = tall[pl.ds(pl.multiple_of(at[0, 1], 8), wide.shape[0]), :]


def counts_window(at, received, swaps, rows):
    def window(member):
        parts = []
        for first in range(0, received.shape[1] - 8, rows):
            slab = pl.ds(first, rows)
            own = received[member, slab, :]
            before, after = [], []
            for hop in range(len(swaps) // 2):
                even, odd = (ref[member, slab, :] for ref in swaps[2 * hop : 2 * hop + 2])
                is_even = at[0, 3 + hop] == 0
                before.insert(0, jnp.where(is_even, odd, even))
                after.append(jnp.where(is_even, even, odd))
            parts.append(jnp.concatenate(before + [own] + after, axis=0))
        return parts

    return window


def mirror_kernel(received, out):
    members = received.shape[0]
    count = 8 * members
    table = received[:, pl.ds(received.shape[1] - 8, 8), :].reshape(count, LANES)
    high, low = split(table)
    row = lax.broadcasted_iota(jnp.int32, (count, count), 0)
    turn = (lane_of((count, count)) == row // 8 * 8 + (8 - row % 8) % 8).astype(jnp.bfloat16)
    move = functools.partial(jnp.dot, preferred_element_type=jnp.float32)
    turned = [move(turn, part).astype(jnp.bfloat16) for part in (high, low)]
    source = lax.broadcasted_iota(jnp.int32, (LANES, 2 * LANES), 0)
    target = lane_of((LANES, 2 * LANES))
    slot, tap = target // WINDOW, target % TAPS
    mirror = target % WINDOW >= TAPS
    covers = (target % LANES == 0) & (source == target // LANES * TAPS)
    straight = (~mirror & (tap >= 1) & (source == TAPS * slot + tap)) | covers
    mirrored = [mirror & (tap >= 1) & (source == TAPS * (last - slot) + TAPS - tap) for last in (3, 4)]
    picks = [pick.astype(jnp.bfloat16) for pick in (straight, *mirrored)]
    parts = [move(high, picks[0]) + move(low, picks[0])]
    parts += [move(turned[0], pick) + move(turned[1], pick) for pick in picks[1:]]
    first = lax.broadcasted_iota(jnp.int32, parts[0].shape, 0) % 8 == 0
    out[...] = (parts[0] + jnp.where(first, parts[2], parts[1])).reshape(out.shape)


def first_kernel(
    norm_at, at, received, even_swap, own, odd_swap, wb_high, wb_low, wc_high, wc_low, blurred, norm, tall, wide, x_ref, g_ref
):
    members, rows, width = blurred.shape
    table_row = received.shape[1] - 8
    lane = lane_of((8, LANES)) % WINDOW
    used = (lane >= 1) & (lane < TAPS)

    def entry_of(member, group):
        return received[member, pl.ds(table_row, 8), pl.ds(LANES * group, LANES)]

    def band_of(base, s):
        band = jnp.broadcast_to(base[s : s + 1], (BLOCK, LANES))
        return split(pltpu.roll(band, 0, 1, stride=1, stride_axis=0))

    def blur_operator(chosen):
        for member in chosen:
            for group in range(2):
                flipped = jnp.where(used, pltpu.roll(entry_of(member, group), LANES - TAPS, 1), 0.0)
                for s in range(8):
                    spot = (pl.ds(BLOCK * member, BLOCK), pl.ds(LANES * (2 * s + group), LANES))
                    wb_high[spot], wb_low[spot] = band_of(flipped, s)

    put_model((even_swap, own, odd_swap), at, tall, wide)
    blur_all(blur_operator, wb_high, wb_low, wide, x_ref, g_ref)
    for member in range(members):
        for group in range(2):
            straight = jnp.where(used, entry_of(member, group), 0.0)
            for s in range(8):
                spot = (pl.ds(BLOCK * s, BLOCK), pl.ds((2 * member + group) * LANES, LANES))
                wc_high[spot], wc_low[spot] = band_of(straight, s)
    for member in range(members):
        for slab, part in enumerate(blurred_parts(g_ref, member, rows, width // LANES)):
            blurred[member, :, pl.ds(LANES * slab, LANES)] = part
    norm_at(at[0, 0], received=received, norm=norm)


def second_kernel(weight_at, at, wc_high, wc_low, received, blurred, model, norm, *refs):
    swaps, (out, z_ref, t_ref) = refs[:-3], refs[-3:]
    out_rows, width = out.shape

    def blurred_of(member):
        return [blurred[member, :, pl.ds(first, LANES)] for first in range(0, width, LANES)]

    counts_of = counts_window(at, received, swaps, out_rows)
    weight_of_shard = functools.partial(weight_at, first_row=at[0, 0], received=received, rows=out_rows + TAPS)
    update(blurred_of, weight_of_shard, counts_of, model[...], norm[...], wc_high, wc_low, z_ref, t_ref, out)


def third_kernel(weight_at, at, wb_high, wb_low, wc_high, wc_low, received, model, norm, even_swap, own, odd_swap, *refs):
    swaps, (out, tall, wide, x_ref, g_ref, z_ref, t_ref) = refs[:-7], refs[-7:]
    out_rows, width = out.shape
    rows = out_rows + TAPS
    put_model((even_swap, own, odd_swap), at, tall, wide)
    blur_all(lambda chosen: None, wb_high, wb_low, wide, x_ref, g_ref)
    blurred_of = functools.partial(blurred_parts, g_ref, rows=rows, slabs=width // LANES)
    counts_of = counts_window(at, received, swaps, out_rows)
    weight_of_shard = functools.partial(weight_at, first_row=at[0, 0], received=received, rows=rows)
    update(blurred_of, weight_of_shard, counts_of, model[...], norm[...], wc_high, wc_low, z_ref, t_ref, out)


def call(kernel, out_shape, scratch_shapes, flops, *operands, scalars=0):
    whole = pl.BlockSpec(memory_space=pltpu.VMEM)
    scalar = pl.BlockSpec(memory_space=pltpu.SMEM)
    return pl.pallas_call(
        kernel,
        out_shape=out_shape,
        in_specs=[scalar] * scalars + [whole] * (len(operands) - scalars),
        out_specs=jax.tree.map(lambda _: whole, out_shape),
        scratch_shapes=scratch_shapes,
        compiler_params=pltpu.CompilerParams(vmem_limit_bytes=VMEM_BYTES),
        cost_estimate=pl.CostEstimate(flops=flops, bytes_accessed=4 * 1024 * 1024, transcendentals=0),
    )(*operands)


def strip_permute(array, target):
    tiles, members = lax.axis_size("tile"), lax.axis_size("visit")
    count = tiles * members
    place = [i % members * tiles + i // members for i in range(count)]
    pairs = [(place[i], place[target(i)]) for i in range(count) if 0 <= target(i) < count]
    return lax.ppermute(array, ("visit", "tile"), pairs)


def group_gather(array, group):
    return [array] + [strip_permute(array, lambda i: i // group * group + (i + k) % group) for k in range(1, group)]


def group_order(arrays, place):
    ordered = []
    for slot in range(len(arrays)):
        back = (place - slot) % len(arrays)
        picked = arrays[0]
        for k in range(1, len(arrays)):
            picked = jnp.where(back == k, arrays[k], picked)
        ordered.append(picked)
    return ordered


def group_swaps(rows, group):
    def partner(first):
        return lambda i: i + group if i // group % 2 == first else i - group

    return [strip_permute(rows, partner(0)), rows, strip_permute(rows, partner(1))]


def body(exposures, sky_model, blur_kernels, coverage):
    tile_rows, width = exposures.shape[1:]
    shard_rows = sky_model.shape[0]
    members = lax.axis_size("visit")
    tiles = lax.axis_size("tile")
    visit = lax.axis_index("visit")
    group = TAPS // shard_rows
    place = visit % group
    hops = TAPS // 2 // shard_rows
    first_row = lax.axis_index("tile") * tile_rows + visit * shard_rows
    parities = [visit // hop % 2 for hop in [group, *range(1, hops + 1)]]
    at = jnp.stack([first_row, place * shard_rows, *parities]).reshape(1, -1)

    f32, bf16 = jnp.float32, jnp.bfloat16
    shape = jax.ShapeDtypeStruct
    blocks = width // BLOCK
    depth = TAPS * WINDOW
    rows = shard_rows + TAPS

    def halo_of(model):
        mine = jnp.concatenate(group_order(group_gather(model, group), place), axis=0)
        return group_swaps(mine, group)

    sent = call(
        send_kernel,
        shape((members, width // LANES * shard_rows + 8, LANES), f32),
        [pltpu.VMEM((TAPS, LANES), f32)],
        1 << 22,
        *(coverage, jnp.transpose(blur_kernels, (1, 0, 2)), exposures),
    )
    received = lax.all_to_all(sent, "visit", 0, 0)
    received, near = lax.optimization_barrier((received, halo_of(sky_model)))
    swaps = []
    for hop in range(1, hops + 1):
        even, _, odd = group_swaps(received[:, : width // LANES * shard_rows], hop)
        swaps += [even, odd]

    blur_scratch = [
        pltpu.VMEM((3 * TAPS, width), f32),
        pltpu.VMEM((rows + TAPS, width), f32),
        pltpu.VMEM((2 * blocks * rows, depth), bf16),
        pltpu.VMEM((blocks * rows, members * BLOCK), f32),
    ]
    sum_scratch = [
        pltpu.VMEM((2 * blocks * (shard_rows + 8), members * 4 * WINDOW), bf16),
        pltpu.VMEM((blocks * (shard_rows + 8), 8 * BLOCK), f32),
    ]
    blur_flops = 6 * blocks * rows * depth * members * BLOCK
    sum_flops = 6 * blocks * (shard_rows + 8) * members * 4 * WINDOW * 8 * BLOCK
    weight_at = functools.partial(weight_of, tile_rows=tile_rows, tiles=tiles)
    tables = call(mirror_kernel, shape((members, 8, 2 * LANES), f32), [], blur_flops + sum_flops, received)
    wb_high, wb_low, wc_high, wc_low, blurred, norm = call(
        functools.partial(first_kernel, functools.partial(norm_field, tile_rows=tile_rows, tiles=tiles)),
        (
            shape((members * BLOCK, depth), bf16),
            shape((members * BLOCK, depth), bf16),
            shape((8 * BLOCK, members * 4 * WINDOW), bf16),
            shape((8 * BLOCK, members * 4 * WINDOW), bf16),
            shape((members, rows, width), f32),
            shape((shard_rows, width), f32),
        ),
        blur_scratch,
        1,
        *(at, tables, *near),
        scalars=1,
    )
    model = call(
        functools.partial(second_kernel, weight_at),
        shape((shard_rows, width), f32),
        sum_scratch,
        sum_flops,
        *(at, wc_high, wc_low, received, blurred, sky_model, norm, *swaps),
        scalars=1,
    )
    return call(
        functools.partial(third_kernel, weight_at),
        shape((shard_rows, width), f32),
        blur_scratch + sum_scratch,
        blur_flops + sum_flops,
        *(at, wb_high, wb_low, wc_high, wc_low, received, model, norm, *halo_of(model), *swaps),
        scalars=1,
    )


def solution(mesh):
    return jax.shard_map(
        body,
        mesh=mesh,
        in_specs=(
            P("visit", "tile", None),
            P(("tile", "visit"), None),
            P("visit", None, None),
            P("visit", None),
        ),
        out_specs=P(("tile", "visit"), None),
        check_vma=False,
    )
```
